128 devices in a mesh: slab: 8 (over z, core), pencil: 16 (over y, x).
Axes of the slice: x: 4, y: 4, z: 4, core: 2. Of those that a mesh axis runs over, the one named last changes fastest.
Arguments:
- charges: float32 [32768, 128], P(('slab', 'pencil')), may hold values from -6 to 6
- projection: float32 [32768, 64, 128], P(('slab', 'pencil')), may hold values from -0.5 to 0.5
- anchors: int32 [32768, 3], P(('slab', 'pencil')), may hold values from 0 to 511, as said below
- block_count: int32 [128], P(('slab', 'pencil')), may hold values from 64 to 256, as said below
- near_pairs: int32 [32768, 2], P(('slab', 'pencil')), may hold values from 0 to 255, as said below
- near_matrices: bfloat16 [32768, 128, 128], P(('slab', 'pencil')), may hold values from -0.5 to 0.5
- kernel_hat: float32 [512, 512, 256], P(None, ('slab', 'pencil')), may hold values from 0.2 to 2, as said below
Outputs:
- panel_potential: float32 [32768, 128], P(('slab', 'pencil'))
The draws below stay inside these ranges and needn't reach their ends.
Inputs may be any that keep to these rules, and one draw needn't show every extreme that they name: Device d = slab index * pencil size + pencil index holds slots d * 256 to (d + 1) * 256 - 1; its first block_count[d] slots are in use, and some device uses all 256. `anchors`: column 0 is x, 1 is y, 2 is z. A block of the device with slab index s and pencil index p has x in [p * 32, (p + 1) * 32) and z in [s * 32, (s + 1) * 32). `near_pairs`: both slots of each pair of a device are in use on that device; target and source may coincide. The Green's function is real and even in space: kernel_hat[kx, ky, kz] equals kernel_hat[(-kx) mod 512, (-ky) mod 512, (-kz) mod 256].
All inputs are finite; a program needn't handle non-finite values.
Results may differ from the reference program's by a relative error of at most 0.0025.
Values sent between devices are 32-bit elements; how exact they have to be, the bound alone decides.
A program may use at most 192 MiB of HBM per device.

```python
import jax
import jax.numpy as jnp
from jax import lax

NX = 512
NY = 512
NZ = 256
PANELS = 128
BOX = 64
BLK_DEV = 256
NEAR_DEV = 256
X_DEV = 32
Z_DEV = 32
BLOCKS = 32768
NEAR = 32768
DEVICES = 128


def count_draw(key):
    key = jax.random.fold_in(key, 11)
    key_a, key_b, key_c, key_d = jax.random.split(key, 4)
    drawn = BLK_DEV // 4 + jax.random.randint(key_a, (DEVICES,), 0, BLK_DEV // 4 + 1)
    heavy = jax.random.randint(key_b, (DEVICES,), BLK_DEV // 2, BLK_DEV + 1)
    chosen = jax.random.randint(key_c, (DEVICES,), 0, 4) == 0
    counts = jnp.where(chosen, heavy, drawn)
    fullest = jax.random.randint(key_d, (), 0, DEVICES)
    return jnp.where(jnp.arange(DEVICES) == fullest, BLK_DEV, counts).astype(jnp.int32)


def draw_block_count(key, part):
    return count_draw(key)


def draw_near_pairs(key, part):
    counts = count_draw(key)
    key = jax.random.fold_in(key, 23)
    key_a, key_b = jax.random.split(key, 2)
    limit_of = jnp.repeat(counts, NEAR_DEV)
    position = jnp.arange(NEAR, dtype=jnp.int32) % NEAR_DEV
    target = jax.random.randint(key_a, (NEAR,), 0, limit_of)
    source = jax.random.randint(key_b, (NEAR,), 0, limit_of)
    target = jnp.where(position == 0, limit_of - 1, target)
    source = jnp.where(position == 1, 0, source)
    return jnp.stack([target, source], axis=1).astype(jnp.int32)


def draw_anchors(key, part):
    key = jax.random.fold_in(key, 37)
    key_a, key_b, key_c = jax.random.split(key, 3)
    pencils = NX // X_DEV
    device = jnp.arange(BLOCKS, dtype=jnp.int32) // BLK_DEV
    pencil_at = device % pencils
    slab_at = device // pencils
    cell_x = pencil_at * X_DEV + jax.random.randint(key_a, (BLOCKS,), 0, X_DEV)
    cell_y = jax.random.randint(key_b, (BLOCKS,), 0, NY)
    cell_z = slab_at * Z_DEV + jax.random.randint(key_c, (BLOCKS,), 0, Z_DEV)
    return jnp.stack([cell_x, cell_y, cell_z], axis=1).astype(jnp.int32)


def draw_kernel_hat(key, part):
    key = jax.random.fold_in(key, 53)
    level = jax.random.uniform(key, (NX, NY, NZ), jnp.float32, 0.2, 2.0)
    mirrored = jnp.roll(jnp.flip(level, (0, 1, 2)), (1, 1, 1), (0, 1, 2))
    return (0.5 * (level + mirrored)).astype(jnp.float32)


def steps_of(stream_key, dims, cuts, smallest, top_value):
    loudness, own = 1.0, jax.random.fold_in(stream_key, 6)
    for axis_at, shards_of in cuts:
        heights = jnp.exp(jax.random.uniform(jax.random.fold_in(own, axis_at), (shards_of,), jnp.float32, smallest / len(cuts), top_value / len(cuts)))
        loudness = loudness * jnp.repeat(heights, dims[axis_at] // shards_of).reshape([-1 if axis == axis_at else 1 for axis in range(len(dims))])
    return loudness


def gaussian(rng, dims, spread, bound, cuts=(), held_as=jnp.bfloat16):
    gain = steps_of(rng, dims, cuts, -0.22, 0.18) if cuts else 1.0
    result = jax.random.normal(rng, dims, jnp.float32) * spread * gain
    return jnp.minimum(jnp.maximum(result, -bound), bound).astype(held_as)


def setup_inputs(seed: int = 0) -> dict:
    streams_of = jax.random.split(jax.random.key(seed), 8)
    return {
        "charges": gaussian(streams_of[0], (BLOCKS, PANELS), 1.0, 6.0, ((0, 128),), jnp.float32),
        "projection": gaussian(streams_of[1], (BLOCKS, BOX, PANELS), PANELS ** -0.5, 0.5, ((0, 128),), jnp.float32),
        "anchors": draw_anchors(jax.random.fold_in(streams_of[7], 71), 0),
        "block_count": draw_block_count(jax.random.fold_in(streams_of[7], 71), 0),
        "near_pairs": draw_near_pairs(jax.random.fold_in(streams_of[7], 71), 0),
        "near_matrices": gaussian(streams_of[5], (NEAR, PANELS, PANELS), PANELS ** -0.5, 0.5, ((0, 128),)),
        "kernel_hat": draw_kernel_hat(jax.random.fold_in(streams_of[7], 71), 0),
    }


precise = lax.Precision.HIGHEST


def box_points(anchors):
    point_id = jnp.arange(BOX, dtype=jnp.int32)
    off_x = point_id // 16 - 2
    off_y = (point_id // 4) % 4 - 2
    off_z = point_id % 4 - 2
    grid_x = (anchors[:, 0:1] + off_x[None, :]) % NX
    grid_y = (anchors[:, 1:2] + off_y[None, :]) % NY
    grid_z = (anchors[:, 2:3] + off_z[None, :]) % NZ
    return ((grid_x * NZ + grid_z) * NY + grid_y).astype(jnp.int32)


def pair_block(operands):
    matrices, sources = operands
    return jnp.einsum("ntp,np->nt", matrices.astype(jnp.float32), sources.astype(jnp.float32), precision=precise)


def reference(charges, projection, anchors, block_count, near_pairs, near_matrices, kernel_hat):
    slot_index = jnp.arange(BLOCKS, dtype=jnp.int32)
    in_use = (slot_index % BLK_DEV) < block_count[slot_index // BLK_DEV]
    masked = jnp.where(in_use[:, None], charges, jnp.zeros_like(charges))
    box_charge = jnp.einsum("bnp,bp->bn", projection, masked, precision=precise)
    flat_index = box_points(anchors).reshape(-1)
    grid_charge = jnp.zeros((NX * NZ * NY,), jnp.float32).at[flat_index].add(box_charge.reshape(-1))
    grid_charge = grid_charge.reshape(NX, NZ, NY)
    spectrum = jnp.fft.fftn(grid_charge) * jnp.transpose(kernel_hat, (0, 2, 1))
    potential = jnp.real(jnp.fft.ifftn(spectrum)).astype(jnp.float32)
    box_potential = potential.reshape(-1)[flat_index].reshape(BLOCKS, BOX)
    far_term = jnp.einsum("bnp,bn->bp", projection, box_potential, precision=precise)
    coarse = masked.astype(jnp.bfloat16)
    device = jnp.arange(NEAR, dtype=jnp.int32) // NEAR_DEV
    target = device * BLK_DEV + near_pairs[:, 0]
    source = device * BLK_DEV + near_pairs[:, 1]
    pair_terms = lax.map(pair_block, (near_matrices.reshape(DEVICES, NEAR_DEV, PANELS, PANELS), coarse[source].reshape(DEVICES, NEAR_DEV, PANELS)))
    near_term = jnp.zeros((BLOCKS, PANELS), jnp.float32).at[target].add(pair_terms.reshape(NEAR, PANELS))
    return jnp.where(in_use[:, None], far_term + near_term, jnp.zeros_like(far_term))
```

```python
import jax
import jax.numpy as jnp
from jax import lax
from jax.experimental import pallas as pl
from jax.experimental.pallas import tpu as pltpu
from jax.sharding import PartitionSpec as P

NX, NY, NZ, BOX = 512, 512, 256, 64
GROUP = 16
F32, BF16 = jnp.float32, jnp.bfloat16


def halves(value):
    high = value.astype(BF16)
    return high, (value - high.astype(F32)).astype(BF16)


def lane_sums(value):
    ones = jnp.ones((128, 128), BF16)
    high, low = halves(value)
    return jnp.dot(high, ones, preferred_element_type=F32) + jnp.dot(low, ones, preferred_element_type=F32)


def window(code):
    x_at = code % 32
    z_at = code // 32 % 32
    y_at = code // 1024
    tile_0 = y_at // 128
    return x_at, z_at + 6, tile_0, (tile_0 + 1) % 4, y_at % 128


def window_masks(lane_0):
    row = lax.broadcasted_iota(jnp.int32, (8, 128), 0)
    lane = lax.broadcasted_iota(jnp.int32, (8, 128), 1)
    shifted = lane - row // 4 - lane_0
    return (shifted == 0, shifted == 2), (shifted == -128, shifted == -126)


def scatter_kernel(codes, count, projection, charges, grid, values):
    step = pl.program_id(0)

    @pl.when(step == 0)
    def _():
        def clear(x, carry):
            grid[x] = jnp.zeros(grid.shape[1:], F32)
            return carry

        lax.fori_loop(0, grid.shape[0], clear, 0)

    slot = step * GROUP + lax.broadcasted_iota(jnp.int32, (GROUP, 128), 0)
    masked = jnp.where(slot < count[0], charges[...], 0.0)
    products = projection[...] * masked[:, None, :]
    values[...] = lane_sums(products.reshape(GROUP * BOX, 128)).reshape(GROUP, BOX, 128)
    top = lax.broadcasted_iota(jnp.int32, (8, 128), 0) < 4

    def place(b, carry):
        x_at, z_row, tile_0, tile_1, lane_0 = window(codes[step * GROUP + b])
        for tile, masks in zip((tile_0, tile_1), window_masks(lane_0)):
            for i in range(4):
                patch = jnp.where(masks[0], values[b, 16 * i : 16 * i + 8], 0.0)
                patch = jnp.where(masks[1], values[b, 16 * i + 8 : 16 * i + 16], patch)
                patch = jnp.where(top, patch + pltpu.roll(patch, 4, 0), 0.0)
                grid[x_at + i, tile, pl.ds(z_row, 8), :] += patch
        return carry

    lax.fori_loop(0, GROUP, place, 0)


def scatter(codes, count, projection, charges):
    slots = charges.shape[0]
    return pl.pallas_call(
        scatter_kernel,
        grid_spec=pltpu.PrefetchScalarGridSpec(
            num_scalar_prefetch=2,
            grid=(slots // GROUP,),
            in_specs=[
                pl.BlockSpec((GROUP, BOX, 128), lambda i, *_: (i, 0, 0)),
                pl.BlockSpec((GROUP, 128), lambda i, *_: (i, 0)),
            ],
            out_specs=pl.BlockSpec((36, 4, 48, 128), lambda i, *_: (0, 0, 0, 0)),
            scratch_shapes=[pltpu.VMEM((GROUP, BOX, 128), F32)],
        ),
        out_shape=jax.ShapeDtypeStruct((36, 4, 48, 128), F32),
        compiler_params=pltpu.CompilerParams(vmem_limit_bytes=32 << 20),
    )(codes, count, projection, charges)


def gather_kernel(codes, count, targets, projection, grid, pair_terms, out, near, picked):
    step = pl.program_id(0)

    @pl.when(step == 0)
    def _():
        slots, pairs = near.shape[0], pair_terms.shape[0]
        slot = lax.broadcasted_iota(jnp.int32, (slots, pairs), 0)
        chosen = jnp.where(slot == targets[...], 1.0, 0.0).astype(BF16)
        rest = pair_terms[...]
        total = jnp.zeros(near.shape, F32)
        for _ in range(3):
            part = rest.astype(BF16)
            rest = rest - part.astype(F32)
            total = total + jnp.dot(chosen, part, preferred_element_type=F32)
        near[...] = total

    top = lax.broadcasted_iota(jnp.int32, (8, 128), 0) < 4

    def pick(b, carry):
        x_at, z_row, tile_0, tile_1, lane_0 = window(codes[step * GROUP + b])
        masks_0, masks_1 = window_masks(lane_0)
        for i in range(4):
            both = []
            for tile in (tile_0, tile_1):
                rows = grid[x_at + i, tile, pl.ds(z_row, 8), :]
                both.append(jnp.where(top, rows, pltpu.roll(rows, 4, 0)))
            for j in range(2):
                value = jnp.where(masks_0[j], both[0], jnp.where(masks_1[j], both[1], 0.0))
                picked[b, 16 * i + 8 * j : 16 * i + 8 * j + 8] = value
        return carry

    lax.fori_loop(0, GROUP, pick, 0)
    box = lane_sums(picked[...].reshape(GROUP * BOX, 128)).reshape(GROUP, BOX, 128)
    far = jnp.sum(projection[...] * box, axis=1)
    slot = step * GROUP + lax.broadcasted_iota(jnp.int32, (GROUP, 128), 0)
    total = far + near[pl.ds(pl.multiple_of(step * GROUP, GROUP), GROUP), :]
    out[...] = jnp.where(slot < count[0], total, 0.0)


def gather(codes, count, targets, projection, grid, pair_terms):
    slots, pairs = projection.shape[0], pair_terms.shape[0]
    return pl.pallas_call(
        gather_kernel,
        grid_spec=pltpu.PrefetchScalarGridSpec(
            num_scalar_prefetch=2,
            grid=(slots // GROUP,),
            in_specs=[
                pl.BlockSpec((1, pairs), lambda i, *_: (0, 0)),
                pl.BlockSpec((GROUP, BOX, 128), lambda i, *_: (i, 0, 0)),
                pl.BlockSpec((36, 4, 48, 128), lambda i, *_: (0, 0, 0, 0)),
                pl.BlockSpec((pairs, 128), lambda i, *_: (0, 0)),
            ],
            out_specs=pl.BlockSpec((GROUP, 128), lambda i, *_: (i, 0)),
            scratch_shapes=[pltpu.VMEM((slots, 128), F32), pltpu.VMEM((GROUP, BOX, 128), F32)],
        ),
        out_shape=jax.ShapeDtypeStruct((slots, 128), F32),
        compiler_params=pltpu.CompilerParams(vmem_limit_bytes=32 << 20),
    )(codes, count, targets, projection, grid, pair_terms)


precise = lax.Precision.HIGHEST


def extended_2(cells, sides, width):
    for axis, dim in sides:
        count = lax.axis_size(axis)
        head = lax.slice_in_dim(cells, 0, width, axis=dim)
        tail = lax.slice_in_dim(cells, cells.shape[dim] - width, cells.shape[dim], axis=dim)
        cells = jnp.concatenate(
            [
                lax.ppermute(tail, axis, [(i, (i + 1) % count) for i in range(count)]),
                cells,
                lax.ppermute(head, axis, [((i + 1) % count, i) for i in range(count)]),
            ],
            axis=dim,
        )
    return cells


def tables(length):
    position = jnp.arange(length, dtype=jnp.int32)
    phase_angle = (position[:, None] * position[None, :] % length).astype(jnp.float32) * (
        2.0 * jnp.pi / length
    )
    return (jnp.cos(phase_angle), jnp.sin(phase_angle))


def forward_x(table, field):
    return jnp.einsum("kx,wxz->kwz", table, field, precision=precise)


def inverse_x(table, field):
    return jnp.einsum("xk,kwz->xwz", table, field, precision=precise)


def last_dim(field, table):
    return jnp.dot(field, table, precision=precise)


def frequency_of(owner, within, y_dev):
    return owner * y_dev + within


def shards(charges, projection, anchors, block_count, near_pairs, near_matrices, kernel_hat):
    slot_count, panels = charges.shape
    n_slab = lax.axis_size("slab")
    n_pencil = lax.axis_size("pencil")
    n_dev = n_slab * n_pencil
    x_dev = NX // n_pencil
    z_dev = NZ // n_slab
    y_dev = NY // n_dev
    x_start = lax.axis_index("pencil") * x_dev
    z_start = lax.axis_index("slab") * z_dev
    in_use = jnp.arange(slot_count, dtype=jnp.int32) < block_count[0]
    masked = jnp.where(in_use[:, None], charges, 0.0)
    local = anchors - jnp.stack([x_start, 2, z_start])[None, :]
    codes = local[:, 0] + 32 * local[:, 2] + 1024 * (local[:, 1] % NY)
    extended = scatter(codes, block_count, projection, charges)
    extended = jnp.transpose(extended[:, :, 6:42, :], (0, 2, 1, 3)).reshape(x_dev + 4, z_dev + 4, NY)
    plane_rims = jnp.concatenate([extended[:, :2], extended[:, z_dev + 2 :]], axis=1)
    plane_rims = extended_2(plane_rims, (("slab", 1),), 2)
    planes = extended[:, 2 : z_dev + 2]
    planes = planes.at[:, :2].add(plane_rims[:, :2])
    planes = planes.at[:, z_dev - 2 :].add(plane_rims[:, 6:])
    row_rims = jnp.concatenate([planes[:2], planes[x_dev + 2 :]], axis=0)
    row_rims = extended_2(row_rims, (("pencil", 0),), 2)
    grid_charge = planes[2 : x_dev + 2]
    grid_charge = grid_charge.at[:2].add(row_rims[:2])
    grid_charge = grid_charge.at[x_dev - 2 :].add(row_rims[6:])
    position = jnp.arange(NY, dtype=jnp.int32)
    columns = jnp.arange(n_dev * y_dev, dtype=jnp.int32)
    forward_freq = frequency_of(columns // y_dev, columns % y_dev, y_dev)
    forward_angle = (position[:, None] * forward_freq[None, :] % NY).astype(jnp.float32) * (
        2.0 * jnp.pi / NY
    )
    forward_cos = jnp.cos(forward_angle)
    forward_sin = jnp.sin(forward_angle)
    flat_charge = grid_charge.reshape(x_dev * z_dev, NY)
    real_cols = jnp.einsum("yc,ay->ca", forward_cos, flat_charge, precision=precise)
    imag_cols = -jnp.einsum("yc,ay->ca", forward_sin, flat_charge, precision=precise)
    stacked = jnp.stack([real_cols, imag_cols]).reshape(2, n_dev * y_dev, x_dev, z_dev)
    cos_x, sin_x = tables(NX)
    cos_z, sin_z = tables(NZ)
    spectrum = lax.all_to_all(
        lax.all_to_all(stacked, "slab", split_axis=1, concat_axis=3, tiled=True),
        "pencil",
        split_axis=1,
        concat_axis=2,
        tiled=True,
    )
    real_part, imag_part = (spectrum[0], spectrum[1])
    real_z = last_dim(real_part, cos_z) + last_dim(imag_part, sin_z)
    imag_z = last_dim(imag_part, cos_z) - last_dim(real_part, sin_z)
    real_x = forward_x(cos_x, real_z) + forward_x(sin_x, imag_z)
    imag_x = forward_x(cos_x, imag_z) - forward_x(sin_x, real_z)
    real_kernel = real_x * kernel_hat
    imag_kernel = imag_x * kernel_hat
    real_back = inverse_x(cos_x, real_kernel) - inverse_x(sin_x, imag_kernel)
    imag_back = inverse_x(cos_x, imag_kernel) + inverse_x(sin_x, real_kernel)
    real_space = last_dim(real_back, cos_z) - last_dim(imag_back, sin_z)
    imag_space = last_dim(imag_back, cos_z) + last_dim(real_back, sin_z)
    outgoing = jnp.stack([real_space, imag_space])
    returned = lax.all_to_all(
        lax.all_to_all(outgoing, "slab", split_axis=3, concat_axis=2, tiled=True),
        "pencil",
        split_axis=1,
        concat_axis=2,
        tiled=True,
    )
    from_pencil = columns // (n_slab * y_dev)
    from_slab = columns // y_dev % n_slab
    back_owner = from_slab * n_pencil + from_pencil
    back_within = columns % y_dev
    back_freq = frequency_of(back_owner, back_within, y_dev)
    back_angle = (back_freq[:, None] * position[None, :] % NY).astype(jnp.float32) * (
        2.0 * jnp.pi / NY
    )
    back_cos = jnp.cos(back_angle)
    back_sin = jnp.sin(back_angle)
    scale = 1.0 / (NX * NY * NZ)
    potential = (
        jnp.einsum("xcz,cy->xzy", returned[0], back_cos, precision=precise)
        - jnp.einsum("xcz,cy->xzy", returned[1], back_sin, precision=precise)
    ) * scale
    rimmed = extended_2(potential, (("slab", 1), ("pencil", 0)), 2)
    coarse = masked.astype(jnp.bfloat16)
    sources = coarse[near_pairs[:, 1]]
    pair_terms = jnp.einsum(
        "ntp,np->nt", near_matrices, sources, preferred_element_type=jnp.float32
    )
    rimmed = jnp.transpose(rimmed.reshape(x_dev + 4, z_dev + 4, 4, 128), (0, 2, 1, 3))
    rimmed = jnp.pad(rimmed, ((0, 0), (0, 0), (6, 6), (0, 0)))
    return gather(codes, block_count, near_pairs[:, 0][None, :], projection, rimmed, pair_terms)


def solution(mesh):
    return jax.shard_map(
        shards,
        mesh=mesh,
        in_specs=(
            P(("slab", "pencil"), None),
            P(("slab", "pencil"), None, None),
            P(("slab", "pencil"), None),
            P(("slab", "pencil")),
            P(("slab", "pencil"), None),
            P(("slab", "pencil"), None, None),
            P(None, ("slab", "pencil"), None),
        ),
        out_specs=P(("slab", "pencil"), None),
        check_vma=False,
    )
```

```python
import jax
import jax.numpy as jnp
import ml_dtypes
import numpy as np
from jax import lax
from jax.experimental import pallas as pl
from jax.experimental.pallas import tpu as pltpu
from jax.sharding import PartitionSpec as P

NX, NY, NZ, BOX = 512, 512, 256, 64
GROUP = 16
F32, BF16 = jnp.float32, jnp.bfloat16


def halves(value):
    high = value.astype(BF16)
    return high, (value - high.astype(F32)).astype(BF16)


def lane_sums(value):
    ones = jnp.ones((128, 128), BF16)
    high, low = halves(value)
    return jnp.dot(high, ones, preferred_element_type=F32) + jnp.dot(low, ones, preferred_element_type=F32)


def window(code):
    x_at = code % 32
    z_at = code // 32 % 32
    y_at = code // 1024
    tile_0 = y_at // 128
    return x_at, z_at + 6, tile_0, (tile_0 + 1) % 4, y_at % 128


def window_masks(lane_0):
    row = lax.broadcasted_iota(jnp.int32, (8, 128), 0)
    lane = lax.broadcasted_iota(jnp.int32, (8, 128), 1)
    shifted = lane - row // 4 - lane_0
    return (shifted == 0, shifted == 2), (shifted == -128, shifted == -126)


def scatter_kernel(codes, count, projection, charges, grid, values):
    step = pl.program_id(0)

    @pl.when(step == 0)
    def _():
        def clear(x, carry):
            grid[x] = jnp.zeros(grid.shape[1:], F32)
            return carry

        lax.fori_loop(0, grid.shape[0], clear, 0)

    slot = step * GROUP + lax.broadcasted_iota(jnp.int32, (GROUP, 128), 0)
    masked = jnp.where(slot < count[0], charges[...], 0.0)
    products = projection[...] * masked[:, None, :]
    values[...] = lane_sums(products.reshape(GROUP * BOX, 128)).reshape(GROUP, BOX, 128)
    top = lax.broadcasted_iota(jnp.int32, (8, 128), 0) < 4

    def place(b, carry):
        x_at, z_row, tile_0, tile_1, lane_0 = window(codes[step * GROUP + b])
        for tile, masks in zip((tile_0, tile_1), window_masks(lane_0)):
            for i in range(4):
                patch = jnp.where(masks[0], values[b, 16 * i : 16 * i + 8], 0.0)
                patch = jnp.where(masks[1], values[b, 16 * i + 8 : 16 * i + 16], patch)
                patch = jnp.where(top, patch + pltpu.roll(patch, 4, 0), 0.0)
                grid[x_at + i, tile, pl.ds(z_row, 8), :] += patch
        return carry

    lax.fori_loop(0, GROUP, place, 0)


def scatter(codes, count, projection, charges):
    slots = charges.shape[0]
    return pl.pallas_call(
        scatter_kernel,
        grid_spec=pltpu.PrefetchScalarGridSpec(
            num_scalar_prefetch=2,
            grid=(slots // GROUP,),
            in_specs=[
                pl.BlockSpec((GROUP, BOX, 128), lambda i, *_: (i, 0, 0)),
                pl.BlockSpec((GROUP, 128), lambda i, *_: (i, 0)),
            ],
            out_specs=pl.BlockSpec((36, 4, 48, 128), lambda i, *_: (0, 0, 0, 0)),
            scratch_shapes=[pltpu.VMEM((GROUP, BOX, 128), F32)],
        ),
        out_shape=jax.ShapeDtypeStruct((36, 4, 48, 128), F32),
        compiler_params=pltpu.CompilerParams(vmem_limit_bytes=32 << 20),
    )(codes, count, projection, charges)


def gather_kernel(codes, count, targets, projection, grid, pair_terms, out, near, picked):
    step = pl.program_id(0)

    @pl.when(step == 0)
    def _():
        slots, pairs = near.shape[0], pair_terms.shape[0]
        slot = lax.broadcasted_iota(jnp.int32, (slots, pairs), 0)
        chosen = jnp.where(slot == targets[...], 1.0, 0.0).astype(BF16)
        rest = pair_terms[...]
        total = jnp.zeros(near.shape, F32)
        for _ in range(3):
            part = rest.astype(BF16)
            rest = rest - part.astype(F32)
            total = total + jnp.dot(chosen, part, preferred_element_type=F32)
        near[...] = total

    top = lax.broadcasted_iota(jnp.int32, (8, 128), 0) < 4

    def pick(b, carry):
        x_at, z_row, tile_0, tile_1, lane_0 = window(codes[step * GROUP + b])
        masks_0, masks_1 = window_masks(lane_0)
        for i in range(4):
            both = []
            for tile in (tile_0, tile_1):
                rows = grid[x_at + i, tile, pl.ds(z_row, 8), :]
                both.append(jnp.where(top, rows, pltpu.roll(rows, 4, 0)))
            for j in range(2):
                value = jnp.where(masks_0[j], both[0], jnp.where(masks_1[j], both[1], 0.0))
                picked[b, 16 * i + 8 * j : 16 * i + 8 * j + 8] = value
        return carry

    lax.fori_loop(0, GROUP, pick, 0)
    box = lane_sums(picked[...].reshape(GROUP * BOX, 128)).reshape(GROUP, BOX, 128)
    far = jnp.sum(projection[...] * box, axis=1)
    slot = step * GROUP + lax.broadcasted_iota(jnp.int32, (GROUP, 128), 0)
    total = far + near[pl.ds(pl.multiple_of(step * GROUP, GROUP), GROUP), :]
    out[...] = jnp.where(slot < count[0], total, 0.0)


def gather(codes, count, targets, projection, grid, pair_terms):
    slots, pairs = projection.shape[0], pair_terms.shape[0]
    return pl.pallas_call(
        gather_kernel,
        grid_spec=pltpu.PrefetchScalarGridSpec(
            num_scalar_prefetch=2,
            grid=(slots // GROUP,),
            in_specs=[
                pl.BlockSpec((1, pairs), lambda i, *_: (0, 0)),
                pl.BlockSpec((GROUP, BOX, 128), lambda i, *_: (i, 0, 0)),
                pl.BlockSpec((36, 4, 48, 128), lambda i, *_: (0, 0, 0, 0)),
                pl.BlockSpec((pairs, 128), lambda i, *_: (0, 0)),
            ],
            out_specs=pl.BlockSpec((GROUP, 128), lambda i, *_: (i, 0)),
            scratch_shapes=[pltpu.VMEM((slots, 128), F32), pltpu.VMEM((GROUP, BOX, 128), F32)],
        ),
        out_shape=jax.ShapeDtypeStruct((slots, 128), F32),
        compiler_params=pltpu.CompilerParams(vmem_limit_bytes=32 << 20),
    )(codes, count, targets, projection, grid, pair_terms)


CHUNKS = 4
MESH = pl.DeviceIdType.MESH


def phases(product, length):
    angle = 2.0 * np.pi * (product % length) / length
    return np.cos(angle), np.sin(angle)


def split_table(table):
    table = table.astype(np.float32)
    high = table.astype(ml_dtypes.bfloat16)
    return high, (table - high.astype(np.float32)).astype(ml_dtypes.bfloat16)


def y_tables():
    slab, part, pencil = np.meshgrid(np.arange(8), np.arange(2), np.arange(16), indexing="ij")
    device = (slab * 16 + pencil).reshape(-1, 1)
    part = part.reshape(-1, 1)
    even = np.where(device < 64, 4 * device, 4 * device + 2)
    odd = 4 * device + 1
    position = np.arange(256)[None, :]
    result = []
    for freq in (even, odd):
        cos, sin = phases(freq * position, NY)
        table = np.where(part == 0, cos, -sin)
        if freq is even:
            table[(device[:, 0] == 0) & (part[:, 0] == 1)] = 1.0 - 2.0 * (position[0] % 2)
        result.append(table)
    return np.stack(result)


def z_table():
    position = np.arange(NZ)
    cos, sin = phases(position[:, None] * position[None, :], NZ)
    return np.block([[cos, -sin], [sin, cos]])


def x_tables():
    position = np.arange(256)
    result = []
    for parity in range(2):
        cos, sin = phases((2 * position[:, None] + parity) * position[None, :], NX)
        result.append(np.concatenate([cos, sin], axis=1))
        if parity:
            result.append(np.concatenate([cos.T, sin.T], axis=1))
    return np.stack(result)


def dot_3(left, right, dims=((1,), (0,))):
    def one(a, b):
        return lax.dot_general(a, b, (dims, ((), ())), preferred_element_type=F32)

    return one(left[0], right[0]) + (one(left[0], right[1]) + one(left[1], right[0]))


def swap_groups(tiles):
    lane = lax.broadcasted_iota(jnp.int32, tiles[0].shape, 1)
    low, even = lane < 64, lane % 64 < 32
    firsts, lasts = [], []
    for a, b in ((tiles[0], tiles[2]), (tiles[1], tiles[3])):
        firsts.append(jnp.where(low, a, pltpu.roll(b, 64, 1)))
        lasts.append(jnp.where(low, pltpu.roll(a, 64, 1), b))
    result = []
    for a, b in (firsts, lasts):
        result.append(jnp.where(even, a, pltpu.roll(b, 32, 1)))
        result.append(jnp.where(even, pltpu.roll(a, 96, 1), b))
    return result


def field_kernel(
    grid, kernel, nyquist, ty_high, ty_low, tz_high, tz_low, tx_high, tx_low,
    out,
    charge, z_out, z_in, x_in, sent_1, got_1, sent_2, got_2, spectra, back_2, took_2, back_1, took_1, lines,
    last_z_out, last_z_in, last_x_out, last_x_in,
    rim_send, rim_recv, send_1, recv_1, send_2, recv_2, send_3, recv_3, send_4, recv_4,
):
    slab, pencil = lax.axis_index("slab"), lax.axis_index("pencil")
    n_slab, n_pencil = 8, 16

    def on_slab(step):
        return (lax.rem(slab + step, n_slab), pencil)

    def on_pencil(step):
        return (slab, lax.rem(pencil + step, n_pencil))

    def remote(source, target, send_sem, recv_sem, device):
        return pltpu.make_async_remote_copy(
            src_ref=source, dst_ref=target, send_sem=send_sem, recv_sem=recv_sem, device_id=device, device_id_type=MESH
        )

    def wait_recv(ref, sem):
        remote(ref, ref, sem, sem, on_slab(1)).wait_recv()

    def wait_send(ref, sem):
        remote(ref, ref, sem, sem, on_slab(1)).wait_send()

    barrier = pltpu.get_barrier_semaphore()

    def greet_slab(step, carry):
        pl.semaphore_signal(barrier, inc=1, device_id=on_slab(step), device_id_type=MESH)
        return carry

    def greet_pencil(step, carry):
        pl.semaphore_signal(barrier, inc=1, device_id=on_pencil(step), device_id_type=MESH)
        return carry

    lax.fori_loop(1, n_slab, greet_slab, 0)
    lax.fori_loop(1, n_pencil, greet_pencil, 0)

    def pack_rims(x, carry):
        for tile in range(4):
            z_out[0, x, 2 * tile : 2 * tile + 2, :] = grid[x, tile, 6:8, :]
            z_out[1, x, 2 * tile : 2 * tile + 2, :] = grid[x, tile, 40:42, :]
        return carry

    lax.fori_loop(0, 36, pack_rims, 0)
    pl.semaphore_wait(barrier, n_slab + n_pencil - 2)
    remote(z_out.at[0], z_in.at[1], rim_send.at[0], rim_recv.at[0], on_slab(n_slab - 1)).start()
    remote(z_out.at[1], z_in.at[0], rim_send.at[1], rim_recv.at[1], on_slab(1)).start()
    def clear(x, carry):
        out[x] = jnp.zeros(out.shape[1:], F32)
        return carry

    lax.fori_loop(0, 36, clear, 0)
    wait_recv(z_in.at[1], rim_recv.at[0])
    wait_recv(z_in.at[0], rim_recv.at[1])

    def add_rims(step, carry):
        x = lax.rem(step + 34, 36)
        for tile in range(4):
            charge[x, tile] = grid[x, tile, 8:40, :]
            charge[x, tile, 0:2, :] += z_in[0, x, 2 * tile : 2 * tile + 2, :]
            charge[x, tile, 30:32, :] += z_in[1, x, 2 * tile : 2 * tile + 2, :]
        return carry

    lax.fori_loop(0, 4, add_rims, 0)
    remote(charge.at[0:2], x_in.at[1], rim_send.at[2], rim_recv.at[2], on_pencil(n_pencil - 1)).start()
    remote(charge.at[34:36], x_in.at[0], rim_send.at[3], rim_recv.at[3], on_pencil(1)).start()
    lax.fori_loop(4, 36, add_rims, 0)

    def forward_y(step, carry):
        chunk = lax.rem(step + 1, CHUNKS)

        @pl.when(step == 2)
        def _():
            wait_recv(x_in.at[1], rim_recv.at[2])
            wait_recv(x_in.at[0], rim_recv.at[3])
            charge[2:4] += x_in[0]
            charge[32:34] += x_in[1]

        tiles = [charge[pl.ds(2 + 8 * chunk, 8), tile].reshape(256, 128) for tile in range(4)]
        for parity in range(2):
            if parity:
                halved = [tiles[0] - tiles[2], tiles[1] - tiles[3]]
            else:
                halved = [tiles[0] + tiles[2], tiles[1] + tiles[3]]
            columns = halves(jnp.concatenate(halved, axis=1))
            freqs = dot_3((ty_high[parity], ty_low[parity]), columns, ((1,), (1,)))
            sent_1[chunk, :, 32 * parity : 32 * parity + 32, :] = freqs.reshape(n_slab, 32, 256)
        got_1[chunk, slab] = sent_1[chunk, slab]

        def send(k, carry):
            device = on_slab(k)
            remote(sent_1.at[chunk, device[0]], got_1.at[chunk, slab], send_1, recv_1.at[chunk], device).start()
            return carry

        return lax.fori_loop(1, n_slab, send, carry)

    lax.fori_loop(0, CHUNKS, forward_y, 0)

    def forward_z(step, carry):
        chunk = lax.rem(step + 1, CHUNKS)
        wait_recv(got_1.at[chunk, 0 : n_slab - 1], recv_1.at[chunk])
        for h in range(2):
            for q in range(2):
                tiles = swap_groups([got_1[chunk, 4 * q + s, :, 128 * h : 128 * h + 128] for s in range(4)])
                for a in range(4):
                    for parity in range(2):
                        for part in range(2):
                            row = 32 * parity + 16 * part
                            lines[2 * part + q, pl.ds(128 * parity + 4 * h + a, 16, stride=8), :] = tiles[a][row : row + 16]
        rows = halves(jnp.concatenate([lines[i] for i in range(4)], axis=1))
        freqs = dot_3(rows, (tz_high[...], tz_low[...]))
        for parity in range(2):
            for part in range(2):
                block = freqs[128 * parity : 128 * parity + 128, 256 * part : 256 * part + 256]
                sent_2[chunk, :, parity, part] = block.reshape(n_pencil, 8, 256)
        mine = pl.ds(pl.multiple_of(pencil * 32 + chunk * 8, 8), 8)
        got_2[:, :, mine, :] = sent_2[chunk, pencil]

        def send(k, carry):
            device = on_pencil(k)
            remote(sent_2.at[chunk, device[1]], got_2.at[:, :, mine, :], send_2, recv_2, device).start()
            return carry

        return lax.fori_loop(1, n_pencil, send, carry)

    lax.fori_loop(0, CHUNKS, forward_z, 0)
    wait_recv(got_2.at[:, :, 0 : 32 * (n_pencil - 1), :], recv_2)

    first = jnp.logical_and(slab == 0, pencil == 0)
    unit = 1.0 / (NX * NY * NZ)

    def level(ref, start, stride):
        return jnp.concatenate([ref[pl.ds(start + i, 256, stride=stride), :] for i in range(2)], axis=1)

    def stacked(real, imag):
        real, imag = halves(real), halves(imag)
        return tuple(
            jnp.concatenate([jnp.concatenate([r, i], axis=1), jnp.concatenate([i, -r], axis=1)], axis=0)
            for r, i in zip(real, imag)
        )

    for parity in range(2):
        for kx in range(2):
            parts = []
            for part in range(2):
                low, high = got_2[parity, part, 0:256, :], got_2[parity, part, 256:512, :]
                parts.append(low - high if kx else low + high)
            table = (tx_high[kx], tx_low[kx])
            found = dot_3(table, stacked(*parts))
            if parity:
                green = jnp.concatenate(
                    [kernel[pl.ds(8 * kx + 4 * i + 1, 256, stride=16), :] for i in range(2)], axis=1
                ) * (2.0 * unit)
            else:
                own = jnp.where(slab < 4, 0, 2)
                green = jnp.concatenate(
                    [kernel[pl.ds(own + 8 * kx + 4 * i, 256, stride=16), :] for i in range(2)], axis=1
                ) * jnp.where(first, unit, 2.0 * unit)
            spectra[kx, 0] = found[:, 0:256] * green
            spectra[kx, 1] = found[:, 256:512] * green
            if not parity:

                @pl.when(first)
                def _():
                    other = level(nyquist, 2 * kx, 4) * unit
                    row = lax.broadcasted_iota(jnp.int32, (256, 256), 0)
                    lane = lax.broadcasted_iota(jnp.int32, (256, 256), 1)
                    mirror = jnp.where((row + lane) % 256 == 0, 1.0, 0.0).astype(BF16)
                    flipped = [
                        sum(jnp.dot(piece, mirror, preferred_element_type=F32) for piece in halves(value)) for value in parts
                    ]
                    twin = dot_3(table, stacked(flipped[0], -flipped[1]))
                    mean, rest = 0.5 * (green + other), 0.5 * (green - other)
                    for part in range(2):
                        lanes = slice(256 * part, 256 * part + 256)
                        spectra[kx, part] = mean * found[:, lanes] + rest * twin[:, lanes]

        ends = []
        for kx in range(2):
            table = (tx_high[2 * kx], tx_low[2 * kx])
            real, imag = halves(spectra[kx, 0]), halves(spectra[kx, 1])
            right = tuple(
                jnp.concatenate([jnp.concatenate([r, i], axis=1), jnp.concatenate([-i, r], axis=1)], axis=0)
                for r, i in zip(real, imag)
            )
            ends.append(dot_3(table, right))
        for part in range(2):
            lanes = slice(256 * part, 256 * part + 256)
            back_2[parity, part, 0:256, :] = ends[0][:, lanes] + ends[1][:, lanes]
            back_2[parity, part, 256:512, :] = ends[0][:, lanes] - ends[1][:, lanes]

    def return_x(chunk, carry):
        own = pl.ds(pl.multiple_of(pencil * 32 + chunk * 8, 8), 8)
        took_2[chunk, pencil] = back_2[:, :, own, :]

        def send(k, carry):
            device = on_pencil(k)
            rows = pl.ds(pl.multiple_of(device[1] * 32 + chunk * 8, 8), 8)
            remote(back_2.at[:, :, rows, :], took_2.at[chunk, pencil], send_3, recv_3.at[chunk], device).start()
            return carry

        return lax.fori_loop(1, n_pencil, send, carry)

    lax.fori_loop(0, CHUNKS, return_x, 0)

    def inverse_z(chunk, carry):
        wait_recv(took_2.at[chunk, 0 : n_pencil - 1], recv_3.at[chunk])
        blocks = []
        for parity in range(2):
            blocks.append(jnp.concatenate([took_2[chunk, :, parity, part].reshape(128, 256) for part in range(2)], axis=1))
        rows = halves(jnp.concatenate(blocks, axis=0))
        space = dot_3(rows, (tz_high[...], tz_low[...]), ((1,), (1,)))
        for i in range(4):
            lines[i] = space[:, 128 * i : 128 * i + 128]
        for h in range(2):
            for q in range(2):
                tiles = []
                for a in range(4):
                    tiles.append(
                        jnp.concatenate(
                            [
                                lines[2 * part + q, pl.ds(128 * parity + 4 * h + a, 16, stride=8), :]
                                for parity in range(2)
                                for part in range(2)
                            ],
                            axis=0,
                        )
                    )
                for s, tile in enumerate(swap_groups(tiles)):
                    back_1[chunk, 4 * q + s, :, 128 * h : 128 * h + 128] = tile
        took_1[chunk, slab] = back_1[chunk, slab]

        def send(k, carry):
            device = on_slab(k)
            remote(back_1.at[chunk, device[0]], took_1.at[chunk, slab], send_4, recv_4.at[chunk], device).start()
            return carry

        return lax.fori_loop(1, n_slab, send, carry)

    lax.fori_loop(0, CHUNKS, inverse_z, 0)

    def inverse_y(chunk, carry):
        wait_recv(took_1.at[chunk, 0 : n_slab - 1], recv_4.at[chunk])
        ends = []
        for parity in range(2):
            columns = took_1[chunk, :, 32 * parity : 32 * parity + 32, :].reshape(256, 256).T
            ends.append(dot_3(halves(columns), (ty_high[parity], ty_low[parity])))
        space = (ends[0] + ends[1], ends[0] - ends[1])
        for tile in range(4):
            lanes = slice(128 * (tile % 2), 128 * (tile % 2) + 128)
            cells = space[tile // 2][:, lanes].reshape(8, 32, 128)
            out[pl.ds(2 + 8 * chunk, 8), tile, 8:40, :] = cells
            last_z_out[chunk, 0, :, 2 * tile : 2 * tile + 2, :] = cells[:, 0:2, :]
            last_z_out[chunk, 1, :, 2 * tile : 2 * tile + 2, :] = cells[:, 30:32, :]
        remote(
            last_z_out.at[chunk, 0], last_z_in.at[chunk, 1], rim_send.at[4], rim_recv.at[4], on_slab(n_slab - 1)
        ).start()
        remote(last_z_out.at[chunk, 1], last_z_in.at[chunk, 0], rim_send.at[5], rim_recv.at[5], on_slab(1)).start()
        return carry

    lax.fori_loop(0, CHUNKS, inverse_y, 0)
    wait_recv(last_z_in.at[:, 1], rim_recv.at[4])
    wait_recv(last_z_in.at[:, 0], rim_recv.at[5])

    def spread(step, carry):
        for tile in range(4):
            out[2 + step, tile, 6:8, :] = last_z_in[step // 8, 0, step % 8, 2 * tile : 2 * tile + 2, :]
            out[2 + step, tile, 40:42, :] = last_z_in[step // 8, 1, step % 8, 2 * tile : 2 * tile + 2, :]
        return carry

    lax.fori_loop(0, 32, spread, 0)
    last_x_out[0] = out[2:4]
    last_x_out[1] = out[32:34]
    remote(last_x_out.at[0], last_x_in.at[1], rim_send.at[6], rim_recv.at[6], on_pencil(n_pencil - 1)).start()
    remote(last_x_out.at[1], last_x_in.at[0], rim_send.at[7], rim_recv.at[7], on_pencil(1)).start()
    wait_send(z_out.at[0], rim_send.at[0])
    wait_send(z_out.at[1], rim_send.at[1])
    wait_send(charge.at[0:2], rim_send.at[2])
    wait_send(charge.at[34:36], rim_send.at[3])
    wait_send(sent_1.at[:, 0 : n_slab - 1], send_1)
    wait_send(got_2.at[:, :, 0 : 32 * (n_pencil - 1), :], send_2)
    wait_send(got_2.at[:, :, 0 : 32 * (n_pencil - 1), :], send_3)
    wait_send(back_1.at[:, 0 : n_slab - 1], send_4)
    wait_send(last_z_out.at[:, 0], rim_send.at[4])
    wait_send(last_z_out.at[:, 1], rim_send.at[5])
    wait_recv(last_x_in.at[1], rim_recv.at[6])
    wait_recv(last_x_in.at[0], rim_recv.at[7])
    out[0:2] = last_x_in[0]
    out[34:36] = last_x_in[1]
    wait_send(last_x_out.at[0], rim_send.at[6])
    wait_send(last_x_out.at[1], rim_send.at[7])


def field(grid, kernel, nyquist):
    ty, tz, tx = (split_table(table) for table in (y_tables(), z_table(), x_tables()))
    dma = pltpu.SemaphoreType.DMA
    vmem = pltpu.VMEM
    operands = (grid, kernel, nyquist, *map(jnp.asarray, (*ty, *tz, *tx)))
    return pl.pallas_call(
        field_kernel,
        in_specs=[pl.BlockSpec(memory_space=vmem)] * len(operands),
        out_specs=pl.BlockSpec(memory_space=vmem),
        out_shape=jax.ShapeDtypeStruct((36, 4, 48, 128), F32),
        scratch_shapes=[
            vmem((36, 4, 32, 128), F32),
            vmem((2, 36, 8, 128), F32),
            vmem((2, 36, 8, 128), F32),
            vmem((2, 2, 4, 32, 128), F32),
            vmem((CHUNKS, 8, 64, 256), F32),
            vmem((CHUNKS, 8, 64, 256), F32),
            vmem((CHUNKS, 16, 2, 2, 8, 256), F32),
            vmem((2, 2, 512, 256), F32),
            vmem((2, 2, 256, 256), F32),
            vmem((2, 2, 512, 256), F32),
            vmem((CHUNKS, 16, 2, 2, 8, 256), F32),
            vmem((CHUNKS, 8, 64, 256), F32),
            vmem((CHUNKS, 8, 64, 256), F32),
            vmem((4, 256, 128), F32),
            vmem((CHUNKS, 2, 8, 8, 128), F32),
            vmem((CHUNKS, 2, 8, 8, 128), F32),
            vmem((2, 2, 4, 48, 128), F32),
            vmem((2, 2, 4, 48, 128), F32),
            dma((8,)),
            dma((8,)),
            dma,
            dma((CHUNKS,)),
            dma,
            dma,
            dma,
            dma((CHUNKS,)),
            dma,
            dma((CHUNKS,)),
        ],
        compiler_params=pltpu.CompilerParams(
            collective_id=0, has_side_effects=True, vmem_limit_bytes=56 << 20
        ),
        cost_estimate=pl.CostEstimate(flops=10**10, bytes_accessed=10**7, transcendentals=0),
    )(*operands)


def shards(charges, projection, anchors, block_count, near_pairs, near_matrices, kernel_hat):
    slot_count, panels = charges.shape
    x_start = lax.axis_index("pencil") * 32
    z_start = lax.axis_index("slab") * 32
    nyquist = lax.ppermute(kernel_hat[:, 0, :], ("slab", "pencil"), [(64, 0)])
    local = anchors - jnp.stack([x_start, 2, z_start])[None, :]
    codes = local[:, 0] + 32 * local[:, 2] + 1024 * (local[:, 1] % NY)
    grid = scatter(codes, block_count, projection, charges)
    levels = jnp.transpose(kernel_hat.reshape(NX, 4, 2, 128), (0, 2, 1, 3)).reshape(NX * 8, 128)
    potential = field(grid, levels, nyquist.reshape(NX * 2, 128))
    in_use = jnp.arange(slot_count, dtype=jnp.int32) < block_count[0]
    coarse = jnp.where(in_use[:, None], charges, 0.0).astype(BF16)
    sources = coarse[near_pairs[:, 1]]
    pair_terms = jnp.einsum("ntp,np->nt", near_matrices, sources, preferred_element_type=F32)
    return gather(codes, block_count, near_pairs[:, 0][None, :], projection, potential, pair_terms)


def solution(mesh):
    return jax.shard_map(
        shards,
        mesh=mesh,
        in_specs=(
            P(("slab", "pencil"), None),
            P(("slab", "pencil"), None, None),
            P(("slab", "pencil"), None),
            P(("slab", "pencil")),
            P(("slab", "pencil"), None),
            P(("slab", "pencil"), None, None),
            P(None, ("slab", "pencil"), None),
        ),
        out_specs=P(("slab", "pencil"), None),
        check_vma=False,
    )
```

```python
import jax
import jax.numpy as jnp
import ml_dtypes
import numpy as np
from jax import lax
from jax.experimental import pallas as pl
from jax.experimental.pallas import tpu as pltpu
from jax.sharding import PartitionSpec as P

NX, NY, NZ, BOX = 512, 512, 256, 64
GROUP = 32
UNROLL = 4
F32, BF16 = jnp.float32, jnp.bfloat16


def halves(value):
    high = value.astype(BF16)
    return high, (value - high.astype(F32)).astype(BF16)


def lane_sums(value):
    both = jnp.concatenate(halves(value), axis=1)
    return jnp.dot(both, jnp.ones((256, 128), BF16), preferred_element_type=F32)


def window(anchors, slot):
    x_at = anchors[0, slot] - lax.axis_index("pencil") * 32
    z_at = anchors[2, slot] - lax.axis_index("slab") * 32
    y_at = lax.rem(anchors[1, slot] + (NY - 2), NY)
    tile_0 = y_at // 128
    return x_at, z_at + 6, tile_0, lax.rem(tile_0 + 1, 4), lax.rem(y_at, 128)


def window_masks(lane_0):
    row = lax.broadcasted_iota(jnp.int32, (8, 128), 0)
    lane = lax.broadcasted_iota(jnp.int32, (8, 128), 1)
    shifted = lane - row // 4 - lane_0
    return (shifted == 0, shifted == 2), (shifted == -128, shifted == -126)


def scatter_kernel(anchors, count, projection, charges, grid, values):
    step = pl.program_id(0)

    @pl.when(step == 0)
    def _():
        def clear(x, carry):
            grid[x] = jnp.zeros(grid.shape[1:], F32)
            return carry

        lax.fori_loop(0, grid.shape[0], clear, 0)

    slot = step * GROUP + lax.broadcasted_iota(jnp.int32, (GROUP, 128), 0)
    masked = jnp.where(slot < count[0], charges[...], 0.0)
    products = projection[...] * masked[:, None, :]
    values[...] = lane_sums(products.reshape(GROUP * BOX, 128)).reshape(GROUP, BOX, 128)
    top = lax.broadcasted_iota(jnp.int32, (8, 128), 0) < 4

    def place(turn, carry):
        patches = []
        for u in range(UNROLL):
            b = turn * UNROLL + u
            x_at, z_row, tile_0, tile_1, lane_0 = window(anchors, step * GROUP + b)
            for tile, masks in zip((tile_0, tile_1), window_masks(lane_0)):
                for i in range(4):
                    patch = jnp.where(masks[0], values[b, 16 * i : 16 * i + 8], 0.0)
                    patch = jnp.where(masks[1], values[b, 16 * i + 8 : 16 * i + 16], patch)
                    patch = jnp.where(top, patch + pltpu.roll(patch, 4, 0), 0.0)
                    patches.append((x_at + i, tile, pl.ds(z_row, 8), patch))
        for x_at, tile, rows, patch in patches:
            grid[x_at, tile, rows, :] += patch
        return carry

    lax.fori_loop(0, GROUP // UNROLL, place, 0)


def scatter(anchors, count, projection, charges):
    slots = charges.shape[0]
    return pl.pallas_call(
        scatter_kernel,
        grid_spec=pltpu.PrefetchScalarGridSpec(
            num_scalar_prefetch=2,
            grid=(slots // GROUP,),
            in_specs=[
                pl.BlockSpec((GROUP, BOX, 128), lambda i, *_: (i, 0, 0)),
                pl.BlockSpec((GROUP, 128), lambda i, *_: (i, 0)),
            ],
            out_specs=pl.BlockSpec((36, 4, 48, 128), lambda i, *_: (0, 0, 0, 0)),
            scratch_shapes=[pltpu.VMEM((GROUP, BOX, 128), F32)],
        ),
        out_shape=jax.ShapeDtypeStruct((36, 4, 48, 128), F32),
        compiler_params=pltpu.CompilerParams(vmem_limit_bytes=60 << 20),
    )(anchors, count, projection, charges)


def gather_kernel(anchors, count, projection, grid, near, out, picked):
    step = pl.program_id(0)
    top = lax.broadcasted_iota(jnp.int32, (8, 128), 0) < 4

    def pick(turn, carry):
        for u in range(UNROLL):
            b = turn * UNROLL + u
            x_at, z_row, tile_0, tile_1, lane_0 = window(anchors, step * GROUP + b)
            masks_0, masks_1 = window_masks(lane_0)
            for i in range(4):
                both = []
                for tile in (tile_0, tile_1):
                    rows = grid[x_at + i, tile, pl.ds(z_row, 8), :]
                    both.append(jnp.where(top, rows, pltpu.roll(rows, 4, 0)))
                for j in range(2):
                    value = jnp.where(masks_0[j], both[0], jnp.where(masks_1[j], both[1], 0.0))
                    picked[b, 16 * i + 8 * j : 16 * i + 8 * j + 8] = value
        return carry

    lax.fori_loop(0, GROUP // UNROLL, pick, 0)
    box = lane_sums(picked[...].reshape(GROUP * BOX, 128)).reshape(GROUP, BOX, 128)
    far = jnp.sum(projection[...] * box, axis=1)
    slot = step * GROUP + lax.broadcasted_iota(jnp.int32, (GROUP, 128), 0)
    out[...] = jnp.where(slot < count[0], far + near[...], 0.0)


def gather(anchors, count, projection, grid, near):
    slots = projection.shape[0]
    return pl.pallas_call(
        gather_kernel,
        grid_spec=pltpu.PrefetchScalarGridSpec(
            num_scalar_prefetch=2,
            grid=(slots // GROUP,),
            in_specs=[
                pl.BlockSpec((GROUP, BOX, 128), lambda i, *_: (i, 0, 0)),
                pl.BlockSpec((36, 4, 48, 128), lambda i, *_: (0, 0, 0, 0)),
                pl.BlockSpec((GROUP, 128), lambda i, *_: (i, 0)),
            ],
            out_specs=pl.BlockSpec((GROUP, 128), lambda i, *_: (i, 0)),
            scratch_shapes=[pltpu.VMEM((GROUP, BOX, 128), F32)],
        ),
        out_shape=jax.ShapeDtypeStruct((slots, 128), F32),
        compiler_params=pltpu.CompilerParams(vmem_limit_bytes=60 << 20),
    )(anchors, count, projection, grid, near)


CHUNKS = 4
MESH = pl.DeviceIdType.MESH


def phases(product, length):
    angle = 2.0 * np.pi * (product % length) / length
    return np.cos(angle), np.sin(angle)


def split_table(table):
    table = table.astype(np.float32)
    high = table.astype(ml_dtypes.bfloat16)
    return high, (table - high.astype(np.float32)).astype(ml_dtypes.bfloat16)


def y_tables():
    slab, part, pencil = np.meshgrid(np.arange(8), np.arange(2), np.arange(16), indexing="ij")
    device = (slab * 16 + pencil).reshape(-1, 1)
    part = part.reshape(-1, 1)
    even = np.where(device < 64, 4 * device, 4 * device + 2)
    odd = 4 * device + 1
    position = np.arange(256)[None, :]
    result = []
    for freq in (even, odd):
        cos, sin = phases(freq * position, NY)
        table = np.where(part == 0, cos, -sin)
        if freq is even:
            table[(device[:, 0] == 0) & (part[:, 0] == 1)] = 1.0 - 2.0 * (position[0] % 2)
        result.append(table)
    return np.stack(result)


def z_table():
    position = np.arange(NZ)
    cos, sin = phases(position[:, None] * position[None, :], NZ)
    return np.block([[cos, -sin], [sin, cos]])


def x_tables():
    position = np.arange(256)
    result = []
    for parity in range(2):
        cos, sin = phases((2 * position[:, None] + parity) * position[None, :], NX)
        result.append(np.concatenate([cos, sin], axis=1))
        if parity:
            result.append(np.concatenate([cos.T, sin.T], axis=1))
    return np.stack(result)


def dot_3(left, right, dims=((1,), (0,))):
    def one(a, b):
        return lax.dot_general(a, b, (dims, ((), ())), preferred_element_type=F32)

    return one(left[0], right[0]) + (one(left[0], right[1]) + one(left[1], right[0]))


def swap_groups(tiles):
    lane = lax.broadcasted_iota(jnp.int32, tiles[0].shape, 1)
    low, even = lane < 64, lane % 64 < 32
    firsts, lasts = [], []
    for a, b in ((tiles[0], tiles[2]), (tiles[1], tiles[3])):
        firsts.append(jnp.where(low, a, pltpu.roll(b, 64, 1)))
        lasts.append(jnp.where(low, pltpu.roll(a, 64, 1), b))
    result = []
    for a, b in (firsts, lasts):
        result.append(jnp.where(even, a, pltpu.roll(b, 32, 1)))
        result.append(jnp.where(even, pltpu.roll(a, 96, 1), b))
    return result


def field_kernel(
    grid, count, pairs, charges, matrices_at, kernel_at, ty_at, tz_at, tx_at,
    out, near,
    matrices, kernel, ty, tz, tx, sources, terms,
    charge, z_out, z_in, x_in, corner_in, sent_1, got_1, sent_2, got_2, level_out, level_in, spectra, back_2, took_2,
    back_1, took_1, lines, last_z_out, last_z_in, last_x_in, last_corner_in,
    load, level_send, level_recv, rim_send, rim_recv, last_send, last_recv, corner_recv,
    send_1, recv_1, send_2, recv_2, send_3, recv_3, send_4, recv_4,
):
    slab, pencil = lax.axis_index("slab"), lax.axis_index("pencil")
    n_slab, n_pencil = 8, 16

    def at(slab_step, pencil_step):
        return (lax.rem(slab + n_slab + slab_step, n_slab), lax.rem(pencil + n_pencil + pencil_step, n_pencil))

    def on_slab(step):
        return at(step, 0)

    def on_pencil(step):
        return at(0, step)

    def remote(source, target, send_sem, recv_sem, device):
        return pltpu.make_async_remote_copy(
            src_ref=source, dst_ref=target, send_sem=send_sem, recv_sem=recv_sem, device_id=device, device_id_type=MESH
        )

    def wait_recv(ref, sem):
        remote(ref, ref, sem, sem, on_slab(1)).wait_recv()

    def wait_send(ref, sem):
        remote(ref, ref, sem, sem, on_slab(1)).wait_send()

    barrier = pltpu.get_barrier_semaphore()

    def greet(device):
        pl.semaphore_signal(barrier, inc=1, device_id=device, device_id_type=MESH)

    def greet_slab(step, carry):
        greet(on_slab(step))
        return carry

    def greet_pencil(step, carry):
        greet(on_pencil(step))
        return carry

    sides = ((0, -1), (1, 1))
    lax.fori_loop(1, n_slab, greet_slab, 0)
    lax.fori_loop(1, n_pencil, greet_pencil, 0)
    for _, dz in sides:
        for _, dx in sides:
            greet(at(dz, dx))

    loads = [
        pltpu.make_async_copy(source, target, load.at[i])
        for i, (source, target) in enumerate(
            ((ty_at, ty), (tz_at, tz), (kernel_at, kernel), (tx_at, tx), (matrices_at, matrices))
        )
    ]
    for copy in loads:
        copy.start()

    def pack_rims(x, carry):
        for tile in range(4):
            z_out[0, x, 2 * tile : 2 * tile + 2, :] = grid[x, tile, 6:8, :]
            z_out[1, x, 2 * tile : 2 * tile + 2, :] = grid[x, tile, 40:42, :]
        return carry

    lax.fori_loop(0, 36, pack_rims, 0, unroll=4)
    pl.semaphore_wait(barrier, n_slab + n_pencil + 2)
    ends = ((0, 2), (34, 36))
    rims = []
    for a, dz in sides:
        rims.append((z_out.at[a, 2:34], z_in.at[1 - a], on_slab(dz)))
    for b, dx in sides:
        rims.append((grid.at[ends[b][0] : ends[b][1], :, 8:40, :], x_in.at[1 - b], on_pencil(dx)))
    for a, dz in sides:
        for b, dx in sides:
            rims.append((z_out.at[a, ends[b][0] : ends[b][1]], corner_in.at[1 - a, 1 - b], at(dz, dx)))
    for i, (source, target, device) in enumerate(rims):
        remote(source, target, rim_send.at[i], rim_recv.at[i], device).start()

    def bring(x, carry):
        charge[x] = grid[2 + x, :, 8:40, :]
        return carry

    lax.fori_loop(0, 32, bring, 0, unroll=2)
    wait_recv(z_in.at[1], rim_recv.at[0])
    wait_recv(z_in.at[0], rim_recv.at[1])

    def add_rims(x, carry):
        for tile in range(4):
            charge[x, tile, 0:2, :] += z_in[0, x, 2 * tile : 2 * tile + 2, :]
            charge[x, tile, 30:32, :] += z_in[1, x, 2 * tile : 2 * tile + 2, :]
        return carry

    lax.fori_loop(0, 32, add_rims, 0, unroll=4)
    loads[0].wait()

    def forward_y(step, carry):
        chunk = lax.rem(step + 1, CHUNKS)

        @pl.when(step == 2)
        def _():
            for i in range(2, 8):
                wait_recv(rims[i][1], rim_recv.at[i])
            for b, start in ((0, 0), (1, 30)):
                charge[start : start + 2] += x_in[b]
                for a, row in ((0, 0), (1, 30)):
                    for x in range(2):
                        for tile in range(4):
                            charge[start + x, tile, row : row + 2, :] += corner_in[a, b, x, 2 * tile : 2 * tile + 2, :]

        tiles = [charge[pl.ds(8 * chunk, 8), tile].reshape(256, 128) for tile in range(4)]
        for parity in range(2):
            if parity:
                halved = [tiles[0] - tiles[2], tiles[1] - tiles[3]]
            else:
                halved = [tiles[0] + tiles[2], tiles[1] + tiles[3]]
            columns = halves(jnp.concatenate(halved, axis=1))
            freqs = dot_3((ty[0, parity], ty[1, parity]), columns, ((1,), (1,)))
            sent_1[chunk, :, 32 * parity : 32 * parity + 32, :] = freqs.reshape(n_slab, 32, 256)
        got_1[chunk, slab] = sent_1[chunk, slab]

        def send(k, carry):
            device = on_slab(k)
            remote(sent_1.at[chunk, device[0]], got_1.at[chunk, slab], send_1, recv_1.at[chunk], device).start()
            return carry

        return lax.fori_loop(1, n_slab, send, carry)

    lax.fori_loop(0, CHUNKS, forward_y, 0)

    slots, panels = charges.shape
    loads[2].wait()
    first = jnp.logical_and(slab == 0, pencil == 0)
    middle = jnp.logical_and(slab == 4, pencil == 0)

    @pl.when(middle)
    def _():
        for kx in range(2):
            for i in range(2):
                level_out[kx, :, 128 * i : 128 * i + 128] = kernel[pl.ds(8 * kx + 4 * i, 256, stride=16), :]
        remote(level_out, level_in, level_send, level_recv, (0, pencil)).start()

    slot = lax.broadcasted_iota(jnp.int32, (slots, panels), 0)
    coarse = jnp.where(slot < count[...], charges[...], 0.0).astype(BF16)
    slot = lax.broadcasted_iota(jnp.int32, (slots, slots), 0)
    chosen = jnp.where(slot == pairs[1:2, :], 1.0, 0.0)
    sources[...] = jnp.dot(chosen.T.astype(BF16), coarse, preferred_element_type=F32)
    loads[1].wait()
    loads[4].wait()

    def near_group(group, carry):
        rows = pl.ds(pl.multiple_of(8 * group, 8), 8)
        taken = sources[rows, :].astype(BF16)
        row = lax.broadcasted_iota(jnp.int32, (8, panels), 0)
        total = jnp.zeros((8, panels), F32)
        for i in range(8):
            found = lax.dot_general(
                taken, matrices[8 * group + i], (((1,), (1,)), ((), ())), preferred_element_type=F32
            )
            total = jnp.where(row == i, found, total)
        terms[rows, :] = total
        return carry

    near_groups = slots // 8 // (2 * CHUNKS)

    def near_share(turn):
        lax.fori_loop(turn * near_groups, (turn + 1) * near_groups, near_group, 0)

    def forward_z(step, carry):
        chunk = lax.rem(step + 1, CHUNKS)
        near_share(step)
        wait_recv(got_1.at[chunk, 0 : n_slab - 1], recv_1.at[chunk])
        for h in range(2):
            for q in range(2):
                tiles = swap_groups([got_1[chunk, 4 * q + s, :, 128 * h : 128 * h + 128] for s in range(4)])
                for a in range(4):
                    for parity in range(2):
                        for part in range(2):
                            row = 32 * parity + 16 * part
                            lines[2 * part + q, pl.ds(128 * parity + 4 * h + a, 16, stride=8), :] = tiles[a][row : row + 16]
        rows = halves(jnp.concatenate([lines[i] for i in range(4)], axis=1))
        freqs = dot_3(rows, (tz[0], tz[1]))
        for parity in range(2):
            for part in range(2):
                block = freqs[128 * parity : 128 * parity + 128, 256 * part : 256 * part + 256]
                sent_2[chunk, :, parity, part] = block.reshape(n_pencil, 8, 256)
        mine = pl.ds(pl.multiple_of(pencil * 32 + chunk * 8, 8), 8)
        got_2[:, :, mine, :] = sent_2[chunk, pencil]

        def send(k, carry):
            device = on_pencil(k)
            remote(sent_2.at[chunk, device[1]], got_2.at[:, :, mine, :], send_2, recv_2, device).start()
            return carry

        return lax.fori_loop(1, n_pencil, send, carry)

    lax.fori_loop(0, CHUNKS, forward_z, 0)
    wait_recv(got_2.at[:, :, 0 : 32 * (n_pencil - 1), :], recv_2)

    loads[3].wait()
    unit = 1.0 / (NX * NY * NZ)

    def stacked(real, imag):
        real, imag = halves(real), halves(imag)
        return tuple(
            jnp.concatenate([jnp.concatenate([r, i], axis=1), jnp.concatenate([i, -r], axis=1)], axis=0)
            for r, i in zip(real, imag)
        )

    for parity in range(2):
        for kx in range(2):
            parts = []
            for part in range(2):
                low, high = got_2[parity, part, 0:256, :], got_2[parity, part, 256:512, :]
                parts.append(low - high if kx else low + high)
            table = (tx[0, kx], tx[1, kx])
            found = dot_3(table, stacked(*parts))
            if parity:
                green = jnp.concatenate(
                    [kernel[pl.ds(8 * kx + 4 * i + 1, 256, stride=16), :] for i in range(2)], axis=1
                ) * (2.0 * unit)
            else:
                own = jnp.where(slab < 4, 0, 2)
                green = jnp.concatenate(
                    [kernel[pl.ds(own + 8 * kx + 4 * i, 256, stride=16), :] for i in range(2)], axis=1
                ) * jnp.where(first, unit, 2.0 * unit)
            spectra[kx, 0] = found[:, 0:256] * green
            spectra[kx, 1] = found[:, 256:512] * green
            if not parity:

                @pl.when(first)
                def _():
                    if not kx:
                        wait_recv(level_in, level_recv)
                    other = level_in[kx] * unit
                    row = lax.broadcasted_iota(jnp.int32, (256, 256), 0)
                    lane = lax.broadcasted_iota(jnp.int32, (256, 256), 1)
                    mirror = jnp.where((row + lane) % 256 == 0, 1.0, 0.0).astype(BF16)
                    flipped = [
                        sum(jnp.dot(piece, mirror, preferred_element_type=F32) for piece in halves(value)) for value in parts
                    ]
                    twin = dot_3(table, stacked(flipped[0], -flipped[1]))
                    mean, rest = 0.5 * (green + other), 0.5 * (green - other)
                    for part in range(2):
                        lanes = slice(256 * part, 256 * part + 256)
                        spectra[kx, part] = mean * found[:, lanes] + rest * twin[:, lanes]

        ends = []
        for kx in range(2):
            table = (tx[0, 2 * kx], tx[1, 2 * kx])
            real, imag = halves(spectra[kx, 0]), halves(spectra[kx, 1])
            right = tuple(
                jnp.concatenate([jnp.concatenate([r, i], axis=1), jnp.concatenate([-i, r], axis=1)], axis=0)
                for r, i in zip(real, imag)
            )
            ends.append(dot_3(table, right))
        for part in range(2):
            lanes = slice(256 * part, 256 * part + 256)
            back_2[parity, part, 0:256, :] = ends[0][:, lanes] + ends[1][:, lanes]
            back_2[parity, part, 256:512, :] = ends[0][:, lanes] - ends[1][:, lanes]

    def turns(step):
        return jnp.where(step < 2, 3 * step, step - 1)

    def return_x(step, carry):
        chunk = turns(step)
        own = pl.ds(pl.multiple_of(pencil * 32 + chunk * 8, 8), 8)
        took_2[chunk, pencil] = back_2[:, :, own, :]

        def send(k, carry):
            device = on_pencil(k)
            rows = pl.ds(pl.multiple_of(device[1] * 32 + chunk * 8, 8), 8)
            remote(back_2.at[:, :, rows, :], took_2.at[chunk, pencil], send_3, recv_3.at[chunk], device).start()
            return carry

        return lax.fori_loop(1, n_pencil, send, carry)

    lax.fori_loop(0, CHUNKS, return_x, 0)

    def inverse_z(step, carry):
        chunk = turns(step)
        near_share(CHUNKS + step)
        wait_recv(took_2.at[chunk, 0 : n_pencil - 1], recv_3.at[chunk])
        blocks = []
        for parity in range(2):
            blocks.append(jnp.concatenate([took_2[chunk, :, parity, part].reshape(128, 256) for part in range(2)], axis=1))
        rows = halves(jnp.concatenate(blocks, axis=0))
        space = dot_3(rows, (tz[0], tz[1]), ((1,), (1,)))
        for i in range(4):
            lines[i] = space[:, 128 * i : 128 * i + 128]
        for h in range(2):
            for q in range(2):
                tiles = []
                for a in range(4):
                    tiles.append(
                        jnp.concatenate(
                            [
                                lines[2 * part + q, pl.ds(128 * parity + 4 * h + a, 16, stride=8), :]
                                for parity in range(2)
                                for part in range(2)
                            ],
                            axis=0,
                        )
                    )
                for s, tile in enumerate(swap_groups(tiles)):
                    back_1[chunk, 4 * q + s, :, 128 * h : 128 * h + 128] = tile
        took_1[chunk, slab] = back_1[chunk, slab]

        def send(k, carry):
            device = on_slab(k)
            remote(back_1.at[chunk, device[0]], took_1.at[chunk, slab], send_4, recv_4.at[chunk], device).start()
            return carry

        return lax.fori_loop(1, n_slab, send, carry)

    lax.fori_loop(0, CHUNKS, inverse_z, 0)

    slot = lax.broadcasted_iota(jnp.int32, (slots, slots), 0)
    chosen = jnp.where(slot == pairs[0:1, :], 1.0, 0.0).astype(BF16)
    rest = terms[...]
    total = jnp.zeros(near.shape, F32)
    for _ in range(3):
        part = rest.astype(BF16)
        rest = rest - part.astype(F32)
        total = total + jnp.dot(chosen, part, preferred_element_type=F32)
    near[...] = total

    row_ends = ((2, 4), (32, 34))
    last = []
    for b, dx in sides:
        last.append((out.at[row_ends[b][0] : row_ends[b][1], :, 8:40, :], last_x_in.at[1 - b], on_pencil(dx)))
        for a, dz in sides:
            rows = (0, 2) if b == 0 else (6, 8)
            last.append(
                (last_z_out.at[3 * b, a, rows[0] : rows[1]], last_corner_in.at[1 - b, 1 - a], at(dz, dx))
            )

    def planes(chunk, a):
        return (last_z_out.at[chunk, a], last_z_in.at[chunk, 1 - a], last_send.at[6 + a], last_recv.at[chunk, 1 - a])

    def take_planes(step, carry):
        chunk = turns(step)
        for a, row in ((0, 6), (1, 40)):
            wait_recv(last_z_in.at[chunk, a], last_recv.at[chunk, a])
            for x in range(8):
                for tile in range(4):
                    out[2 + 8 * chunk + x, tile, row : row + 2, :] = last_z_in[chunk, a, x, 2 * tile : 2 * tile + 2, :]
        return carry

    def inverse_y(step, carry):
        chunk = turns(step)
        wait_recv(took_1.at[chunk, 0 : n_slab - 1], recv_4.at[chunk])
        ends = []
        for parity in range(2):
            columns = took_1[chunk, :, 32 * parity : 32 * parity + 32, :].reshape(256, 256).T
            ends.append(dot_3(halves(columns), (ty[0, parity], ty[1, parity])))
        space = (ends[0] + ends[1], ends[0] - ends[1])
        for tile in range(4):
            lanes = slice(128 * (tile % 2), 128 * (tile % 2) + 128)
            cells = space[tile // 2][:, lanes].reshape(8, 32, 128)
            out[pl.ds(2 + 8 * chunk, 8), tile, 8:40, :] = cells
            last_z_out[chunk, 0, :, 2 * tile : 2 * tile + 2, :] = cells[:, 0:2, :]
            last_z_out[chunk, 1, :, 2 * tile : 2 * tile + 2, :] = cells[:, 30:32, :]
        for a, dz in sides:
            remote(*planes(chunk, a), on_slab(dz)).start()
        for b in range(2):

            @pl.when(chunk == 3 * b)
            def _():
                for i in range(3 * b, 3 * b + 3):
                    source, target, device = last[i]
                    remote(source, target, last_send.at[i], corner_recv.at[i], device).start()

        return carry

    lax.fori_loop(0, CHUNKS, inverse_y, 0)
    lax.fori_loop(0, CHUNKS - 1, take_planes, 0)
    for i, (source, target, device) in enumerate(last):
        wait_recv(target, corner_recv.at[i])
        wait_send(source, last_send.at[i])
    for b, start in ((0, 0), (1, 34)):
        out[start : start + 2, :, 8:40, :] = last_x_in[b]
        for a, row in ((0, 6), (1, 40)):
            for x in range(2):
                for tile in range(4):
                    out[start + x, tile, row : row + 2, :] = last_corner_in[b, a, x, 2 * tile : 2 * tile + 2, :]
    for i, (source, target, device) in enumerate(rims):
        wait_send(source, rim_send.at[i])
    wait_send(sent_1.at[:, 0 : n_slab - 1], send_1)
    wait_send(got_2.at[:, :, 0 : 32 * (n_pencil - 1), :], send_2)
    wait_send(got_2.at[:, :, 0 : 32 * (n_pencil - 1), :], send_3)
    wait_send(back_1.at[:, 0 : n_slab - 1], send_4)

    @pl.when(middle)
    def _():
        wait_send(level_out, level_send)

    take_planes(CHUNKS - 1, 0)
    for a in range(2):
        wait_send(last_z_out.at[:, a], last_send.at[6 + a])


def field(grid, count, pairs, charges, matrices, kernel):
    tables = [jnp.asarray(np.stack(split_table(table))) for table in (y_tables(), z_table(), x_tables())]
    slots, panels = charges.shape
    dma = pltpu.SemaphoreType.DMA
    vmem = pltpu.VMEM
    return pl.pallas_call(
        field_kernel,
        in_specs=[pl.BlockSpec(memory_space=vmem)] * 4 + [pl.BlockSpec(memory_space=pl.ANY)] * 5,
        out_specs=[pl.BlockSpec(memory_space=vmem)] * 2,
        out_shape=[
            jax.ShapeDtypeStruct((36, 4, 48, 128), F32),
            jax.ShapeDtypeStruct((slots, panels), F32),
        ],
        scratch_shapes=[
            vmem(matrices.shape, BF16),
            vmem(kernel.shape, F32),
            *(vmem(table.shape, BF16) for table in tables),
            vmem((slots, panels), F32),
            vmem((slots, panels), F32),
            vmem((32, 4, 32, 128), F32),
            vmem((2, 36, 8, 128), F32),
            vmem((2, 32, 8, 128), F32),
            vmem((2, 2, 4, 32, 128), F32),
            vmem((2, 2, 2, 8, 128), F32),
            vmem((CHUNKS, 8, 64, 256), F32),
            vmem((CHUNKS, 8, 64, 256), F32),
            vmem((CHUNKS, 16, 2, 2, 8, 256), F32),
            vmem((2, 2, 512, 256), F32),
            vmem((2, 256, 256), F32),
            vmem((2, 256, 256), F32),
            vmem((2, 2, 256, 256), F32),
            vmem((2, 2, 512, 256), F32),
            vmem((CHUNKS, 16, 2, 2, 8, 256), F32),
            vmem((CHUNKS, 8, 64, 256), F32),
            vmem((CHUNKS, 8, 64, 256), F32),
            vmem((4, 256, 128), F32),
            vmem((CHUNKS, 2, 8, 8, 128), F32),
            vmem((CHUNKS, 2, 8, 8, 128), F32),
            vmem((2, 2, 4, 32, 128), F32),
            vmem((2, 2, 2, 8, 128), F32),
            dma((5,)),
            dma,
            dma,
            dma((8,)),
            dma((8,)),
            dma((8,)),
            dma((CHUNKS, 2)),
            dma((6,)),
            dma,
            dma((CHUNKS,)),
            dma,
            dma,
            dma,
            dma((CHUNKS,)),
            dma,
            dma((CHUNKS,)),
        ],
        compiler_params=pltpu.CompilerParams(
            collective_id=0, has_side_effects=True, vmem_limit_bytes=58 << 20
        ),
        cost_estimate=pl.CostEstimate(flops=10**10, bytes_accessed=10**7, transcendentals=0),
    )(grid, count, pairs, charges, matrices, kernel, *tables)


def shards(charges, projection, anchors, block_count, near_pairs, near_matrices, kernel_hat):
    panels = charges.shape[1]
    grid = scatter(anchors.T, block_count, projection, charges)
    levels = jnp.transpose(kernel_hat.reshape(NX, 4, 2, 128), (0, 2, 1, 3)).reshape(NX * 8, 128)
    count = jnp.broadcast_to(block_count[:, None], (1, panels))
    potential, near = field(grid, count, near_pairs.T, charges, near_matrices, levels)
    return gather(anchors.T, block_count, projection, potential, near)


def solution(mesh):
    return jax.shard_map(
        shards,
        mesh=mesh,
        in_specs=(
            P(("slab", "pencil"), None),
            P(("slab", "pencil"), None, None),
            P(("slab", "pencil"), None),
            P(("slab", "pencil")),
            P(("slab", "pencil"), None),
            P(("slab", "pencil"), None, None),
            P(None, ("slab", "pencil"), None),
        ),
        out_specs=P(("slab", "pencil"), None),
        check_vma=False,
    )
```

```python
import jax
import jax.numpy as jnp
import ml_dtypes
import numpy as np
from jax import lax
from jax.experimental import pallas as pl
from jax.experimental.pallas import tpu as pltpu
from jax.sharding import PartitionSpec as P

NX, NY, NZ, BOX = 512, 512, 256, 64
GROUP = 32
UNROLL = 4
F32, BF16 = jnp.float32, jnp.bfloat16


def halves(value):
    high = value.astype(BF16)
    return high, (value - high.astype(F32)).astype(BF16)


def lane_sums(value):
    both = jnp.concatenate(halves(value), axis=1)
    return jnp.dot(both, jnp.ones((256, 128), BF16), preferred_element_type=F32)


def window(anchors, slot):
    x_at = lax.rem(anchors[0, slot], 32)
    z_at = lax.rem(anchors[2, slot], 32)
    y_at = lax.rem(anchors[1, slot] + (NY - 2), NY)
    tile_0 = y_at // 128
    return x_at, z_at + 6, tile_0, lax.rem(tile_0 + 1, 4), lax.rem(y_at, 128)


def window_masks(lane_0):
    row = lax.broadcasted_iota(jnp.int32, (8, 128), 0)
    lane = lax.broadcasted_iota(jnp.int32, (8, 128), 1)
    shifted = lane - row // 4 - lane_0
    return (shifted == 0, shifted == 2), (shifted == -128, shifted == -126)


def group_loads(source, target, sems):
    return [
        pltpu.make_async_copy(source.at[i * GROUP : (i + 1) * GROUP], target.at[i * GROUP : (i + 1) * GROUP], sems.at[i])
        for i in range(source.shape[0] // GROUP)
    ]


def group_wait(step, source, target, sems):
    rows = pl.ds(pl.multiple_of(step * GROUP, GROUP), GROUP)
    pltpu.make_async_copy(source.at[rows], target.at[rows], sems.at[step]).wait()
    return rows


def scatter_kernel(anchors, count, projection_at, charges, grid, projection, values, load):
    for copy in group_loads(projection_at, projection, load):
        copy.start()

    def clear(x, carry):
        grid[x] = jnp.zeros(grid.shape[1:], F32)
        return carry

    lax.fori_loop(0, grid.shape[0], clear, 0)
    top = lax.broadcasted_iota(jnp.int32, (8, 128), 0) < 4

    def group(step, carry):
        rows = group_wait(step, projection_at, projection, load)
        slot = step * GROUP + lax.broadcasted_iota(jnp.int32, (GROUP, 128), 0)
        masked = jnp.where(slot < count[0], charges[rows, :], 0.0)
        products = projection[rows] * masked[:, None, :]
        values[...] = lane_sums(products.reshape(GROUP * BOX, 128)).reshape(GROUP, BOX, 128)

        def place(turn, carry):
            patches = []
            for u in range(UNROLL):
                b = turn * UNROLL + u
                x_at, z_row, tile_0, tile_1, lane_0 = window(anchors, step * GROUP + b)
                for tile, masks in zip((tile_0, tile_1), window_masks(lane_0)):
                    for i in range(4):
                        patch = jnp.where(masks[0], values[b, 16 * i : 16 * i + 8], 0.0)
                        patch = jnp.where(masks[1], values[b, 16 * i + 8 : 16 * i + 16], patch)
                        patch = jnp.where(top, patch + pltpu.roll(patch, 4, 0), 0.0)
                        patches.append((x_at + i, tile, pl.ds(z_row, 8), patch))
            for x_at, tile, rows, patch in patches:
                grid[x_at, tile, rows, :] += patch
            return carry

        return lax.fori_loop(0, GROUP // UNROLL, place, carry)

    lax.fori_loop(0, charges.shape[0] // GROUP, group, 0)


def scatter(anchors, count, projection, charges):
    slots = charges.shape[0]
    smem, vmem = pl.BlockSpec(memory_space=pltpu.SMEM), pl.BlockSpec(memory_space=pltpu.VMEM)
    return pl.pallas_call(
        scatter_kernel,
        in_specs=[smem, smem, pl.BlockSpec(memory_space=pl.ANY), vmem],
        out_specs=vmem,
        scratch_shapes=[
            pltpu.VMEM(projection.shape, F32),
            pltpu.VMEM((GROUP, BOX, 128), F32),
            pltpu.SemaphoreType.DMA((slots // GROUP,)),
        ],
        out_shape=jax.ShapeDtypeStruct((36, 4, 48, 128), F32),
        compiler_params=pltpu.CompilerParams(vmem_limit_bytes=60 << 20),
    )(anchors, count, projection, charges)


CHUNKS = 4
MESH = pl.DeviceIdType.MESH


def phases(product, length):
    angle = 2.0 * np.pi * (product % length) / length
    return np.cos(angle), np.sin(angle)


def split_table(table):
    table = table.astype(np.float32)
    high = table.astype(ml_dtypes.bfloat16)
    return high, (table - high.astype(np.float32)).astype(ml_dtypes.bfloat16)


def y_tables():
    slab, part, pencil = np.meshgrid(np.arange(8), np.arange(2), np.arange(16), indexing="ij")
    device = (slab * 16 + pencil).reshape(-1, 1)
    part = part.reshape(-1, 1)
    even = np.where(device < 64, 4 * device, 4 * device + 2)
    odd = 4 * device + 1
    position = np.arange(256)[None, :]
    result = []
    for freq in (even, odd):
        cos, sin = phases(freq * position, NY)
        table = np.where(part == 0, cos, -sin)
        if freq is even:
            table[(device[:, 0] == 0) & (part[:, 0] == 1)] = 1.0 - 2.0 * (position[0] % 2)
        result.append(table)
    return np.stack(result)


def z_table():
    position = np.arange(NZ)
    cos, sin = phases(position[:, None] * position[None, :], NZ)
    return np.block([[cos, -sin], [sin, cos]])


def x_tables():
    position = np.arange(256)
    result = []
    for parity in range(2):
        cos, sin = phases((2 * position[:, None] + parity) * position[None, :], NX)
        result.append(np.concatenate([cos, sin], axis=1))
        if parity:
            result.append(np.concatenate([cos.T, sin.T], axis=1))
    return np.stack(result)


def dot_3(left, right, dims=((1,), (0,))):
    def one(a, b):
        return lax.dot_general(a, b, (dims, ((), ())), preferred_element_type=F32)

    return one(left[0], right[0]) + (one(left[0], right[1]) + one(left[1], right[0]))


def swap_groups(tiles):
    lane = lax.broadcasted_iota(jnp.int32, tiles[0].shape, 1)
    low, even = lane < 64, lane % 64 < 32
    firsts, lasts = [], []
    for a, b in ((tiles[0], tiles[2]), (tiles[1], tiles[3])):
        firsts.append(jnp.where(low, a, pltpu.roll(b, 64, 1)))
        lasts.append(jnp.where(low, pltpu.roll(a, 64, 1), b))
    result = []
    for a, b in (firsts, lasts):
        result.append(jnp.where(even, a, pltpu.roll(b, 32, 1)))
        result.append(jnp.where(even, pltpu.roll(a, 96, 1), b))
    return result


def field_kernel(
    anchors, count, pairs, charges, grid_at, projection_at, matrices_at, kernel_at, ty_at, tz_at, tx_at,
    result,
    projection, matrices, kernel, ty, tz, tx, sources, terms, near, values, out,
    charge, z_rows, z_out, z_in, x_in, corner_in, sent_1, got_1, sent_2, got_2, level_out, level_in, spectra, back_2, took_2,
    back_1, took_1, lines, last_z_out, last_z_in, last_x_in, last_corner_in,
    load, group_load, level_send, level_recv, rim_send, rim_recv, last_send, last_recv, corner_recv,
    send_1, recv_1, send_2, recv_2, send_3, recv_3, send_4, recv_4,
):
    slab, pencil = lax.axis_index("slab"), lax.axis_index("pencil")
    n_slab, n_pencil = 8, 16

    def at(slab_step, pencil_step):
        return (lax.rem(slab + n_slab + slab_step, n_slab), lax.rem(pencil + n_pencil + pencil_step, n_pencil))

    def on_slab(step):
        return at(step, 0)

    def on_pencil(step):
        return at(0, step)

    def remote(source, target, send_sem, recv_sem, device):
        return pltpu.make_async_remote_copy(
            src_ref=source, dst_ref=target, send_sem=send_sem, recv_sem=recv_sem, device_id=device, device_id_type=MESH
        )

    def wait_recv(ref, sem):
        remote(ref, ref, sem, sem, on_slab(1)).wait_recv()

    def wait_send(ref, sem):
        remote(ref, ref, sem, sem, on_slab(1)).wait_send()

    barrier = pltpu.get_barrier_semaphore()

    def greet(device):
        pl.semaphore_signal(barrier, inc=1, device_id=device, device_id_type=MESH)

    def greet_slab(step, carry):
        greet(on_slab(step))
        return carry

    def greet_pencil(step, carry):
        greet(on_pencil(step))
        return carry

    sides = ((0, -1), (1, 1))
    lax.fori_loop(1, n_slab, greet_slab, 0)
    lax.fori_loop(1, n_pencil, greet_pencil, 0)
    for _, dz in sides:
        for _, dx in sides:
            greet(at(dz, dx))

    loads = [
        pltpu.make_async_copy(source, target, load.at[i])
        for i, (source, target) in enumerate(
            (
                (grid_at.at[:, :, 0:8, :], z_rows.at[0]),
                (grid_at.at[:, :, 40:48, :], z_rows.at[1]),
                (grid_at.at[2:34, :, 8:40, :], charge),
                (ty_at, ty),
                (tz_at, tz),
                (kernel_at, kernel),
                (tx_at, tx),
                (matrices_at, matrices),
            )
        )
    ]
    for copy in loads + group_loads(projection_at, projection, group_load):
        copy.start()

    def pack_rims(x, carry):
        for tile in range(4):
            z_out[0, x, 2 * tile : 2 * tile + 2, :] = z_rows[0, x, tile, 6:8, :]
            z_out[1, x, 2 * tile : 2 * tile + 2, :] = z_rows[1, x, tile, 0:2, :]
        return carry

    loads[0].wait()
    loads[1].wait()
    lax.fori_loop(0, 36, pack_rims, 0, unroll=4)
    pl.semaphore_wait(barrier, n_slab + n_pencil + 2)
    ends = ((0, 2), (34, 36))
    rims = []
    for a, dz in sides:
        rims.append((z_out.at[a, 2:34], z_in.at[1 - a], on_slab(dz)))
    for b, dx in sides:
        rims.append((grid_at.at[ends[b][0] : ends[b][1], :, 8:40, :], x_in.at[1 - b], on_pencil(dx)))
    for a, dz in sides:
        for b, dx in sides:
            rims.append((z_out.at[a, ends[b][0] : ends[b][1]], corner_in.at[1 - a, 1 - b], at(dz, dx)))
    for i, (source, target, device) in enumerate(rims):
        remote(source, target, rim_send.at[i], rim_recv.at[i], device).start()

    loads[2].wait()
    wait_recv(z_in.at[1], rim_recv.at[0])
    wait_recv(z_in.at[0], rim_recv.at[1])

    def add_rims(x, carry):
        for tile in range(4):
            charge[x, tile, 0:2, :] += z_in[0, x, 2 * tile : 2 * tile + 2, :]
            charge[x, tile, 30:32, :] += z_in[1, x, 2 * tile : 2 * tile + 2, :]
        return carry

    lax.fori_loop(0, 32, add_rims, 0, unroll=4)
    loads[3].wait()

    def forward_y(step, carry):
        chunk = lax.rem(step + 1, CHUNKS)

        @pl.when(step == 2)
        def _():
            for i in range(2, 8):
                wait_recv(rims[i][1], rim_recv.at[i])
            for b, start in ((0, 0), (1, 30)):
                charge[start : start + 2] += x_in[b]
                for a, row in ((0, 0), (1, 30)):
                    for x in range(2):
                        for tile in range(4):
                            charge[start + x, tile, row : row + 2, :] += corner_in[a, b, x, 2 * tile : 2 * tile + 2, :]

        tiles = [charge[pl.ds(8 * chunk, 8), tile].reshape(256, 128) for tile in range(4)]
        for parity in range(2):
            if parity:
                halved = [tiles[0] - tiles[2], tiles[1] - tiles[3]]
            else:
                halved = [tiles[0] + tiles[2], tiles[1] + tiles[3]]
            columns = halves(jnp.concatenate(halved, axis=1))
            freqs = dot_3((ty[0, parity], ty[1, parity]), columns, ((1,), (1,)))
            sent_1[chunk, :, 32 * parity : 32 * parity + 32, :] = freqs.reshape(n_slab, 32, 256)
        got_1[chunk, slab] = sent_1[chunk, slab]

        def send(k, carry):
            device = on_slab(k)
            remote(sent_1.at[chunk, device[0]], got_1.at[chunk, slab], send_1, recv_1.at[chunk], device).start()
            return carry

        return lax.fori_loop(1, n_slab, send, carry)

    lax.fori_loop(0, CHUNKS, forward_y, 0)

    slots, panels = charges.shape
    loads[5].wait()
    first = jnp.logical_and(slab == 0, pencil == 0)
    middle = jnp.logical_and(slab == 4, pencil == 0)

    @pl.when(middle)
    def _():
        for kx in range(2):
            for i in range(2):
                level_out[kx, :, 128 * i : 128 * i + 128] = kernel[pl.ds(8 * kx + 4 * i, 256, stride=16), :]
        remote(level_out, level_in, level_send, level_recv, (0, pencil)).start()

    slot = lax.broadcasted_iota(jnp.int32, (slots, panels), 0)
    coarse = jnp.where(slot < count[...], charges[...], 0.0).astype(BF16)
    slot = lax.broadcasted_iota(jnp.int32, (slots, slots), 0)
    chosen = jnp.where(slot == pairs[1:2, :], 1.0, 0.0)
    sources[...] = jnp.dot(chosen.T.astype(BF16), coarse, preferred_element_type=F32)
    loads[4].wait()
    loads[7].wait()

    def near_group(group, carry):
        rows = pl.ds(pl.multiple_of(8 * group, 8), 8)
        taken = sources[rows, :].astype(BF16)
        row = lax.broadcasted_iota(jnp.int32, (8, panels), 0)
        total = jnp.zeros((8, panels), F32)
        for i in range(8):
            found = lax.dot_general(
                taken, matrices[8 * group + i], (((1,), (1,)), ((), ())), preferred_element_type=F32
            )
            total = jnp.where(row == i, found, total)
        terms[rows, :] = total
        return carry

    near_groups = slots // 8 // (2 * CHUNKS)

    def near_share(turn):
        lax.fori_loop(turn * near_groups, (turn + 1) * near_groups, near_group, 0)

    def forward_z(step, carry):
        chunk = lax.rem(step + 1, CHUNKS)
        near_share(step)
        wait_recv(got_1.at[chunk, 0 : n_slab - 1], recv_1.at[chunk])
        for h in range(2):
            for q in range(2):
                tiles = swap_groups([got_1[chunk, 4 * q + s, :, 128 * h : 128 * h + 128] for s in range(4)])
                for a in range(4):
                    for parity in range(2):
                        for part in range(2):
                            row = 32 * parity + 16 * part
                            lines[2 * part + q, pl.ds(128 * parity + 4 * h + a, 16, stride=8), :] = tiles[a][row : row + 16]
        rows = halves(jnp.concatenate([lines[i] for i in range(4)], axis=1))
        freqs = dot_3(rows, (tz[0], tz[1]))
        for parity in range(2):
            for part in range(2):
                block = freqs[128 * parity : 128 * parity + 128, 256 * part : 256 * part + 256]
                sent_2[chunk, :, parity, part] = block.reshape(n_pencil, 8, 256)
        mine = pl.ds(pl.multiple_of(pencil * 32 + chunk * 8, 8), 8)
        got_2[:, :, mine, :] = sent_2[chunk, pencil]

        def send(k, carry):
            device = on_pencil(k)
            remote(sent_2.at[chunk, device[1]], got_2.at[:, :, mine, :], send_2, recv_2, device).start()
            return carry

        return lax.fori_loop(1, n_pencil, send, carry)

    lax.fori_loop(0, CHUNKS, forward_z, 0)
    wait_recv(got_2.at[:, :, 0 : 32 * (n_pencil - 1), :], recv_2)

    loads[6].wait()
    unit = 1.0 / (NX * NY * NZ)

    def stacked(real, imag):
        real, imag = halves(real), halves(imag)
        return tuple(
            jnp.concatenate([jnp.concatenate([r, i], axis=1), jnp.concatenate([i, -r], axis=1)], axis=0)
            for r, i in zip(real, imag)
        )

    for parity in range(2):
        for kx in range(2):
            parts = []
            for part in range(2):
                low, high = got_2[parity, part, 0:256, :], got_2[parity, part, 256:512, :]
                parts.append(low - high if kx else low + high)
            table = (tx[0, kx], tx[1, kx])
            found = dot_3(table, stacked(*parts))
            if parity:
                green = jnp.concatenate(
                    [kernel[pl.ds(8 * kx + 4 * i + 1, 256, stride=16), :] for i in range(2)], axis=1
                ) * (2.0 * unit)
            else:
                own = jnp.where(slab < 4, 0, 2)
                green = jnp.concatenate(
                    [kernel[pl.ds(own + 8 * kx + 4 * i, 256, stride=16), :] for i in range(2)], axis=1
                ) * jnp.where(first, unit, 2.0 * unit)
            spectra[kx, 0] = found[:, 0:256] * green
            spectra[kx, 1] = found[:, 256:512] * green
            if not parity:

                @pl.when(first)
                def _():
                    if not kx:
                        wait_recv(level_in, level_recv)
                    other = level_in[kx] * unit
                    row = lax.broadcasted_iota(jnp.int32, (256, 256), 0)
                    lane = lax.broadcasted_iota(jnp.int32, (256, 256), 1)
                    mirror = jnp.where((row + lane) % 256 == 0, 1.0, 0.0).astype(BF16)
                    flipped = [
                        sum(jnp.dot(piece, mirror, preferred_element_type=F32) for piece in halves(value)) for value in parts
                    ]
                    twin = dot_3(table, stacked(flipped[0], -flipped[1]))
                    mean, rest = 0.5 * (green + other), 0.5 * (green - other)
                    for part in range(2):
                        lanes = slice(256 * part, 256 * part + 256)
                        spectra[kx, part] = mean * found[:, lanes] + rest * twin[:, lanes]

        ends = []
        for kx in range(2):
            table = (tx[0, 2 * kx], tx[1, 2 * kx])
            real, imag = halves(spectra[kx, 0]), halves(spectra[kx, 1])
            right = tuple(
                jnp.concatenate([jnp.concatenate([r, i], axis=1), jnp.concatenate([-i, r], axis=1)], axis=0)
                for r, i in zip(real, imag)
            )
            ends.append(dot_3(table, right))
        for part in range(2):
            lanes = slice(256 * part, 256 * part + 256)
            back_2[parity, part, 0:256, :] = ends[0][:, lanes] + ends[1][:, lanes]
            back_2[parity, part, 256:512, :] = ends[0][:, lanes] - ends[1][:, lanes]

    def turns(step):
        return jnp.where(step < 2, 3 * step, step - 1)

    def return_x(step, carry):
        chunk = turns(step)
        own = pl.ds(pl.multiple_of(pencil * 32 + chunk * 8, 8), 8)
        took_2[chunk, pencil] = back_2[:, :, own, :]

        def send(k, carry):
            device = on_pencil(k)
            rows = pl.ds(pl.multiple_of(device[1] * 32 + chunk * 8, 8), 8)
            remote(back_2.at[:, :, rows, :], took_2.at[chunk, pencil], send_3, recv_3.at[chunk], device).start()
            return carry

        return lax.fori_loop(1, n_pencil, send, carry)

    lax.fori_loop(0, CHUNKS, return_x, 0)

    def inverse_z(step, carry):
        chunk = turns(step)
        near_share(CHUNKS + step)
        wait_recv(took_2.at[chunk, 0 : n_pencil - 1], recv_3.at[chunk])
        blocks = []
        for parity in range(2):
            blocks.append(jnp.concatenate([took_2[chunk, :, parity, part].reshape(128, 256) for part in range(2)], axis=1))
        rows = halves(jnp.concatenate(blocks, axis=0))
        space = dot_3(rows, (tz[0], tz[1]), ((1,), (1,)))
        for i in range(4):
            lines[i] = space[:, 128 * i : 128 * i + 128]
        for h in range(2):
            for q in range(2):
                tiles = []
                for a in range(4):
                    tiles.append(
                        jnp.concatenate(
                            [
                                lines[2 * part + q, pl.ds(128 * parity + 4 * h + a, 16, stride=8), :]
                                for parity in range(2)
                                for part in range(2)
                            ],
                            axis=0,
                        )
                    )
                for s, tile in enumerate(swap_groups(tiles)):
                    back_1[chunk, 4 * q + s, :, 128 * h : 128 * h + 128] = tile
        took_1[chunk, slab] = back_1[chunk, slab]

        def send(k, carry):
            device = on_slab(k)
            remote(back_1.at[chunk, device[0]], took_1.at[chunk, slab], send_4, recv_4.at[chunk], device).start()
            return carry

        return lax.fori_loop(1, n_slab, send, carry)

    lax.fori_loop(0, CHUNKS, inverse_z, 0)

    slot = lax.broadcasted_iota(jnp.int32, (slots, slots), 0)
    chosen = jnp.where(slot == pairs[0:1, :], 1.0, 0.0).astype(BF16)
    rest = terms[...]
    total = jnp.zeros(near.shape, F32)
    for _ in range(3):
        part = rest.astype(BF16)
        rest = rest - part.astype(F32)
        total = total + jnp.dot(chosen, part, preferred_element_type=F32)
    near[...] = total

    row_ends = ((2, 4), (32, 34))
    last = []
    for b, dx in sides:
        last.append((out.at[row_ends[b][0] : row_ends[b][1], :, 8:40, :], last_x_in.at[1 - b], on_pencil(dx)))
        for a, dz in sides:
            rows = (0, 2) if b == 0 else (6, 8)
            last.append(
                (last_z_out.at[3 * b, a, rows[0] : rows[1]], last_corner_in.at[1 - b, 1 - a], at(dz, dx))
            )

    def planes(chunk, a):
        return (last_z_out.at[chunk, a], last_z_in.at[chunk, 1 - a], last_send.at[6 + a], last_recv.at[chunk, 1 - a])

    def take_planes(step, carry):
        chunk = turns(step)
        for a, row in ((0, 6), (1, 40)):
            wait_recv(last_z_in.at[chunk, a], last_recv.at[chunk, a])
            for x in range(8):
                for tile in range(4):
                    out[2 + 8 * chunk + x, tile, row : row + 2, :] = last_z_in[chunk, a, x, 2 * tile : 2 * tile + 2, :]
        return carry

    def inverse_y(step, carry):
        chunk = turns(step)
        wait_recv(took_1.at[chunk, 0 : n_slab - 1], recv_4.at[chunk])
        ends = []
        for parity in range(2):
            columns = took_1[chunk, :, 32 * parity : 32 * parity + 32, :].reshape(256, 256).T
            ends.append(dot_3(halves(columns), (ty[0, parity], ty[1, parity])))
        space = (ends[0] + ends[1], ends[0] - ends[1])
        for tile in range(4):
            lanes = slice(128 * (tile % 2), 128 * (tile % 2) + 128)
            cells = space[tile // 2][:, lanes].reshape(8, 32, 128)
            out[pl.ds(2 + 8 * chunk, 8), tile, 8:40, :] = cells
            last_z_out[chunk, 0, :, 2 * tile : 2 * tile + 2, :] = cells[:, 0:2, :]
            last_z_out[chunk, 1, :, 2 * tile : 2 * tile + 2, :] = cells[:, 30:32, :]
        for a, dz in sides:
            remote(*planes(chunk, a), on_slab(dz)).start()
        for b in range(2):

            @pl.when(chunk == 3 * b)
            def _():
                for i in range(3 * b, 3 * b + 3):
                    source, target, device = last[i]
                    remote(source, target, last_send.at[i], corner_recv.at[i], device).start()

        return carry

    lax.fori_loop(0, CHUNKS, inverse_y, 0)
    lax.fori_loop(0, CHUNKS - 1, take_planes, 0)
    for i, (source, target, device) in enumerate(last):
        wait_recv(target, corner_recv.at[i])
        wait_send(source, last_send.at[i])
    for b, start in ((0, 0), (1, 34)):
        out[start : start + 2, :, 8:40, :] = last_x_in[b]
        for a, row in ((0, 6), (1, 40)):
            for x in range(2):
                for tile in range(4):
                    out[start + x, tile, row : row + 2, :] = last_corner_in[b, a, x, 2 * tile : 2 * tile + 2, :]
    for i, (source, target, device) in enumerate(rims):
        wait_send(source, rim_send.at[i])
    wait_send(sent_1.at[:, 0 : n_slab - 1], send_1)
    wait_send(got_2.at[:, :, 0 : 32 * (n_pencil - 1), :], send_2)
    wait_send(got_2.at[:, :, 0 : 32 * (n_pencil - 1), :], send_3)
    wait_send(back_1.at[:, 0 : n_slab - 1], send_4)

    @pl.when(middle)
    def _():
        wait_send(level_out, level_send)

    take_planes(CHUNKS - 1, 0)
    for a in range(2):
        wait_send(last_z_out.at[:, a], last_send.at[6 + a])

    top = lax.broadcasted_iota(jnp.int32, (8, 128), 0) < 4

    def gather_group(step, carry):
        def pick(turn, carry):
            for u in range(UNROLL):
                b = turn * UNROLL + u
                x_at, z_row, tile_0, tile_1, lane_0 = window(anchors, step * GROUP + b)
                masks_0, masks_1 = window_masks(lane_0)
                for i in range(4):
                    both = []
                    for tile in (tile_0, tile_1):
                        rows = out[x_at + i, tile, pl.ds(z_row, 8), :]
                        both.append(jnp.where(top, rows, pltpu.roll(rows, 4, 0)))
                    for j in range(2):
                        value = jnp.where(masks_0[j], both[0], jnp.where(masks_1[j], both[1], 0.0))
                        values[b, 16 * i + 8 * j : 16 * i + 8 * j + 8] = value
            return carry

        lax.fori_loop(0, GROUP // UNROLL, pick, 0)
        rows = group_wait(step, projection_at, projection, group_load)
        box = lane_sums(values[...].reshape(GROUP * BOX, 128)).reshape(GROUP, BOX, 128)
        far = jnp.sum(projection[rows] * box, axis=1)
        slot = step * GROUP + lax.broadcasted_iota(jnp.int32, (GROUP, 128), 0)
        result[rows, :] = jnp.where(slot < count[...], far + near[rows, :], 0.0)
        return carry

    lax.fori_loop(0, slots // GROUP, gather_group, 0)


def field(anchors, count, pairs, charges, grid, projection, matrices, kernel):
    tables = [jnp.asarray(np.stack(split_table(table))) for table in (y_tables(), z_table(), x_tables())]
    slots, panels = charges.shape
    dma = pltpu.SemaphoreType.DMA
    vmem = pltpu.VMEM
    return pl.pallas_call(
        field_kernel,
        in_specs=[
            pl.BlockSpec(memory_space=pltpu.SMEM),
            *[pl.BlockSpec(memory_space=vmem)] * 3,
            *[pl.BlockSpec(memory_space=pl.ANY)] * 7,
        ],
        out_specs=pl.BlockSpec(memory_space=vmem),
        out_shape=jax.ShapeDtypeStruct((slots, panels), F32),
        scratch_shapes=[
            vmem(projection.shape, F32),
            vmem(matrices.shape, BF16),
            vmem(kernel.shape, F32),
            *(vmem(table.shape, BF16) for table in tables),
            vmem((slots, panels), F32),
            vmem((slots, panels), F32),
            vmem((slots, panels), F32),
            vmem((GROUP, BOX, panels), F32),
            vmem((36, 4, 48, 128), F32),
            vmem((32, 4, 32, 128), F32),
            vmem((2, 36, 4, 8, 128), F32),
            vmem((2, 36, 8, 128), F32),
            vmem((2, 32, 8, 128), F32),
            vmem((2, 2, 4, 32, 128), F32),
            vmem((2, 2, 2, 8, 128), F32),
            vmem((CHUNKS, 8, 64, 256), F32),
            vmem((CHUNKS, 8, 64, 256), F32),
            vmem((CHUNKS, 16, 2, 2, 8, 256), F32),
            vmem((2, 2, 512, 256), F32),
            vmem((2, 256, 256), F32),
            vmem((2, 256, 256), F32),
            vmem((2, 2, 256, 256), F32),
            vmem((2, 2, 512, 256), F32),
            vmem((CHUNKS, 16, 2, 2, 8, 256), F32),
            vmem((CHUNKS, 8, 64, 256), F32),
            vmem((CHUNKS, 8, 64, 256), F32),
            vmem((4, 256, 128), F32),
            vmem((CHUNKS, 2, 8, 8, 128), F32),
            vmem((CHUNKS, 2, 8, 8, 128), F32),
            vmem((2, 2, 4, 32, 128), F32),
            vmem((2, 2, 2, 8, 128), F32),
            dma((8,)),
            dma((slots // GROUP,)),
            dma,
            dma,
            dma((8,)),
            dma((8,)),
            dma((8,)),
            dma((CHUNKS, 2)),
            dma((6,)),
            dma,
            dma((CHUNKS,)),
            dma,
            dma,
            dma,
            dma((CHUNKS,)),
            dma,
            dma((CHUNKS,)),
        ],
        compiler_params=pltpu.CompilerParams(
            collective_id=0, has_side_effects=True, vmem_limit_bytes=62 << 20
        ),
        cost_estimate=pl.CostEstimate(flops=10**10, bytes_accessed=10**7, transcendentals=0),
    )(anchors, count, pairs, charges, grid, projection, matrices, kernel, *tables)


def shards(charges, projection, anchors, block_count, near_pairs, near_matrices, kernel_hat):
    panels = charges.shape[1]
    grid = scatter(anchors.T, block_count, projection, charges)
    levels = jnp.transpose(kernel_hat.reshape(NX, 4, 2, 128), (0, 2, 1, 3)).reshape(NX * 8, 128)
    count = jnp.broadcast_to(block_count[:, None], (1, panels))
    return field(anchors.T, count, near_pairs.T, charges, grid, projection, near_matrices, levels)


def solution(mesh):
    return jax.shard_map(
        shards,
        mesh=mesh,
        in_specs=(
            P(("slab", "pencil"), None),
            P(("slab", "pencil"), None, None),
            P(("slab", "pencil"), None),
            P(("slab", "pencil")),
            P(("slab", "pencil"), None),
            P(("slab", "pencil"), None, None),
            P(None, ("slab", "pencil"), None),
        ),
        out_specs=P(("slab", "pencil"), None),
        check_vma=False,
    )
```

```python
import jax
import jax.numpy as jnp
import ml_dtypes
import numpy as np
from jax import lax
from jax.experimental import pallas as pl
from jax.experimental.pallas import tpu as pltpu
from jax.sharding import PartitionSpec as P

NX, NY, NZ, BOX = 512, 512, 256, 64
GROUP = 32
UNROLL = 4
AHEAD = 2
F32, BF16 = jnp.float32, jnp.bfloat16


def halves(value):
    high = value.astype(BF16)
    return high, (value - high.astype(F32)).astype(BF16)


def lane_sums(value):
    both = jnp.concatenate(halves(value), axis=1)
    return jnp.dot(both, jnp.ones((256, 128), BF16), preferred_element_type=F32)


def row_of(x, tile, z):
    return (x * 4 + tile) * 48 + z


def window(anchors, slot):
    corner = row_of(anchors[0, slot] & 31, 0, (anchors[2, slot] & 31) + 6)
    y_at = (anchors[1, slot] + (NY - 2)) & (NY - 1)
    tile = y_at >> 7
    return corner + 48 * tile, corner + 48 * ((tile + 1) & 3), y_at & 127


def window_masks(lane_0):
    row = lax.broadcasted_iota(jnp.int32, (8, 128), 0)
    lane = lax.broadcasted_iota(jnp.int32, (8, 128), 1)
    shifted = (lane - row // 4 - lane_0) & 127
    return (shifted == 0, shifted == 2), lane >= lane_0, row < 4


def group_rows(step):
    return pl.ds(pl.multiple_of(step * GROUP, GROUP), GROUP)


def group_copy(step, source, target, sems):
    return pltpu.make_async_copy(source.at[group_rows(step)], target.at[group_rows(step)], sems.at[step])


def scatter_kernel(anchors, count, projection_at, charges, grid, projection, values, load):
    for step in range(AHEAD):
        group_copy(step, projection_at, projection, load).start()

    def clear(x, carry):
        grid[pl.ds(pl.multiple_of(x * 192, 8), 192), :] = jnp.zeros((192, 128), F32)
        return carry

    lax.fori_loop(0, 36, clear, 0)

    def group(step, carry):
        @pl.when(step < charges.shape[0] // GROUP - AHEAD)
        def _():
            group_copy(step + AHEAD, projection_at, projection, load).start()

        group_copy(step, projection_at, projection, load).wait()
        rows = group_rows(step)
        slot = step * GROUP + lax.broadcasted_iota(jnp.int32, (GROUP, 128), 0)
        masked = jnp.where(slot < count[0], charges[rows, :], 0.0)
        products = projection[rows] * masked[:, None, :]
        values[...] = lane_sums(products.reshape(GROUP * BOX, 128)).reshape(GROUP, BOX, 128)

        def place(turn, carry):
            firsts, seconds, furthest = [], [], 0
            for u in range(UNROLL):
                b = turn * UNROLL + u
                row_0, row_1, lane_0 = window(anchors, step * GROUP + b)
                masks, beyond, top = window_masks(lane_0)
                here, there = beyond & top, top & ~beyond
                furthest = jnp.maximum(furthest, lane_0)
                for i in range(4):
                    patch = jnp.where(masks[0], values[b, 16 * i : 16 * i + 8], 0.0)
                    patch = jnp.where(masks[1], values[b, 16 * i + 8 : 16 * i + 16], patch)
                    patch = patch + pltpu.roll(patch, 4, 0)
                    firsts.append((row_0 + 192 * i, jnp.where(here, patch, 0.0)))
                    seconds.append((row_1 + 192 * i, there, patch))
            for row, patch in firsts:
                grid[pl.ds(row, 8), :] += patch

            @pl.when(furthest > 124)
            def _():
                for row, there, patch in seconds:
                    grid[pl.ds(row, 8), :] += jnp.where(there, patch, 0.0)

            return carry

        return lax.fori_loop(0, GROUP // UNROLL, place, carry)

    lax.fori_loop(0, charges.shape[0] // GROUP, group, 0)


def scatter(anchors, count, projection, charges):
    slots = charges.shape[0]
    smem, vmem = pl.BlockSpec(memory_space=pltpu.SMEM), pl.BlockSpec(memory_space=pltpu.VMEM)
    return pl.pallas_call(
        scatter_kernel,
        in_specs=[smem, smem, pl.BlockSpec(memory_space=pl.ANY), vmem],
        out_specs=vmem,
        scratch_shapes=[
            pltpu.VMEM(projection.shape, F32),
            pltpu.VMEM((GROUP, BOX, 128), F32),
            pltpu.SemaphoreType.DMA((slots // GROUP,)),
        ],
        out_shape=jax.ShapeDtypeStruct((36 * 4 * 48, 128), F32),
        compiler_params=pltpu.CompilerParams(vmem_limit_bytes=60 << 20),
    )(anchors, count, projection, charges)


CHUNKS = 4
MESH = pl.DeviceIdType.MESH


def phases(product, length):
    angle = 2.0 * np.pi * (product % length) / length
    return np.cos(angle), np.sin(angle)


def split_table(table):
    table = table.astype(np.float32)
    high = table.astype(ml_dtypes.bfloat16)
    return high, (table - high.astype(np.float32)).astype(ml_dtypes.bfloat16)


def y_tables():
    slab, part, pencil = np.meshgrid(np.arange(8), np.arange(2), np.arange(16), indexing="ij")
    device = (slab * 16 + pencil).reshape(-1, 1)
    part = part.reshape(-1, 1)
    even = np.where(device < 64, 4 * device, 4 * device + 2)
    odd = 4 * device + 1
    position = np.arange(256)[None, :]
    result = []
    for freq in (even, odd):
        cos, sin = phases(freq * position, NY)
        table = np.where(part == 0, cos, -sin)
        if freq is even:
            table[(device[:, 0] == 0) & (part[:, 0] == 1)] = 1.0 - 2.0 * (position[0] % 2)
        result.append(table)
    return np.stack(result)


def z_table():
    position = np.arange(NZ)
    cos, sin = phases(position[:, None] * position[None, :], NZ)
    return np.block([[cos, -sin], [sin, cos]])


def x_tables():
    position = np.arange(256)
    result = []
    for parity in range(2):
        cos, sin = phases((2 * position[:, None] + parity) * position[None, :], NX)
        result.append(np.concatenate([cos, sin], axis=1))
        if parity:
            result.append(np.concatenate([cos.T, sin.T], axis=1))
    return np.stack(result)


def dot_3(left, right, dims=((1,), (0,))):
    def one(a, b):
        return lax.dot_general(a, b, (dims, ((), ())), preferred_element_type=F32)

    return one(left[0], right[0]) + (one(left[0], right[1]) + one(left[1], right[0]))


def swap_groups(tiles):
    lane = lax.broadcasted_iota(jnp.int32, tiles[0].shape, 1)
    low, even = lane < 64, lane % 64 < 32
    firsts, lasts = [], []
    for a, b in ((tiles[0], tiles[2]), (tiles[1], tiles[3])):
        firsts.append(jnp.where(low, a, pltpu.roll(b, 64, 1)))
        lasts.append(jnp.where(low, pltpu.roll(a, 64, 1), b))
    result = []
    for a, b in (firsts, lasts):
        result.append(jnp.where(even, a, pltpu.roll(b, 32, 1)))
        result.append(jnp.where(even, pltpu.roll(a, 96, 1), b))
    return result


def field_kernel(
    anchors, count, pairs, charges, grid_at, projection_at, matrices_at, kernel_at, ty_at, tz_at, tx_at,
    result,
    projection, matrices, kernel, ty, tz, tx, sources, terms, near, values, out,
    charge, z_rows, z_out, z_in, x_in, corner_in, sent_1, got_1, sent_2, got_2, level_out, level_in, spectra, back_2, took_2,
    back_1, took_1, lines, last_z_out, last_z_in, last_x_out, last_x_in, last_corner_in,
    load, group_load, level_send, level_recv, rim_send, rim_recv, last_send, last_recv, corner_recv,
    send_1, recv_1, send_2, recv_2, send_3, recv_3, send_4, recv_4,
):
    slab, pencil = lax.axis_index("slab"), lax.axis_index("pencil")
    n_slab, n_pencil = 8, 16

    def at(slab_step, pencil_step):
        return (lax.rem(slab + n_slab + slab_step, n_slab), lax.rem(pencil + n_pencil + pencil_step, n_pencil))

    def on_slab(step):
        return at(step, 0)

    def on_pencil(step):
        return at(0, step)

    def remote(source, target, send_sem, recv_sem, device):
        return pltpu.make_async_remote_copy(
            src_ref=source, dst_ref=target, send_sem=send_sem, recv_sem=recv_sem, device_id=device, device_id_type=MESH
        )

    def wait_recv(ref, sem):
        remote(ref, ref, sem, sem, on_slab(1)).wait_recv()

    def wait_send(ref, sem):
        remote(ref, ref, sem, sem, on_slab(1)).wait_send()

    barrier = pltpu.get_barrier_semaphore()

    def greet(device):
        pl.semaphore_signal(barrier, inc=1, device_id=device, device_id_type=MESH)

    def greet_slab(step, carry):
        greet(on_slab(step))
        return carry

    def greet_pencil(step, carry):
        greet(on_pencil(step))
        return carry

    sides = ((0, -1), (1, 1))
    lax.fori_loop(1, n_slab, greet_slab, 0)
    lax.fori_loop(1, n_pencil, greet_pencil, 0)
    for _, dz in sides:
        for _, dx in sides:
            greet(at(dz, dx))

    loads = [
        pltpu.make_async_copy(source, target, load.at[i])
        for i, (source, target) in enumerate(
            (
                (grid_at.at[:, :, 0:8, :], z_rows.at[0]),
                (grid_at.at[:, :, 40:48, :], z_rows.at[1]),
                (grid_at.at[2:34, :, 8:40, :], charge),
                (ty_at, ty),
                (tz_at, tz),
                (kernel_at, kernel),
                (tx_at, tx),
                (matrices_at, matrices),
            )
        )
    ]
    for copy in loads:
        copy.start()
    for step in range(charges.shape[0] // GROUP):
        group_copy(step, projection_at, projection, group_load).start()

    def pack_rims(x, carry):
        for tile in range(4):
            z_out[0, x, 2 * tile : 2 * tile + 2, :] = z_rows[0, x, tile, 6:8, :]
            z_out[1, x, 2 * tile : 2 * tile + 2, :] = z_rows[1, x, tile, 0:2, :]
        return carry

    loads[0].wait()
    loads[1].wait()
    lax.fori_loop(0, 36, pack_rims, 0, unroll=4)
    pl.semaphore_wait(barrier, n_slab + n_pencil + 2)
    ends = ((0, 2), (34, 36))
    rims = []
    for a, dz in sides:
        rims.append((z_out.at[a, 2:34], z_in.at[1 - a], on_slab(dz)))
    for b, dx in sides:
        rims.append((grid_at.at[ends[b][0] : ends[b][1], :, 8:40, :], x_in.at[1 - b], on_pencil(dx)))
    for a, dz in sides:
        for b, dx in sides:
            rims.append((z_out.at[a, ends[b][0] : ends[b][1]], corner_in.at[1 - a, 1 - b], at(dz, dx)))
    for i, (source, target, device) in enumerate(rims):
        remote(source, target, rim_send.at[i], rim_recv.at[i], device).start()

    loads[2].wait()
    wait_recv(z_in.at[1], rim_recv.at[0])
    wait_recv(z_in.at[0], rim_recv.at[1])

    def add_rims(x, carry):
        for tile in range(4):
            charge[x, tile, 0:2, :] += z_in[0, x, 2 * tile : 2 * tile + 2, :]
            charge[x, tile, 30:32, :] += z_in[1, x, 2 * tile : 2 * tile + 2, :]
        return carry

    lax.fori_loop(0, 32, add_rims, 0, unroll=4)
    loads[3].wait()

    def forward_y(step, carry):
        chunk = lax.rem(step + 1, CHUNKS)

        @pl.when(step == 2)
        def _():
            for i in range(2, 8):
                wait_recv(rims[i][1], rim_recv.at[i])
            for b, start in ((0, 0), (1, 30)):
                charge[start : start + 2] += x_in[b]
                for a, row in ((0, 0), (1, 30)):
                    for x in range(2):
                        for tile in range(4):
                            charge[start + x, tile, row : row + 2, :] += corner_in[a, b, x, 2 * tile : 2 * tile + 2, :]

        tiles = [charge[pl.ds(8 * chunk, 8), tile].reshape(256, 128) for tile in range(4)]
        for parity in range(2):
            if parity:
                halved = [tiles[0] - tiles[2], tiles[1] - tiles[3]]
            else:
                halved = [tiles[0] + tiles[2], tiles[1] + tiles[3]]
            columns = halves(jnp.concatenate(halved, axis=1))
            freqs = dot_3((ty[0, parity], ty[1, parity]), columns, ((1,), (1,)))
            sent_1[chunk, :, 32 * parity : 32 * parity + 32, :] = freqs.reshape(n_slab, 32, 256)
        got_1[chunk, slab] = sent_1[chunk, slab]

        def send(k, carry):
            device = on_slab(k)
            remote(sent_1.at[chunk, device[0]], got_1.at[chunk, slab], send_1, recv_1.at[chunk], device).start()
            return carry

        return lax.fori_loop(1, n_slab, send, carry)

    lax.fori_loop(0, CHUNKS, forward_y, 0)

    slots, panels = charges.shape
    loads[5].wait()
    first = jnp.logical_and(slab == 0, pencil == 0)
    middle = jnp.logical_and(slab == 4, pencil == 0)

    @pl.when(middle)
    def _():
        for kx in range(2):
            for i in range(2):
                level_out[kx, :, 128 * i : 128 * i + 128] = kernel[pl.ds(8 * kx + 4 * i, 256, stride=16), :]
        remote(level_out, level_in, level_send, level_recv, (0, pencil)).start()

    slot = lax.broadcasted_iota(jnp.int32, (slots, panels), 0)
    coarse = jnp.where(slot < count[...], charges[...], 0.0).astype(BF16)
    slot = lax.broadcasted_iota(jnp.int32, (slots, slots), 0)
    chosen = jnp.where(slot == pairs[1:2, :], 1.0, 0.0)
    sources[...] = jnp.dot(chosen.T.astype(BF16), coarse, preferred_element_type=F32)
    loads[4].wait()
    loads[7].wait()

    def near_group(group, carry):
        rows = pl.ds(pl.multiple_of(8 * group, 8), 8)
        taken = sources[rows, :].astype(BF16)
        row = lax.broadcasted_iota(jnp.int32, (8, panels), 0)
        total = jnp.zeros((8, panels), F32)
        for i in range(8):
            found = lax.dot_general(
                taken, matrices[8 * group + i], (((1,), (1,)), ((), ())), preferred_element_type=F32
            )
            total = jnp.where(row == i, found, total)
        terms[rows, :] = total
        return carry

    near_groups = slots // 8 // (2 * CHUNKS)

    def near_share(turn):
        lax.fori_loop(turn * near_groups, (turn + 1) * near_groups, near_group, 0)

    def forward_z(step, carry):
        chunk = lax.rem(step + 1, CHUNKS)
        near_share(step)
        wait_recv(got_1.at[chunk, 0 : n_slab - 1], recv_1.at[chunk])
        for h in range(2):
            for q in range(2):
                tiles = swap_groups([got_1[chunk, 4 * q + s, :, 128 * h : 128 * h + 128] for s in range(4)])
                for a in range(4):
                    for parity in range(2):
                        for part in range(2):
                            row = 32 * parity + 16 * part
                            lines[2 * part + q, pl.ds(128 * parity + 4 * h + a, 16, stride=8), :] = tiles[a][row : row + 16]
        rows = halves(jnp.concatenate([lines[i] for i in range(4)], axis=1))
        freqs = dot_3(rows, (tz[0], tz[1]))
        for parity in range(2):
            for part in range(2):
                block = freqs[128 * parity : 128 * parity + 128, 256 * part : 256 * part + 256]
                sent_2[chunk, :, parity, part] = block.reshape(n_pencil, 8, 256)
        mine = pl.ds(pl.multiple_of(pencil * 32 + chunk * 8, 8), 8)
        got_2[:, :, mine, :] = sent_2[chunk, pencil]

        def send(k, carry):
            device = on_pencil(k)
            remote(sent_2.at[chunk, device[1]], got_2.at[:, :, mine, :], send_2, recv_2, device).start()
            return carry

        return lax.fori_loop(1, n_pencil, send, carry)

    lax.fori_loop(0, CHUNKS, forward_z, 0)
    wait_recv(got_2.at[:, :, 0 : 32 * (n_pencil - 1), :], recv_2)

    loads[6].wait()
    unit = 1.0 / (NX * NY * NZ)

    def stacked(real, imag):
        real, imag = halves(real), halves(imag)
        return tuple(
            jnp.concatenate([jnp.concatenate([r, i], axis=1), jnp.concatenate([i, -r], axis=1)], axis=0)
            for r, i in zip(real, imag)
        )

    for parity in range(2):
        for kx in range(2):
            parts = []
            for part in range(2):
                low, high = got_2[parity, part, 0:256, :], got_2[parity, part, 256:512, :]
                parts.append(low - high if kx else low + high)
            table = (tx[0, kx], tx[1, kx])
            found = dot_3(table, stacked(*parts))
            if parity:
                green = jnp.concatenate(
                    [kernel[pl.ds(8 * kx + 4 * i + 1, 256, stride=16), :] for i in range(2)], axis=1
                ) * (2.0 * unit)
            else:
                own = jnp.where(slab < 4, 0, 2)
                green = jnp.concatenate(
                    [kernel[pl.ds(own + 8 * kx + 4 * i, 256, stride=16), :] for i in range(2)], axis=1
                ) * jnp.where(first, unit, 2.0 * unit)
            spectra[kx, 0] = found[:, 0:256] * green
            spectra[kx, 1] = found[:, 256:512] * green
            if not parity:

                @pl.when(first)
                def _():
                    if not kx:
                        wait_recv(level_in, level_recv)
                    other = level_in[kx] * unit
                    row = lax.broadcasted_iota(jnp.int32, (256, 256), 0)
                    lane = lax.broadcasted_iota(jnp.int32, (256, 256), 1)
                    mirror = jnp.where((row + lane) % 256 == 0, 1.0, 0.0).astype(BF16)
                    flipped = [
                        sum(jnp.dot(piece, mirror, preferred_element_type=F32) for piece in halves(value)) for value in parts
                    ]
                    twin = dot_3(table, stacked(flipped[0], -flipped[1]))
                    mean, rest = 0.5 * (green + other), 0.5 * (green - other)
                    for part in range(2):
                        lanes = slice(256 * part, 256 * part + 256)
                        spectra[kx, part] = mean * found[:, lanes] + rest * twin[:, lanes]

        ends = []
        for kx in range(2):
            table = (tx[0, 2 * kx], tx[1, 2 * kx])
            real, imag = halves(spectra[kx, 0]), halves(spectra[kx, 1])
            right = tuple(
                jnp.concatenate([jnp.concatenate([r, i], axis=1), jnp.concatenate([-i, r], axis=1)], axis=0)
                for r, i in zip(real, imag)
            )
            ends.append(dot_3(table, right))
        for part in range(2):
            lanes = slice(256 * part, 256 * part + 256)
            back_2[parity, part, 0:256, :] = ends[0][:, lanes] + ends[1][:, lanes]
            back_2[parity, part, 256:512, :] = ends[0][:, lanes] - ends[1][:, lanes]

    def turns(step):
        return jnp.where(step < 2, 3 * step, step - 1)

    def return_x(step, carry):
        chunk = turns(step)
        own = pl.ds(pl.multiple_of(pencil * 32 + chunk * 8, 8), 8)
        took_2[chunk, pencil] = back_2[:, :, own, :]

        def send(k, carry):
            device = on_pencil(k)
            rows = pl.ds(pl.multiple_of(device[1] * 32 + chunk * 8, 8), 8)
            remote(back_2.at[:, :, rows, :], took_2.at[chunk, pencil], send_3, recv_3.at[chunk], device).start()
            return carry

        return lax.fori_loop(1, n_pencil, send, carry)

    lax.fori_loop(0, CHUNKS, return_x, 0)

    def inverse_z(step, carry):
        chunk = turns(step)
        near_share(CHUNKS + step)
        wait_recv(took_2.at[chunk, 0 : n_pencil - 1], recv_3.at[chunk])
        blocks = []
        for parity in range(2):
            blocks.append(jnp.concatenate([took_2[chunk, :, parity, part].reshape(128, 256) for part in range(2)], axis=1))
        rows = halves(jnp.concatenate(blocks, axis=0))
        space = dot_3(rows, (tz[0], tz[1]), ((1,), (1,)))
        for i in range(4):
            lines[i] = space[:, 128 * i : 128 * i + 128]
        for h in range(2):
            for q in range(2):
                tiles = []
                for a in range(4):
                    tiles.append(
                        jnp.concatenate(
                            [
                                lines[2 * part + q, pl.ds(128 * parity + 4 * h + a, 16, stride=8), :]
                                for parity in range(2)
                                for part in range(2)
                            ],
                            axis=0,
                        )
                    )
                for s, tile in enumerate(swap_groups(tiles)):
                    back_1[chunk, 4 * q + s, :, 128 * h : 128 * h + 128] = tile
        took_1[chunk, slab] = back_1[chunk, slab]

        def send(k, carry):
            device = on_slab(k)
            remote(back_1.at[chunk, device[0]], took_1.at[chunk, slab], send_4, recv_4.at[chunk], device).start()
            return carry

        return lax.fori_loop(1, n_slab, send, carry)

    lax.fori_loop(0, CHUNKS, inverse_z, 0)

    slot = lax.broadcasted_iota(jnp.int32, (slots, slots), 0)
    chosen = jnp.where(slot == pairs[0:1, :], 1.0, 0.0).astype(BF16)
    rest = terms[...]
    total = jnp.zeros(near.shape, F32)
    for _ in range(3):
        part = rest.astype(BF16)
        rest = rest - part.astype(F32)
        total = total + jnp.dot(chosen, part, preferred_element_type=F32)
    near[...] = total

    row_starts = (2, 32)
    last = []
    for b, dx in sides:
        last.append((last_x_out.at[b], last_x_in.at[1 - b], on_pencil(dx)))
        for a, dz in sides:
            rows = (0, 2) if b == 0 else (6, 8)
            last.append(
                (last_z_out.at[3 * b, a, rows[0] : rows[1]], last_corner_in.at[1 - b, 1 - a], at(dz, dx))
            )

    def planes(chunk, a):
        return (last_z_out.at[chunk, a], last_z_in.at[chunk, 1 - a], last_send.at[6 + a], last_recv.at[chunk, 1 - a])

    def take_planes(step, carry):
        chunk = turns(step)
        for a, row in ((0, 6), (1, 40)):
            wait_recv(last_z_in.at[chunk, a], last_recv.at[chunk, a])
            for x in range(8):
                for tile in range(4):
                    out[pl.ds(row_of(2 + 8 * chunk + x, tile, row), 2), :] = last_z_in[chunk, a, x, 2 * tile : 2 * tile + 2, :]
        return carry

    def inverse_y(step, carry):
        chunk = turns(step)
        wait_recv(took_1.at[chunk, 0 : n_slab - 1], recv_4.at[chunk])
        ends = []
        for parity in range(2):
            columns = took_1[chunk, :, 32 * parity : 32 * parity + 32, :].reshape(256, 256).T
            ends.append(dot_3(halves(columns), (ty[0, parity], ty[1, parity])))
        space = (ends[0] + ends[1], ends[0] - ends[1])
        for tile in range(4):
            lanes = slice(128 * (tile % 2), 128 * (tile % 2) + 128)
            cells = space[tile // 2][:, lanes].reshape(8, 32, 128)
            for x in range(8):
                out[pl.ds(pl.multiple_of(row_of(2 + 8 * chunk + x, tile, 8), 8), 32), :] = cells[x]
            last_z_out[chunk, 0, :, 2 * tile : 2 * tile + 2, :] = cells[:, 0:2, :]
            last_z_out[chunk, 1, :, 2 * tile : 2 * tile + 2, :] = cells[:, 30:32, :]
        for a, dz in sides:
            remote(*planes(chunk, a), on_slab(dz)).start()
        for b in range(2):

            @pl.when(chunk == 3 * b)
            def _():
                for x in range(2):
                    for tile in range(4):
                        last_x_out[b, x, tile] = out[pl.ds(row_of(row_starts[b] + x, tile, 8), 32), :]
                for i in range(3 * b, 3 * b + 3):
                    source, target, device = last[i]
                    remote(source, target, last_send.at[i], corner_recv.at[i], device).start()

        return carry

    lax.fori_loop(0, CHUNKS, inverse_y, 0)
    lax.fori_loop(0, CHUNKS - 1, take_planes, 0)
    for i, (source, target, device) in enumerate(last):
        wait_recv(target, corner_recv.at[i])
        wait_send(source, last_send.at[i])
    for b, start in ((0, 0), (1, 34)):
        for x in range(2):
            for tile in range(4):
                out[pl.ds(row_of(start + x, tile, 8), 32), :] = last_x_in[b, x, tile]
                for a, row in ((0, 6), (1, 40)):
                    out[pl.ds(row_of(start + x, tile, row), 2), :] = last_corner_in[b, a, x, 2 * tile : 2 * tile + 2, :]
    for i, (source, target, device) in enumerate(rims):
        wait_send(source, rim_send.at[i])
    wait_send(sent_1.at[:, 0 : n_slab - 1], send_1)
    wait_send(got_2.at[:, :, 0 : 32 * (n_pencil - 1), :], send_2)
    wait_send(got_2.at[:, :, 0 : 32 * (n_pencil - 1), :], send_3)
    wait_send(back_1.at[:, 0 : n_slab - 1], send_4)

    @pl.when(middle)
    def _():
        wait_send(level_out, level_send)

    take_planes(CHUNKS - 1, 0)
    for a in range(2):
        wait_send(last_z_out.at[:, a], last_send.at[6 + a])

    def gather_group(step, carry):
        def pick(turn, carry):
            for u in range(UNROLL):
                b = turn * UNROLL + u
                row_0, row_1, lane_0 = window(anchors, step * GROUP + b)
                masks, beyond, top = window_masks(lane_0)
                for i in range(4):
                    cells = jnp.where(beyond, out[pl.ds(row_0 + 192 * i, 8), :], out[pl.ds(row_1 + 192 * i, 8), :])
                    cells = jnp.where(top, cells, pltpu.roll(cells, 4, 0))
                    for j in range(2):
                        values[b, 16 * i + 8 * j : 16 * i + 8 * j + 8] = jnp.where(masks[j], cells, 0.0)
            return carry

        lax.fori_loop(0, GROUP // UNROLL, pick, 0)
        group_copy(step, projection_at, projection, group_load).wait()
        rows = group_rows(step)
        box = lane_sums(values[...].reshape(GROUP * BOX, 128)).reshape(GROUP, BOX, 128)
        far = jnp.sum(projection[rows] * box, axis=1)
        slot = step * GROUP + lax.broadcasted_iota(jnp.int32, (GROUP, 128), 0)
        result[rows, :] = jnp.where(slot < count[...], far + near[rows, :], 0.0)
        return carry

    lax.fori_loop(0, slots // GROUP, gather_group, 0)


def field(anchors, count, pairs, charges, grid, projection, matrices, kernel):
    tables = [jnp.asarray(np.stack(split_table(table))) for table in (y_tables(), z_table(), x_tables())]
    slots, panels = charges.shape
    dma = pltpu.SemaphoreType.DMA
    vmem = pltpu.VMEM
    return pl.pallas_call(
        field_kernel,
        in_specs=[
            pl.BlockSpec(memory_space=pltpu.SMEM),
            *[pl.BlockSpec(memory_space=vmem)] * 3,
            *[pl.BlockSpec(memory_space=pl.ANY)] * 7,
        ],
        out_specs=pl.BlockSpec(memory_space=vmem),
        out_shape=jax.ShapeDtypeStruct((slots, panels), F32),
        scratch_shapes=[
            vmem(projection.shape, F32),
            vmem(matrices.shape, BF16),
            vmem(kernel.shape, F32),
            *(vmem(table.shape, BF16) for table in tables),
            vmem((slots, panels), F32),
            vmem((slots, panels), F32),
            vmem((slots, panels), F32),
            vmem((GROUP, BOX, panels), F32),
            vmem((36 * 4 * 48, 128), F32),
            vmem((32, 4, 32, 128), F32),
            vmem((2, 36, 4, 8, 128), F32),
            vmem((2, 36, 8, 128), F32),
            vmem((2, 32, 8, 128), F32),
            vmem((2, 2, 4, 32, 128), F32),
            vmem((2, 2, 2, 8, 128), F32),
            vmem((CHUNKS, 8, 64, 256), F32),
            vmem((CHUNKS, 8, 64, 256), F32),
            vmem((CHUNKS, 16, 2, 2, 8, 256), F32),
            vmem((2, 2, 512, 256), F32),
            vmem((2, 256, 256), F32),
            vmem((2, 256, 256), F32),
            vmem((2, 2, 256, 256), F32),
            vmem((2, 2, 512, 256), F32),
            vmem((CHUNKS, 16, 2, 2, 8, 256), F32),
            vmem((CHUNKS, 8, 64, 256), F32),
            vmem((CHUNKS, 8, 64, 256), F32),
            vmem((4, 256, 128), F32),
            vmem((CHUNKS, 2, 8, 8, 128), F32),
            vmem((CHUNKS, 2, 8, 8, 128), F32),
            vmem((2, 2, 4, 32, 128), F32),
            vmem((2, 2, 4, 32, 128), F32),
            vmem((2, 2, 2, 8, 128), F32),
            dma((8,)),
            dma((slots // GROUP,)),
            dma,
            dma,
            dma((8,)),
            dma((8,)),
            dma((8,)),
            dma((CHUNKS, 2)),
            dma((6,)),
            dma,
            dma((CHUNKS,)),
            dma,
            dma,
            dma,
            dma((CHUNKS,)),
            dma,
            dma((CHUNKS,)),
        ],
        compiler_params=pltpu.CompilerParams(
            collective_id=0, has_side_effects=True, vmem_limit_bytes=62 << 20
        ),
        cost_estimate=pl.CostEstimate(flops=10**10, bytes_accessed=10**7, transcendentals=0),
    )(anchors, count, pairs, charges, grid, projection, matrices, kernel, *tables)


def shards(charges, projection, anchors, block_count, near_pairs, near_matrices, kernel_hat):
    panels = charges.shape[1]
    grid = scatter(anchors.T, block_count, projection, charges).reshape(36, 4, 48, 128)
    levels = jnp.transpose(kernel_hat.reshape(NX, 4, 2, 128), (0, 2, 1, 3)).reshape(NX * 8, 128)
    count = jnp.broadcast_to(block_count[:, None], (1, panels))
    return field(anchors.T, count, near_pairs.T, charges, grid, projection, near_matrices, levels)


def solution(mesh):
    return jax.shard_map(
        shards,
        mesh=mesh,
        in_specs=(
            P(("slab", "pencil"), None),
            P(("slab", "pencil"), None, None),
            P(("slab", "pencil"), None),
            P(("slab", "pencil")),
            P(("slab", "pencil"), None),
            P(("slab", "pencil"), None, None),
            P(None, ("slab", "pencil"), None),
        ),
        out_specs=P(("slab", "pencil"), None),
        check_vma=False,
    )
```

```python
import jax
import jax.numpy as jnp
import ml_dtypes
import numpy as np
from jax import lax
from jax.experimental import pallas as pl
from jax.experimental.pallas import tpu as pltpu
from jax.sharding import PartitionSpec as P

NX, NY, NZ, BOX = 512, 512, 256, 64
GROUP = 32
UNROLL = 4
AHEAD = 2
F32, BF16 = jnp.float32, jnp.bfloat16


def halves(value):
    high = value.astype(BF16)
    return high, (value - high.astype(F32)).astype(BF16)


def lane_sums(value):
    both = jnp.concatenate(halves(value), axis=1)
    return jnp.dot(both, jnp.ones((256, 128), BF16), preferred_element_type=F32)


def row_of(x, tile, z):
    return (x * 4 + tile) * 48 + z


def window(anchors, slot):
    corner = row_of(anchors[0, slot] & 31, 0, (anchors[2, slot] & 31) + 6)
    y_at = (anchors[1, slot] + (NY - 2)) & (NY - 1)
    tile = y_at >> 7
    return corner + 48 * tile, corner + 48 * ((tile + 1) & 3), y_at & 127


def window_masks(lane_0):
    row = lax.broadcasted_iota(jnp.int32, (8, 128), 0)
    lane = lax.broadcasted_iota(jnp.int32, (8, 128), 1)
    shifted = (lane - row // 4 - lane_0) & 127
    return (shifted == 0, shifted == 2), lane >= lane_0, row < 4


def group_rows(step):
    return pl.ds(pl.multiple_of(step * GROUP, GROUP), GROUP)


def group_copy(step, source, target, sems):
    return pltpu.make_async_copy(source.at[group_rows(step)], target.at[group_rows(step)], sems.at[step])


def scatter_kernel(anchors, count, projection_at, charges, grid, projection, values, load):
    for step in range(AHEAD):
        group_copy(step, projection_at, projection, load).start()

    def clear(x, carry):
        grid[pl.ds(pl.multiple_of(x * 192, 8), 192), :] = jnp.zeros((192, 128), F32)
        return carry

    lax.fori_loop(0, 36, clear, 0)

    def group(step, carry):
        @pl.when(step < charges.shape[0] // GROUP - AHEAD)
        def _():
            group_copy(step + AHEAD, projection_at, projection, load).start()

        group_copy(step, projection_at, projection, load).wait()
        rows = group_rows(step)
        slot = step * GROUP + lax.broadcasted_iota(jnp.int32, (GROUP, 128), 0)
        masked = jnp.where(slot < count[0], charges[rows, :], 0.0)
        products = projection[rows] * masked[:, None, :]
        values[...] = lane_sums(products.reshape(GROUP * BOX, 128)).reshape(GROUP, BOX, 128)

        def place(turn, carry):
            firsts, seconds, furthest = [], [], 0
            for u in range(UNROLL):
                b = turn * UNROLL + u
                row_0, row_1, lane_0 = window(anchors, step * GROUP + b)
                masks, beyond, top = window_masks(lane_0)
                here, there = beyond & top, top & ~beyond
                furthest = jnp.maximum(furthest, lane_0)
                for i in range(4):
                    patch = jnp.where(masks[0], values[b, 16 * i : 16 * i + 8], 0.0)
                    patch = jnp.where(masks[1], values[b, 16 * i + 8 : 16 * i + 16], patch)
                    patch = patch + pltpu.roll(patch, 4, 0)
                    firsts.append((row_0 + 192 * i, jnp.where(here, patch, 0.0)))
                    seconds.append((row_1 + 192 * i, there, patch))
            for row, patch in firsts:
                grid[pl.ds(row, 8), :] += patch

            @pl.when(furthest > 124)
            def _():
                for row, there, patch in seconds:
                    grid[pl.ds(row, 8), :] += jnp.where(there, patch, 0.0)

            return carry

        return lax.fori_loop(0, GROUP // UNROLL, place, carry)

    lax.fori_loop(0, charges.shape[0] // GROUP, group, 0)


def scatter(anchors, count, projection, charges):
    slots = charges.shape[0]
    smem, vmem = pl.BlockSpec(memory_space=pltpu.SMEM), pl.BlockSpec(memory_space=pltpu.VMEM)
    return pl.pallas_call(
        scatter_kernel,
        in_specs=[smem, smem, pl.BlockSpec(memory_space=pl.ANY), vmem],
        out_specs=vmem,
        scratch_shapes=[
            pltpu.VMEM(projection.shape, F32),
            pltpu.VMEM((GROUP, BOX, 128), F32),
            pltpu.SemaphoreType.DMA((slots // GROUP,)),
        ],
        out_shape=jax.ShapeDtypeStruct((36 * 4 * 48, 128), F32),
        compiler_params=pltpu.CompilerParams(vmem_limit_bytes=60 << 20),
    )(anchors, count, projection, charges)


CHUNKS = 4
MESH = pl.DeviceIdType.MESH


def phases(product, length):
    angle = 2.0 * np.pi * (product % length) / length
    return np.cos(angle), np.sin(angle)


def split_table(table):
    table = table.astype(np.float32)
    high = table.astype(ml_dtypes.bfloat16)
    return high, (table - high.astype(np.float32)).astype(ml_dtypes.bfloat16)


def y_tables():
    slab, part, pencil = np.meshgrid(np.arange(8), np.arange(2), np.arange(16), indexing="ij")
    device = (slab * 16 + pencil).reshape(-1, 1)
    part = part.reshape(-1, 1)
    even = np.where(device < 64, 4 * device, 4 * device + 2)
    odd = 4 * device + 1
    position = np.arange(256)[None, :]
    result = []
    for freq in (even, odd):
        cos, sin = phases(freq * position, NY)
        table = np.where(part == 0, cos, -sin)
        if freq is even:
            table[(device[:, 0] == 0) & (part[:, 0] == 1)] = 1.0 - 2.0 * (position[0] % 2)
        result.append(table)
    return np.stack(result)


def z_table():
    position = np.arange(NZ)
    cos, sin = phases(position[:, None] * position[None, :], NZ)
    return np.block([[cos, -sin], [sin, cos]])


def x_tables():
    position = np.arange(256)
    result = []
    for parity in range(2):
        cos, sin = phases((2 * position[:, None] + parity) * position[None, :], NX)
        result.append(np.concatenate([cos, sin], axis=1))
        if parity:
            result.append(np.concatenate([cos.T, sin.T], axis=1))
    return np.stack(result)


def dot_3(left, right, dims=((1,), (0,))):
    def one(a, b):
        return lax.dot_general(a, b, (dims, ((), ())), preferred_element_type=F32)

    return one(left[0], right[0]) + (one(left[0], right[1]) + one(left[1], right[0]))


def swap_groups(tiles):
    lane = lax.broadcasted_iota(jnp.int32, tiles[0].shape, 1)
    low, even = lane < 64, lane % 64 < 32
    firsts, lasts = [], []
    for a, b in ((tiles[0], tiles[2]), (tiles[1], tiles[3])):
        firsts.append(jnp.where(low, a, pltpu.roll(b, 64, 1)))
        lasts.append(jnp.where(low, pltpu.roll(a, 64, 1), b))
    result = []
    for a, b in (firsts, lasts):
        result.append(jnp.where(even, a, pltpu.roll(b, 32, 1)))
        result.append(jnp.where(even, pltpu.roll(a, 96, 1), b))
    return result


def field_kernel(
    anchors, count, pairs, charges, grid_at, projection_at, matrices_at, kernel_at, ty_at, tz_at, tx_at,
    result,
    projection, matrices, kernel, ty, tz, tx, sources, terms, near, values, out,
    charge, z_rows, z_out, z_in, x_in, corner_in, sent_1, got_1, sent_2, got_2, level_out, level_in, spectra, back_2, took_2,
    back_1, took_1, lines, last_z_out, last_z_in, last_x_out, last_x_in, last_corner_in,
    load, group_load, level_send, level_recv, rim_send, rim_recv, last_send, last_recv, corner_recv,
    send_1, recv_1, send_2, recv_2, send_3, recv_3, send_4, recv_4,
):
    slab, pencil = lax.axis_index("slab"), lax.axis_index("pencil")
    n_slab, n_pencil = 8, 16

    def at(slab_step, pencil_step):
        return (lax.rem(slab + n_slab + slab_step, n_slab), lax.rem(pencil + n_pencil + pencil_step, n_pencil))

    def on_slab(step):
        return at(step, 0)

    def on_pencil(step):
        return at(0, step)

    def remote(source, target, send_sem, recv_sem, device):
        return pltpu.make_async_remote_copy(
            src_ref=source, dst_ref=target, send_sem=send_sem, recv_sem=recv_sem, device_id=device, device_id_type=MESH
        )

    def wait_recv(ref, sem):
        remote(ref, ref, sem, sem, on_slab(1)).wait_recv()

    def wait_send(ref, sem):
        remote(ref, ref, sem, sem, on_slab(1)).wait_send()

    barrier = pltpu.get_barrier_semaphore()

    def greet(device):
        pl.semaphore_signal(barrier, inc=1, device_id=device, device_id_type=MESH)

    def greet_slab(step, carry):
        greet(on_slab(step))
        return carry

    def greet_pencil(step, carry):
        greet(on_pencil(step))
        return carry

    sides = ((0, -1), (1, 1))
    lax.fori_loop(1, n_slab, greet_slab, 0)
    lax.fori_loop(1, n_pencil, greet_pencil, 0)
    for _, dz in sides:
        for _, dx in sides:
            greet(at(dz, dx))

    loads = [
        pltpu.make_async_copy(source, target, load.at[i])
        for i, (source, target) in enumerate(
            (
                (grid_at.at[:, :, 0:8, :], z_rows.at[0]),
                (grid_at.at[:, :, 40:48, :], z_rows.at[1]),
                (grid_at.at[2:34, :, 8:40, :], charge),
                (ty_at, ty),
                (tz_at, tz),
                (kernel_at, kernel),
                (tx_at, tx),
                (matrices_at, matrices),
            )
        )
    ]
    for copy in loads:
        copy.start()
    for step in range(charges.shape[0] // GROUP):
        group_copy(step, projection_at, projection, group_load).start()

    def pack_rims(x, carry):
        for tile in range(4):
            z_out[0, x, 2 * tile : 2 * tile + 2, :] = z_rows[0, x, tile, 6:8, :]
            z_out[1, x, 2 * tile : 2 * tile + 2, :] = z_rows[1, x, tile, 0:2, :]
        return carry

    loads[0].wait()
    loads[1].wait()
    lax.fori_loop(0, 36, pack_rims, 0, unroll=4)
    pl.semaphore_wait(barrier, n_slab + n_pencil + 2)
    ends = ((0, 2), (34, 36))
    rims = []
    for a, dz in sides:
        rims.append((z_out.at[a, 2:34], z_in.at[1 - a], on_slab(dz)))
    for b, dx in sides:
        rims.append((grid_at.at[ends[b][0] : ends[b][1], :, 8:40, :], x_in.at[1 - b], on_pencil(dx)))
    for a, dz in sides:
        for b, dx in sides:
            rims.append((z_out.at[a, ends[b][0] : ends[b][1]], corner_in.at[1 - a, 1 - b], at(dz, dx)))
    for i, (source, target, device) in enumerate(rims):
        remote(source, target, rim_send.at[i], rim_recv.at[i], device).start()

    loads[2].wait()
    wait_recv(z_in.at[1], rim_recv.at[0])
    wait_recv(z_in.at[0], rim_recv.at[1])

    def add_rims(x, carry):
        for tile in range(4):
            charge[x, tile, 0:2, :] += z_in[0, x, 2 * tile : 2 * tile + 2, :]
            charge[x, tile, 30:32, :] += z_in[1, x, 2 * tile : 2 * tile + 2, :]
        return carry

    lax.fori_loop(0, 32, add_rims, 0, unroll=4)
    loads[3].wait()

    def forward_y(step, carry):
        chunk = lax.rem(step + 1, CHUNKS)

        @pl.when(step == 2)
        def _():
            for i in range(2, 8):
                wait_recv(rims[i][1], rim_recv.at[i])
            for b, start in ((0, 0), (1, 30)):
                charge[start : start + 2] += x_in[b]
                for a, row in ((0, 0), (1, 30)):
                    for x in range(2):
                        for tile in range(4):
                            charge[start + x, tile, row : row + 2, :] += corner_in[a, b, x, 2 * tile : 2 * tile + 2, :]

        tiles = [charge[pl.ds(8 * chunk, 8), tile].reshape(256, 128) for tile in range(4)]
        for parity in range(2):
            if parity:
                halved = [tiles[0] - tiles[2], tiles[1] - tiles[3]]
            else:
                halved = [tiles[0] + tiles[2], tiles[1] + tiles[3]]
            columns = halves(jnp.concatenate(halved, axis=1))
            freqs = dot_3((ty[0, parity], ty[1, parity]), columns, ((1,), (1,)))
            sent_1[parity, chunk] = freqs.reshape(n_slab, 32, 256)
        return to_slabs(0, chunk)

    def to_slabs(parity, chunk):
        got_1[parity, chunk, slab] = sent_1[parity, chunk, slab]

        def send(k, carry):
            device = on_slab(k)
            remote(
                sent_1.at[parity, chunk, device[0]], got_1.at[parity, chunk, slab], send_1, recv_1.at[parity, chunk], device
            ).start()
            return carry

        return lax.fori_loop(1, n_slab, send, 0)

    lax.fori_loop(0, CHUNKS, forward_y, 0)
    lax.fori_loop(0, CHUNKS, lambda step, carry: to_slabs(1, lax.rem(step + 1, CHUNKS)), 0)

    slots, panels = charges.shape
    loads[5].wait()
    first = jnp.logical_and(slab == 0, pencil == 0)
    middle = jnp.logical_and(slab == 4, pencil == 0)

    @pl.when(middle)
    def _():
        for kx in range(2):
            for i in range(2):
                level_out[kx, :, 128 * i : 128 * i + 128] = kernel[pl.ds(8 * kx + 4 * i, 256, stride=16), :]
        remote(level_out, level_in, level_send, level_recv, (0, pencil)).start()

    slot = lax.broadcasted_iota(jnp.int32, (slots, panels), 0)
    coarse = jnp.where(slot < count[...], charges[...], 0.0).astype(BF16)
    slot = lax.broadcasted_iota(jnp.int32, (slots, slots), 0)
    chosen = jnp.where(slot == pairs[1:2, :], 1.0, 0.0)
    sources[...] = jnp.dot(chosen.T.astype(BF16), coarse, preferred_element_type=F32)
    loads[4].wait()
    loads[7].wait()

    def near_group(group, carry):
        rows = pl.ds(pl.multiple_of(8 * group, 8), 8)
        taken = sources[rows, :].astype(BF16)
        row = lax.broadcasted_iota(jnp.int32, (8, panels), 0)
        total = jnp.zeros((8, panels), F32)
        for i in range(8):
            found = lax.dot_general(
                taken, matrices[8 * group + i], (((1,), (1,)), ((), ())), preferred_element_type=F32
            )
            total = jnp.where(row == i, found, total)
        terms[rows, :] = total
        return carry

    near_groups = slots // 8 // (4 * CHUNKS)

    def near_share(turn):
        lax.fori_loop(turn * near_groups, (turn + 1) * near_groups, near_group, 0)

    def forward_z(turn, carry):
        parity, chunk = turn // CHUNKS, lax.rem(turn + 1, CHUNKS)
        near_share(turn)
        wait_recv(got_1.at[parity, chunk, 0 : n_slab - 1], recv_1.at[parity, chunk])
        for h in range(2):
            for q in range(2):
                tiles = swap_groups([got_1[parity, chunk, 4 * q + s, :, 128 * h : 128 * h + 128] for s in range(4)])
                for a in range(4):
                    for part in range(2):
                        lines[2 * part + q, pl.ds(4 * h + a, 16, stride=8), :] = tiles[a][16 * part : 16 * part + 16]
        rows = halves(jnp.concatenate([lines[i] for i in range(4)], axis=1))
        freqs = dot_3(rows, (tz[0], tz[1]))
        for part in range(2):
            sent_2[parity, chunk, :, part] = freqs[:, 256 * part : 256 * part + 256].reshape(n_pencil, 8, 256)
        mine = pl.ds(pl.multiple_of(pencil * 32 + chunk * 8, 8), 8)
        got_2[parity, :, mine, :] = sent_2[parity, chunk, pencil]

        def send(k, carry):
            device = on_pencil(k)
            remote(
                sent_2.at[parity, chunk, device[1]], got_2.at[parity, :, mine, :], send_2, recv_2.at[parity], device
            ).start()
            return carry

        return lax.fori_loop(1, n_pencil, send, carry)

    lax.fori_loop(0, 2 * CHUNKS - 2, forward_z, 0)

    loads[6].wait()
    unit = 1.0 / (NX * NY * NZ)

    def stacked(real, imag):
        real, imag = halves(real), halves(imag)
        return tuple(
            jnp.concatenate([jnp.concatenate([r, i], axis=1), jnp.concatenate([i, -r], axis=1)], axis=0)
            for r, i in zip(real, imag)
        )

    def along_x(parity):
        wait_recv(got_2.at[parity, :, 0 : 32 * (n_pencil - 1), :], recv_2.at[parity])
        for kx in range(2):
            parts = []
            for part in range(2):
                low, high = got_2[parity, part, 0:256, :], got_2[parity, part, 256:512, :]
                parts.append(low - high if kx else low + high)
            table = (tx[0, kx], tx[1, kx])
            found = dot_3(table, stacked(*parts))
            if parity:
                green = jnp.concatenate(
                    [kernel[pl.ds(8 * kx + 4 * i + 1, 256, stride=16), :] for i in range(2)], axis=1
                ) * (2.0 * unit)
            else:
                own = jnp.where(slab < 4, 0, 2)
                green = jnp.concatenate(
                    [kernel[pl.ds(own + 8 * kx + 4 * i, 256, stride=16), :] for i in range(2)], axis=1
                ) * jnp.where(first, unit, 2.0 * unit)
            spectra[kx, 0] = found[:, 0:256] * green
            spectra[kx, 1] = found[:, 256:512] * green
            if not parity:

                @pl.when(first)
                def _():
                    if not kx:
                        wait_recv(level_in, level_recv)
                    other = level_in[kx] * unit
                    row = lax.broadcasted_iota(jnp.int32, (256, 256), 0)
                    lane = lax.broadcasted_iota(jnp.int32, (256, 256), 1)
                    mirror = jnp.where((row + lane) % 256 == 0, 1.0, 0.0).astype(BF16)
                    flipped = [
                        sum(jnp.dot(piece, mirror, preferred_element_type=F32) for piece in halves(value)) for value in parts
                    ]
                    twin = dot_3(table, stacked(flipped[0], -flipped[1]))
                    mean, rest = 0.5 * (green + other), 0.5 * (green - other)
                    for part in range(2):
                        lanes = slice(256 * part, 256 * part + 256)
                        spectra[kx, part] = mean * found[:, lanes] + rest * twin[:, lanes]

        ends = []
        for kx in range(2):
            table = (tx[0, 2 * kx], tx[1, 2 * kx])
            real, imag = halves(spectra[kx, 0]), halves(spectra[kx, 1])
            right = tuple(
                jnp.concatenate([jnp.concatenate([r, i], axis=1), jnp.concatenate([-i, r], axis=1)], axis=0)
                for r, i in zip(real, imag)
            )
            ends.append(dot_3(table, right))
        for part in range(2):
            lanes = slice(256 * part, 256 * part + 256)
            back_2[parity, part, 0:256, :] = ends[0][:, lanes] + ends[1][:, lanes]
            back_2[parity, part, 256:512, :] = ends[0][:, lanes] - ends[1][:, lanes]

    def turns(step):
        return jnp.where(step < 2, 3 * step, step - 1)

    def return_x(turn, carry):
        parity, chunk = turn // CHUNKS, turns(lax.rem(turn, CHUNKS))
        own = pl.ds(pl.multiple_of(pencil * 32 + chunk * 8, 8), 8)
        took_2[parity, chunk, pencil] = back_2[parity, :, own, :]

        def send(k, carry):
            device = on_pencil(k)
            rows = pl.ds(pl.multiple_of(device[1] * 32 + chunk * 8, 8), 8)
            remote(
                back_2.at[parity, :, rows, :], took_2.at[parity, chunk, pencil], send_3, recv_3.at[parity, chunk], device
            ).start()
            return carry

        return lax.fori_loop(1, n_pencil, send, carry)

    def inverse_z(turn, carry):
        parity, chunk = turn // CHUNKS, turns(lax.rem(turn, CHUNKS))
        near_share(2 * CHUNKS + turn)
        wait_recv(took_2.at[parity, chunk, 0 : n_pencil - 1], recv_3.at[parity, chunk])
        rows = jnp.concatenate([took_2[parity, chunk, :, part].reshape(128, 256) for part in range(2)], axis=1)
        space = dot_3(halves(rows), (tz[0], tz[1]), ((1,), (1,)))
        for i in range(4):
            lines[i] = space[:, 128 * i : 128 * i + 128]
        for h in range(2):
            for q in range(2):
                tiles = []
                for a in range(4):
                    pieces = [lines[2 * part + q, pl.ds(4 * h + a, 16, stride=8), :] for part in range(2)]
                    tiles.append(jnp.concatenate(pieces, axis=0))
                for s, tile in enumerate(swap_groups(tiles)):
                    back_1[parity, chunk, 4 * q + s, :, 128 * h : 128 * h + 128] = tile
        took_1[parity, chunk, slab] = back_1[parity, chunk, slab]

        def send(k, carry):
            device = on_slab(k)
            remote(
                back_1.at[parity, chunk, device[0]], took_1.at[parity, chunk, slab], send_4, recv_4.at[parity, chunk], device
            ).start()
            return carry

        return lax.fori_loop(1, n_slab, send, carry)

    along_x(0)
    lax.fori_loop(0, 2, return_x, 0)
    lax.fori_loop(2, 4, lambda turn, carry: return_x(turn, forward_z(turn + 4, carry)), 0)
    lax.fori_loop(0, 2, inverse_z, 0)
    along_x(1)
    lax.fori_loop(4, 8, return_x, 0)
    lax.fori_loop(2, 8, inverse_z, 0)

    slot = lax.broadcasted_iota(jnp.int32, (slots, slots), 0)
    chosen = jnp.where(slot == pairs[0:1, :], 1.0, 0.0).astype(BF16)
    rest = terms[...]
    total = jnp.zeros(near.shape, F32)
    for _ in range(3):
        part = rest.astype(BF16)
        rest = rest - part.astype(F32)
        total = total + jnp.dot(chosen, part, preferred_element_type=F32)
    near[...] = total

    row_starts = (2, 32)
    last = []
    for b, dx in sides:
        last.append((last_x_out.at[b], last_x_in.at[1 - b], on_pencil(dx)))
        for a, dz in sides:
            rows = (0, 2) if b == 0 else (6, 8)
            last.append(
                (last_z_out.at[3 * b, a, rows[0] : rows[1]], last_corner_in.at[1 - b, 1 - a], at(dz, dx))
            )

    def planes(chunk, a):
        return (last_z_out.at[chunk, a], last_z_in.at[chunk, 1 - a], last_send.at[6 + a], last_recv.at[chunk, 1 - a])

    def take_planes(step, carry):
        chunk = turns(step)
        for a, row in ((0, 6), (1, 40)):
            wait_recv(last_z_in.at[chunk, a], last_recv.at[chunk, a])
            for x in range(8):
                for tile in range(4):
                    out[pl.ds(row_of(2 + 8 * chunk + x, tile, row), 2), :] = last_z_in[chunk, a, x, 2 * tile : 2 * tile + 2, :]
        return carry

    def inverse_y(step, carry):
        chunk = turns(step)
        ends = []
        for parity in range(2):
            wait_recv(took_1.at[parity, chunk, 0 : n_slab - 1], recv_4.at[parity, chunk])
            columns = took_1[parity, chunk].reshape(256, 256).T
            ends.append(dot_3(halves(columns), (ty[0, parity], ty[1, parity])))
        space = (ends[0] + ends[1], ends[0] - ends[1])
        for tile in range(4):
            lanes = slice(128 * (tile % 2), 128 * (tile % 2) + 128)
            cells = space[tile // 2][:, lanes].reshape(8, 32, 128)
            for x in range(8):
                out[pl.ds(pl.multiple_of(row_of(2 + 8 * chunk + x, tile, 8), 8), 32), :] = cells[x]
            last_z_out[chunk, 0, :, 2 * tile : 2 * tile + 2, :] = cells[:, 0:2, :]
            last_z_out[chunk, 1, :, 2 * tile : 2 * tile + 2, :] = cells[:, 30:32, :]
        for a, dz in sides:
            remote(*planes(chunk, a), on_slab(dz)).start()
        for b in range(2):

            @pl.when(chunk == 3 * b)
            def _():
                for x in range(2):
                    for tile in range(4):
                        last_x_out[b, x, tile] = out[pl.ds(row_of(row_starts[b] + x, tile, 8), 32), :]
                for i in range(3 * b, 3 * b + 3):
                    source, target, device = last[i]
                    remote(source, target, last_send.at[i], corner_recv.at[i], device).start()

        return carry

    lax.fori_loop(0, CHUNKS, inverse_y, 0)
    lax.fori_loop(0, CHUNKS - 1, take_planes, 0)
    for i, (source, target, device) in enumerate(last):
        wait_recv(target, corner_recv.at[i])
        wait_send(source, last_send.at[i])
    for b, start in ((0, 0), (1, 34)):
        for x in range(2):
            for tile in range(4):
                out[pl.ds(row_of(start + x, tile, 8), 32), :] = last_x_in[b, x, tile]
                for a, row in ((0, 6), (1, 40)):
                    out[pl.ds(row_of(start + x, tile, row), 2), :] = last_corner_in[b, a, x, 2 * tile : 2 * tile + 2, :]
    for i, (source, target, device) in enumerate(rims):
        wait_send(source, rim_send.at[i])
    wait_send(sent_1.at[:, :, 0 : n_slab - 1], send_1)
    wait_send(got_2.at[:, :, 0 : 32 * (n_pencil - 1), :], send_2)
    wait_send(got_2.at[:, :, 0 : 32 * (n_pencil - 1), :], send_3)
    wait_send(back_1.at[:, :, 0 : n_slab - 1], send_4)

    @pl.when(middle)
    def _():
        wait_send(level_out, level_send)

    take_planes(CHUNKS - 1, 0)
    for a in range(2):
        wait_send(last_z_out.at[:, a], last_send.at[6 + a])

    def gather_group(step, carry):
        def pick(turn, carry):
            for u in range(UNROLL):
                b = turn * UNROLL + u
                row_0, row_1, lane_0 = window(anchors, step * GROUP + b)
                masks, beyond, top = window_masks(lane_0)
                for i in range(4):
                    cells = jnp.where(beyond, out[pl.ds(row_0 + 192 * i, 8), :], out[pl.ds(row_1 + 192 * i, 8), :])
                    cells = jnp.where(top, cells, pltpu.roll(cells, 4, 0))
                    for j in range(2):
                        values[b, 16 * i + 8 * j : 16 * i + 8 * j + 8] = jnp.where(masks[j], cells, 0.0)
            return carry

        lax.fori_loop(0, GROUP // UNROLL, pick, 0)
        group_copy(step, projection_at, projection, group_load).wait()
        rows = group_rows(step)
        box = lane_sums(values[...].reshape(GROUP * BOX, 128)).reshape(GROUP, BOX, 128)
        far = jnp.sum(projection[rows] * box, axis=1)
        slot = step * GROUP + lax.broadcasted_iota(jnp.int32, (GROUP, 128), 0)
        result[rows, :] = jnp.where(slot < count[...], far + near[rows, :], 0.0)
        return carry

    lax.fori_loop(0, slots // GROUP, gather_group, 0)


def field(anchors, count, pairs, charges, grid, projection, matrices, kernel):
    tables = [jnp.asarray(np.stack(split_table(table))) for table in (y_tables(), z_table(), x_tables())]
    slots, panels = charges.shape
    dma = pltpu.SemaphoreType.DMA
    vmem = pltpu.VMEM
    return pl.pallas_call(
        field_kernel,
        in_specs=[
            pl.BlockSpec(memory_space=pltpu.SMEM),
            *[pl.BlockSpec(memory_space=vmem)] * 3,
            *[pl.BlockSpec(memory_space=pl.ANY)] * 7,
        ],
        out_specs=pl.BlockSpec(memory_space=vmem),
        out_shape=jax.ShapeDtypeStruct((slots, panels), F32),
        scratch_shapes=[
            vmem(projection.shape, F32),
            vmem(matrices.shape, BF16),
            vmem(kernel.shape, F32),
            *(vmem(table.shape, BF16) for table in tables),
            vmem((slots, panels), F32),
            vmem((slots, panels), F32),
            vmem((slots, panels), F32),
            vmem((GROUP, BOX, panels), F32),
            vmem((36 * 4 * 48, 128), F32),
            vmem((32, 4, 32, 128), F32),
            vmem((2, 36, 4, 8, 128), F32),
            vmem((2, 36, 8, 128), F32),
            vmem((2, 32, 8, 128), F32),
            vmem((2, 2, 4, 32, 128), F32),
            vmem((2, 2, 2, 8, 128), F32),
            vmem((2, CHUNKS, 8, 32, 256), F32),
            vmem((2, CHUNKS, 8, 32, 256), F32),
            vmem((2, CHUNKS, 16, 2, 8, 256), F32),
            vmem((2, 2, 512, 256), F32),
            vmem((2, 256, 256), F32),
            vmem((2, 256, 256), F32),
            vmem((2, 2, 256, 256), F32),
            vmem((2, 2, 512, 256), F32),
            vmem((2, CHUNKS, 16, 2, 8, 256), F32),
            vmem((2, CHUNKS, 8, 32, 256), F32),
            vmem((2, CHUNKS, 8, 32, 256), F32),
            vmem((4, 128, 128), F32),
            vmem((CHUNKS, 2, 8, 8, 128), F32),
            vmem((CHUNKS, 2, 8, 8, 128), F32),
            vmem((2, 2, 4, 32, 128), F32),
            vmem((2, 2, 4, 32, 128), F32),
            vmem((2, 2, 2, 8, 128), F32),
            dma((8,)),
            dma((slots // GROUP,)),
            dma,
            dma,
            dma((8,)),
            dma((8,)),
            dma((8,)),
            dma((CHUNKS, 2)),
            dma((6,)),
            dma,
            dma((2, CHUNKS)),
            dma,
            dma((2,)),
            dma,
            dma((2, CHUNKS)),
            dma,
            dma((2, CHUNKS)),
        ],
        compiler_params=pltpu.CompilerParams(
            collective_id=0, has_side_effects=True, vmem_limit_bytes=62 << 20
        ),
        cost_estimate=pl.CostEstimate(flops=10**10, bytes_accessed=10**7, transcendentals=0),
    )(anchors, count, pairs, charges, grid, projection, matrices, kernel, *tables)


def shards(charges, projection, anchors, block_count, near_pairs, near_matrices, kernel_hat):
    panels = charges.shape[1]
    grid = scatter(anchors.T, block_count, projection, charges).reshape(36, 4, 48, 128)
    levels = jnp.transpose(kernel_hat.reshape(NX, 4, 2, 128), (0, 2, 1, 3)).reshape(NX * 8, 128)
    count = jnp.broadcast_to(block_count[:, None], (1, panels))
    return field(anchors.T, count, near_pairs.T, charges, grid, projection, near_matrices, levels)


def solution(mesh):
    return jax.shard_map(
        shards,
        mesh=mesh,
        in_specs=(
            P(("slab", "pencil"), None),
            P(("slab", "pencil"), None, None),
            P(("slab", "pencil"), None),
            P(("slab", "pencil")),
            P(("slab", "pencil"), None),
            P(("slab", "pencil"), None, None),
            P(None, ("slab", "pencil"), None),
        ),
        out_specs=P(("slab", "pencil"), None),
        check_vma=False,
    )
```

```python
import jax
import jax.numpy as jnp
import ml_dtypes
import numpy as np
from jax import lax
from jax.experimental import pallas as pl
from jax.experimental.pallas import tpu as pltpu
from jax.sharding import PartitionSpec as P

NX, NY, NZ, BOX = 512, 512, 256, 64
GROUP = 64
UNROLL = 4
AHEAD = 2
F32, BF16 = jnp.float32, jnp.bfloat16


def halves(value):
    high = value.astype(BF16)
    return high, (value - high.astype(F32)).astype(BF16)


def lane_sums(value):
    ones = jnp.ones((128, 128), BF16)
    high, low = halves(value)
    return jnp.dot(high, ones, preferred_element_type=F32) + jnp.dot(low, ones, preferred_element_type=F32)


def row_of(x, tile, z):
    return (x * 4 + tile) * 48 + z


def window(anchors, slot):
    corner = row_of(anchors[0, slot] & 31, 0, (anchors[2, slot] & 31) + 6)
    y_at = (anchors[1, slot] + (NY - 2)) & (NY - 1)
    tile = y_at >> 7
    return corner + 48 * tile, corner + 48 * ((tile + 1) & 3), y_at & 127


def window_masks(lane_0):
    row = lax.broadcasted_iota(jnp.int32, (8, 128), 0)
    lane = lax.broadcasted_iota(jnp.int32, (8, 128), 1)
    shifted = (lane - row // 4 - lane_0) & 127
    return (shifted == 0, shifted == 2), lane >= lane_0, row < 4


def group_rows(step):
    return pl.ds(pl.multiple_of(step * GROUP, GROUP), GROUP)


def group_copy(step, source, target, sems):
    return pltpu.make_async_copy(source.at[group_rows(step)], target.at[group_rows(step)], sems.at[step])


def scatter_kernel(anchors, count, projection_at, charges, cells, projection, values, load):
    grid = cells.reshape(36 * 4 * 48, 128)
    for step in range(AHEAD):
        group_copy(step, projection_at, projection, load).start()

    def clear(x, carry):
        grid[pl.ds(pl.multiple_of(x * 192, 8), 192), :] = jnp.zeros((192, 128), F32)
        return carry

    lax.fori_loop(0, 36, clear, 0)

    def group(step, carry):
        @pl.when(step < charges.shape[0] // GROUP - AHEAD)
        def _():
            group_copy(step + AHEAD, projection_at, projection, load).start()

        group_copy(step, projection_at, projection, load).wait()
        rows = group_rows(step)
        slot = step * GROUP + lax.broadcasted_iota(jnp.int32, (GROUP, 128), 0)
        masked = jnp.where(slot < count[0], charges[rows, :], 0.0)
        products = projection[rows] * masked[:, None, :]
        values[...] = lane_sums(products.reshape(GROUP * BOX, 128)).reshape(GROUP, BOX, 128)

        def place(turn, carry):
            firsts, seconds, furthest = [], [], 0
            for u in range(UNROLL):
                b = turn * UNROLL + u
                row_0, row_1, lane_0 = window(anchors, step * GROUP + b)
                masks, beyond, top = window_masks(lane_0)
                here, there = beyond & top, top & ~beyond
                furthest = jnp.maximum(furthest, lane_0)
                for i in range(4):
                    patch = jnp.where(masks[0], values[b, 16 * i : 16 * i + 8], 0.0)
                    patch = jnp.where(masks[1], values[b, 16 * i + 8 : 16 * i + 16], patch)
                    patch = patch + pltpu.roll(patch, 4, 0)
                    firsts.append((row_0 + 192 * i, jnp.where(here, patch, 0.0)))
                    seconds.append((row_1 + 192 * i, there, patch))
            for row, patch in firsts:
                grid[pl.ds(row, 8), :] += patch

            @pl.when(furthest > 124)
            def _():
                for row, there, patch in seconds:
                    grid[pl.ds(row, 8), :] += jnp.where(there, patch, 0.0)

            return carry

        return lax.fori_loop(0, GROUP // UNROLL, place, carry)

    lax.fori_loop(0, charges.shape[0] // GROUP, group, 0)


def scatter(anchors, count, projection, charges):
    slots = charges.shape[0]
    smem, vmem = pl.BlockSpec(memory_space=pltpu.SMEM), pl.BlockSpec(memory_space=pltpu.VMEM)
    return pl.pallas_call(
        scatter_kernel,
        in_specs=[smem, smem, pl.BlockSpec(memory_space=pl.ANY), vmem],
        out_specs=pl.BlockSpec(memory_space=pltpu.VMEM),
        scratch_shapes=[
            pltpu.VMEM(projection.shape, F32),
            pltpu.VMEM((GROUP, BOX, 128), F32),
            pltpu.SemaphoreType.DMA((slots // GROUP,)),
        ],
        out_shape=pltpu.VMEM((36, 4, 48, 128), F32),
        compiler_params=pltpu.CompilerParams(vmem_limit_bytes=57 << 20),
    )(anchors, count, projection, charges)


CHUNKS = 4
MESH = pl.DeviceIdType.MESH


def phases(product, length):
    angle = 2.0 * np.pi * (product % length) / length
    return np.cos(angle), np.sin(angle)


def split_table(table):
    table = table.astype(np.float32)
    high = table.astype(ml_dtypes.bfloat16)
    return high, (table - high.astype(np.float32)).astype(ml_dtypes.bfloat16)


def y_tables():
    slab, part, pencil = np.meshgrid(np.arange(8), np.arange(2), np.arange(16), indexing="ij")
    device = (slab * 16 + pencil).reshape(-1, 1)
    part = part.reshape(-1, 1)
    even = np.where(device < 64, 4 * device, 4 * device + 2)
    odd = 4 * device + 1
    position = np.arange(256)[None, :]
    result = []
    for freq in (even, odd):
        cos, sin = phases(freq * position, NY)
        table = np.where(part == 0, cos, -sin)
        if freq is even:
            table[(device[:, 0] == 0) & (part[:, 0] == 1)] = 1.0 - 2.0 * (position[0] % 2)
        result.append(table)
    return np.stack(result)


def z_table():
    position = np.arange(NZ)
    cos, sin = phases(position[:, None] * position[None, :], NZ)
    return np.block([[cos, -sin], [sin, cos]])


def x_tables():
    position = np.arange(256)
    result = []
    for parity in range(2):
        cos, sin = phases((2 * position[:, None] + parity) * position[None, :], NX)
        result.append(np.concatenate([cos, sin], axis=1))
        if parity:
            result.append(np.concatenate([cos.T, sin.T], axis=1))
    return np.stack(result)


def dot_3(left, right, dims=((1,), (0,))):
    def one(a, b):
        return lax.dot_general(a, b, (dims, ((), ())), preferred_element_type=F32)

    return one(left[0], right[0]) + (one(left[0], right[1]) + one(left[1], right[0]))


def swap_groups(tiles):
    lane = lax.broadcasted_iota(jnp.int32, tiles[0].shape, 1)
    low, even = lane < 64, lane % 64 < 32
    firsts, lasts = [], []
    for a, b in ((tiles[0], tiles[2]), (tiles[1], tiles[3])):
        firsts.append(jnp.where(low, a, pltpu.roll(b, 64, 1)))
        lasts.append(jnp.where(low, pltpu.roll(a, 64, 1), b))
    result = []
    for a, b in (firsts, lasts):
        result.append(jnp.where(even, a, pltpu.roll(b, 32, 1)))
        result.append(jnp.where(even, pltpu.roll(a, 96, 1), b))
    return result


def field_kernel(
    anchors, count, pairs, charges, grid, projection_at, matrices_at, kernel_at, ty_at, tz_at, tx_at,
    result,
    projection, matrices, kernel, ty, tz, tx, sources, terms, near, values, out,
    charge, z_out, z_in, x_in, corner_in, sent_1, got_1, sent_2, got_2, level_out, level_in, spectra, back_2, took_2,
    back_1, took_1, lines, last_z_out, last_z_in, last_x_out, last_x_in, last_corner_in,
    load, group_load, level_send, level_recv, rim_send, rim_recv, last_send, last_recv, corner_recv,
    send_1, recv_1, send_2, recv_2, send_3, recv_3, send_4, recv_4,
):
    slab, pencil = lax.axis_index("slab"), lax.axis_index("pencil")
    n_slab, n_pencil = 8, 16

    def at(slab_step, pencil_step):
        return (lax.rem(slab + n_slab + slab_step, n_slab), lax.rem(pencil + n_pencil + pencil_step, n_pencil))

    def on_slab(step):
        return at(step, 0)

    def on_pencil(step):
        return at(0, step)

    def remote(source, target, send_sem, recv_sem, device):
        return pltpu.make_async_remote_copy(
            src_ref=source, dst_ref=target, send_sem=send_sem, recv_sem=recv_sem, device_id=device, device_id_type=MESH
        )

    def wait_recv(ref, sem):
        remote(ref, ref, sem, sem, on_slab(1)).wait_recv()

    def wait_send(ref, sem):
        remote(ref, ref, sem, sem, on_slab(1)).wait_send()

    barrier = pltpu.get_barrier_semaphore()

    def greet(device):
        pl.semaphore_signal(barrier, inc=1, device_id=device, device_id_type=MESH)

    def greet_slab(step, carry):
        greet(on_slab(step))
        return carry

    def greet_pencil(step, carry):
        greet(on_pencil(step))
        return carry

    sides = ((0, -1), (1, 1))
    lax.fori_loop(1, n_slab, greet_slab, 0)
    lax.fori_loop(1, n_pencil, greet_pencil, 0)
    for _, dz in sides:
        for _, dx in sides:
            greet(at(dz, dx))

    loads = [
        pltpu.make_async_copy(source, target, load.at[i])
        for i, (source, target) in enumerate(
            (
                (grid.at[2:34, :, 8:40, :], charge),
                (ty_at, ty),
                (tz_at, tz),
                (kernel_at, kernel),
                (tx_at, tx),
                (matrices_at, matrices),
            )
        )
    ]
    for copy in loads[:2]:
        copy.start()

    def pack_rims(x, carry):
        for tile in range(4):
            z_out[0, x, 2 * tile : 2 * tile + 2, :] = grid[x, tile, 6:8, :]
            z_out[1, x, 2 * tile : 2 * tile + 2, :] = grid[x, tile, 40:42, :]
        return carry

    lax.fori_loop(0, 36, pack_rims, 0, unroll=4)
    pl.semaphore_wait(barrier, n_slab + n_pencil + 2)
    ends = ((0, 2), (34, 36))
    rims = []
    for a, dz in sides:
        rims.append((z_out.at[a, 2:34], z_in.at[1 - a], on_slab(dz)))
    for b, dx in sides:
        rims.append((grid.at[ends[b][0] : ends[b][1], :, 8:40, :], x_in.at[1 - b], on_pencil(dx)))
    for a, dz in sides:
        for b, dx in sides:
            rims.append((z_out.at[a, ends[b][0] : ends[b][1]], corner_in.at[1 - a, 1 - b], at(dz, dx)))
    for i, (source, target, device) in enumerate(rims):
        remote(source, target, rim_send.at[i], rim_recv.at[i], device).start()
    for copy in loads[2:]:
        copy.start()

    loads[0].wait()
    wait_recv(z_in.at[1], rim_recv.at[0])
    wait_recv(z_in.at[0], rim_recv.at[1])

    def add_rims(x, carry):
        for tile in range(4):
            charge[x, tile, 0:2, :] += z_in[0, x, 2 * tile : 2 * tile + 2, :]
            charge[x, tile, 30:32, :] += z_in[1, x, 2 * tile : 2 * tile + 2, :]
        return carry

    lax.fori_loop(0, 32, add_rims, 0, unroll=4)
    loads[1].wait()

    def forward_y(step, carry):
        chunk = lax.rem(step + 1, CHUNKS)

        @pl.when(step == 2)
        def _():
            for i in range(2, 8):
                wait_recv(rims[i][1], rim_recv.at[i])
            for b, start in ((0, 0), (1, 30)):
                charge[start : start + 2] += x_in[b]
                for a, row in ((0, 0), (1, 30)):
                    for x in range(2):
                        for tile in range(4):
                            charge[start + x, tile, row : row + 2, :] += corner_in[a, b, x, 2 * tile : 2 * tile + 2, :]

        tiles = [charge[pl.ds(8 * chunk, 8), tile].reshape(256, 128) for tile in range(4)]
        for parity in range(2):
            if parity:
                halved = [tiles[0] - tiles[2], tiles[1] - tiles[3]]
            else:
                halved = [tiles[0] + tiles[2], tiles[1] + tiles[3]]
            columns = halves(jnp.concatenate(halved, axis=1))
            freqs = dot_3((ty[0, parity], ty[1, parity]), columns, ((1,), (1,)))
            sent_1[parity, chunk] = freqs.reshape(n_slab, 32, 256)
        return to_slabs(0, chunk)

    def to_slabs(parity, chunk):
        got_1[parity, chunk, slab] = sent_1[parity, chunk, slab]

        def send(k, carry):
            device = on_slab(k)
            remote(
                sent_1.at[parity, chunk, device[0]], got_1.at[parity, chunk, slab], send_1, recv_1.at[parity, chunk], device
            ).start()
            return carry

        return lax.fori_loop(1, n_slab, send, 0)

    lax.fori_loop(0, CHUNKS, forward_y, 0)
    lax.fori_loop(0, CHUNKS, lambda step, carry: to_slabs(1, lax.rem(step + 1, CHUNKS)), 0)
    for step in range(charges.shape[0] // GROUP):
        group_copy(step, projection_at, projection, group_load).start()

    slots, panels = charges.shape
    loads[3].wait()
    first = jnp.logical_and(slab == 0, pencil == 0)
    middle = jnp.logical_and(slab == 4, pencil == 0)

    @pl.when(middle)
    def _():
        for kx in range(2):
            for i in range(2):
                level_out[kx, :, 128 * i : 128 * i + 128] = kernel[pl.ds(8 * kx + 4 * i, 256, stride=16), :]
        remote(level_out, level_in, level_send, level_recv, (0, pencil)).start()

    slot = lax.broadcasted_iota(jnp.int32, (slots, panels), 0)
    coarse = jnp.where(slot < count[0], charges[...], 0.0).astype(BF16)
    slot = lax.broadcasted_iota(jnp.int32, (slots, slots), 0)
    chosen = jnp.where(slot == pairs[1:2, :], 1.0, 0.0)
    sources[...] = jnp.dot(chosen.T.astype(BF16), coarse, preferred_element_type=F32)
    loads[2].wait()
    loads[5].wait()

    def near_group(group, carry):
        rows = pl.ds(pl.multiple_of(8 * group, 8), 8)
        taken = sources[rows, :].astype(BF16)
        row = lax.broadcasted_iota(jnp.int32, (8, panels), 0)
        total = jnp.zeros((8, panels), F32)
        for i in range(8):
            found = lax.dot_general(
                taken, matrices[8 * group + i], (((1,), (1,)), ((), ())), preferred_element_type=F32
            )
            total = jnp.where(row == i, found, total)
        terms[rows, :] = total
        return carry

    near_groups = slots // 8 // (4 * CHUNKS)

    def near_share(turn):
        lax.fori_loop(turn * near_groups, (turn + 1) * near_groups, near_group, 0)

    def forward_z(turn, carry):
        parity, chunk = turn // CHUNKS, lax.rem(turn + 1, CHUNKS)
        near_share(turn)
        wait_recv(got_1.at[parity, chunk, 0 : n_slab - 1], recv_1.at[parity, chunk])
        for h in range(2):
            for q in range(2):
                tiles = swap_groups([got_1[parity, chunk, 4 * q + s, :, 128 * h : 128 * h + 128] for s in range(4)])
                for a in range(4):
                    for part in range(2):
                        lines[2 * part + q, pl.ds(4 * h + a, 16, stride=8), :] = tiles[a][16 * part : 16 * part + 16]
        rows = halves(jnp.concatenate([lines[i] for i in range(4)], axis=1))
        freqs = dot_3(rows, (tz[0], tz[1]))
        for part in range(2):
            sent_2[parity, chunk, :, part] = freqs[:, 256 * part : 256 * part + 256].reshape(n_pencil, 8, 256)
        mine = pl.ds(pl.multiple_of(pencil * 32 + chunk * 8, 8), 8)
        got_2[parity, :, mine, :] = sent_2[parity, chunk, pencil]

        def send(k, carry):
            device = on_pencil(k)
            remote(
                sent_2.at[parity, chunk, device[1]], got_2.at[parity, :, mine, :], send_2, recv_2.at[parity], device
            ).start()
            return carry

        return lax.fori_loop(1, n_pencil, send, carry)

    lax.fori_loop(0, 2 * CHUNKS - 2, forward_z, 0)

    loads[4].wait()
    unit = 1.0 / (NX * NY * NZ)

    def stacked(real, imag):
        real, imag = halves(real), halves(imag)
        return tuple(
            jnp.concatenate([jnp.concatenate([r, i], axis=1), jnp.concatenate([i, -r], axis=1)], axis=0)
            for r, i in zip(real, imag)
        )

    def along_x(parity):
        wait_recv(got_2.at[parity, :, 0 : 32 * (n_pencil - 1), :], recv_2.at[parity])
        for kx in range(2):
            parts = []
            for part in range(2):
                low, high = got_2[parity, part, 0:256, :], got_2[parity, part, 256:512, :]
                parts.append(low - high if kx else low + high)
            table = (tx[0, kx], tx[1, kx])
            found = dot_3(table, stacked(*parts))
            if parity:
                green = jnp.concatenate(
                    [kernel[pl.ds(8 * kx + 4 * i + 1, 256, stride=16), :] for i in range(2)], axis=1
                ) * (2.0 * unit)
            else:
                own = jnp.where(slab < 4, 0, 2)
                green = jnp.concatenate(
                    [kernel[pl.ds(own + 8 * kx + 4 * i, 256, stride=16), :] for i in range(2)], axis=1
                ) * jnp.where(first, unit, 2.0 * unit)
            spectra[kx, 0] = found[:, 0:256] * green
            spectra[kx, 1] = found[:, 256:512] * green
            if not parity:

                @pl.when(first)
                def _():
                    if not kx:
                        wait_recv(level_in, level_recv)
                    other = level_in[kx] * unit
                    row = lax.broadcasted_iota(jnp.int32, (256, 256), 0)
                    lane = lax.broadcasted_iota(jnp.int32, (256, 256), 1)
                    mirror = jnp.where((row + lane) % 256 == 0, 1.0, 0.0).astype(BF16)
                    flipped = [
                        sum(jnp.dot(piece, mirror, preferred_element_type=F32) for piece in halves(value)) for value in parts
                    ]
                    twin = dot_3(table, stacked(flipped[0], -flipped[1]))
                    mean, rest = 0.5 * (green + other), 0.5 * (green - other)
                    for part in range(2):
                        lanes = slice(256 * part, 256 * part + 256)
                        spectra[kx, part] = mean * found[:, lanes] + rest * twin[:, lanes]

        ends = []
        for kx in range(2):
            table = (tx[0, 2 * kx], tx[1, 2 * kx])
            real, imag = halves(spectra[kx, 0]), halves(spectra[kx, 1])
            right = tuple(
                jnp.concatenate([jnp.concatenate([r, i], axis=1), jnp.concatenate([-i, r], axis=1)], axis=0)
                for r, i in zip(real, imag)
            )
            ends.append(dot_3(table, right))
        for part in range(2):
            lanes = slice(256 * part, 256 * part + 256)
            back_2[parity, part, 0:256, :] = ends[0][:, lanes] + ends[1][:, lanes]
            back_2[parity, part, 256:512, :] = ends[0][:, lanes] - ends[1][:, lanes]

    def turns(step):
        return jnp.where(step < 2, 3 * step, step - 1)

    def return_x(turn, carry):
        parity, chunk = turn // CHUNKS, turns(lax.rem(turn, CHUNKS))
        own = pl.ds(pl.multiple_of(pencil * 32 + chunk * 8, 8), 8)
        took_2[parity, chunk, pencil] = back_2[parity, :, own, :]

        def send(k, carry):
            device = on_pencil(k)
            rows = pl.ds(pl.multiple_of(device[1] * 32 + chunk * 8, 8), 8)
            remote(
                back_2.at[parity, :, rows, :], took_2.at[parity, chunk, pencil], send_3, recv_3.at[parity, chunk], device
            ).start()
            return carry

        return lax.fori_loop(1, n_pencil, send, carry)

    def inverse_z(turn, carry):
        parity, chunk = turn // CHUNKS, turns(lax.rem(turn, CHUNKS))
        near_share(2 * CHUNKS + turn)
        wait_recv(took_2.at[parity, chunk, 0 : n_pencil - 1], recv_3.at[parity, chunk])
        rows = jnp.concatenate([took_2[parity, chunk, :, part].reshape(128, 256) for part in range(2)], axis=1)
        space = dot_3(halves(rows), (tz[0], tz[1]), ((1,), (1,)))
        for i in range(4):
            lines[i] = space[:, 128 * i : 128 * i + 128]
        for h in range(2):
            for q in range(2):
                tiles = []
                for a in range(4):
                    pieces = [lines[2 * part + q, pl.ds(4 * h + a, 16, stride=8), :] for part in range(2)]
                    tiles.append(jnp.concatenate(pieces, axis=0))
                for s, tile in enumerate(swap_groups(tiles)):
                    back_1[parity, chunk, 4 * q + s, :, 128 * h : 128 * h + 128] = tile
        took_1[parity, chunk, slab] = back_1[parity, chunk, slab]

        def send(k, carry):
            device = on_slab(k)
            remote(
                back_1.at[parity, chunk, device[0]], took_1.at[parity, chunk, slab], send_4, recv_4.at[parity, chunk], device
            ).start()
            return carry

        return lax.fori_loop(1, n_slab, send, carry)

    along_x(0)
    lax.fori_loop(0, 2, return_x, 0)
    lax.fori_loop(2, 4, lambda turn, carry: return_x(turn, forward_z(turn + 4, carry)), 0)
    lax.fori_loop(0, 2, inverse_z, 0)
    along_x(1)
    lax.fori_loop(4, 8, return_x, 0)
    lax.fori_loop(2, 8, inverse_z, 0)

    row_starts = (2, 32)
    last = []
    for b, dx in sides:
        last.append((last_x_out.at[b], last_x_in.at[1 - b], on_pencil(dx)))
        for a, dz in sides:
            rows = (0, 2) if b == 0 else (6, 8)
            last.append(
                (last_z_out.at[3 * b, a, rows[0] : rows[1]], last_corner_in.at[1 - b, 1 - a], at(dz, dx))
            )

    def planes(chunk, a):
        return (last_z_out.at[chunk, a], last_z_in.at[chunk, 1 - a], last_send.at[6 + a], last_recv.at[chunk, 1 - a])

    def take_planes(step, carry):
        chunk = turns(step)
        for a, row in ((0, 6), (1, 40)):
            wait_recv(last_z_in.at[chunk, a], last_recv.at[chunk, a])
            for x in range(8):
                for tile in range(4):
                    out[pl.ds(row_of(2 + 8 * chunk + x, tile, row), 2), :] = last_z_in[chunk, a, x, 2 * tile : 2 * tile + 2, :]
        return carry

    def inverse_y(step, carry):
        chunk = turns(step)
        ends = []
        for parity in range(2):
            wait_recv(took_1.at[parity, chunk, 0 : n_slab - 1], recv_4.at[parity, chunk])
            columns = took_1[parity, chunk].reshape(256, 256).T
            ends.append(dot_3(halves(columns), (ty[0, parity], ty[1, parity])))
        space = (ends[0] + ends[1], ends[0] - ends[1])
        for tile in range(4):
            lanes = slice(128 * (tile % 2), 128 * (tile % 2) + 128)
            cells = space[tile // 2][:, lanes].reshape(8, 32, 128)
            for x in range(8):
                out[pl.ds(pl.multiple_of(row_of(2 + 8 * chunk + x, tile, 8), 8), 32), :] = cells[x]
            last_z_out[chunk, 0, :, 2 * tile : 2 * tile + 2, :] = cells[:, 0:2, :]
            last_z_out[chunk, 1, :, 2 * tile : 2 * tile + 2, :] = cells[:, 30:32, :]
        for a, dz in sides:
            remote(*planes(chunk, a), on_slab(dz)).start()
        for b in range(2):

            @pl.when(chunk == 3 * b)
            def _():
                for x in range(2):
                    for tile in range(4):
                        last_x_out[b, x, tile] = out[pl.ds(row_of(row_starts[b] + x, tile, 8), 32), :]
                for i in range(3 * b, 3 * b + 3):
                    source, target, device = last[i]
                    remote(source, target, last_send.at[i], corner_recv.at[i], device).start()

        return carry

    lax.fori_loop(0, CHUNKS, inverse_y, 0)

    slot = lax.broadcasted_iota(jnp.int32, (slots, slots), 0)
    chosen = jnp.where(slot == pairs[0:1, :], 1.0, 0.0).astype(BF16)
    rest = terms[...]
    total = jnp.zeros(near.shape, F32)
    for _ in range(3):
        part = rest.astype(BF16)
        rest = rest - part.astype(F32)
        total = total + jnp.dot(chosen, part, preferred_element_type=F32)
    near[...] = total

    lax.fori_loop(0, CHUNKS - 1, take_planes, 0)
    for i, (source, target, device) in enumerate(last):
        wait_recv(target, corner_recv.at[i])
        wait_send(source, last_send.at[i])
    for b, start in ((0, 0), (1, 34)):
        for x in range(2):
            for tile in range(4):
                out[pl.ds(row_of(start + x, tile, 8), 32), :] = last_x_in[b, x, tile]
                for a, row in ((0, 6), (1, 40)):
                    out[pl.ds(row_of(start + x, tile, row), 2), :] = last_corner_in[b, a, x, 2 * tile : 2 * tile + 2, :]
    for i, (source, target, device) in enumerate(rims):
        wait_send(source, rim_send.at[i])
    wait_send(sent_1.at[:, :, 0 : n_slab - 1], send_1)
    wait_send(got_2.at[:, :, 0 : 32 * (n_pencil - 1), :], send_2)
    wait_send(got_2.at[:, :, 0 : 32 * (n_pencil - 1), :], send_3)
    wait_send(back_1.at[:, :, 0 : n_slab - 1], send_4)

    @pl.when(middle)
    def _():
        wait_send(level_out, level_send)

    take_planes(CHUNKS - 1, 0)
    for a in range(2):
        wait_send(last_z_out.at[:, a], last_send.at[6 + a])

    def gather_group(step, carry):
        def pick(turn, carry):
            for u in range(UNROLL):
                b = turn * UNROLL + u
                row_0, row_1, lane_0 = window(anchors, step * GROUP + b)
                masks, beyond, top = window_masks(lane_0)
                for i in range(4):
                    cells = jnp.where(beyond, out[pl.ds(row_0 + 192 * i, 8), :], out[pl.ds(row_1 + 192 * i, 8), :])
                    cells = jnp.where(top, cells, pltpu.roll(cells, 4, 0))
                    for j in range(2):
                        values[b, 16 * i + 8 * j : 16 * i + 8 * j + 8] = jnp.where(masks[j], cells, 0.0)
            return carry

        lax.fori_loop(0, GROUP // UNROLL, pick, 0)
        group_copy(step, projection_at, projection, group_load).wait()
        rows = group_rows(step)
        box = lane_sums(values[...].reshape(GROUP * BOX, 128)).reshape(GROUP, BOX, 128)
        far = jnp.sum(projection[rows] * box, axis=1)
        result[rows, :] = far + near[rows, :]
        return carry

    lax.fori_loop(0, slots // GROUP, gather_group, 0)


def field(anchors, count, pairs, charges, grid, projection, matrices, kernel):
    tables = [jnp.asarray(np.stack(split_table(table))) for table in (y_tables(), z_table(), x_tables())]
    slots, panels = charges.shape
    dma = pltpu.SemaphoreType.DMA
    vmem = pltpu.VMEM
    return pl.pallas_call(
        field_kernel,
        in_specs=[
            *[pl.BlockSpec(memory_space=pltpu.SMEM)] * 2,
            *[pl.BlockSpec(memory_space=vmem)] * 3,
            *[pl.BlockSpec(memory_space=pl.ANY)] * 6,
        ],
        out_specs=pl.BlockSpec(memory_space=vmem),
        out_shape=jax.ShapeDtypeStruct((slots, panels), F32),
        scratch_shapes=[
            vmem(projection.shape, F32),
            vmem(matrices.shape, BF16),
            vmem(kernel.shape, F32),
            *(vmem(table.shape, BF16) for table in tables),
            vmem((slots, panels), F32),
            vmem((slots, panels), F32),
            vmem((slots, panels), F32),
            vmem((GROUP, BOX, panels), F32),
            vmem((36 * 4 * 48, 128), F32),
            vmem((32, 4, 32, 128), F32),
            vmem((2, 36, 8, 128), F32),
            vmem((2, 32, 8, 128), F32),
            vmem((2, 2, 4, 32, 128), F32),
            vmem((2, 2, 2, 8, 128), F32),
            vmem((2, CHUNKS, 8, 32, 256), F32),
            vmem((2, CHUNKS, 8, 32, 256), F32),
            vmem((2, CHUNKS, 16, 2, 8, 256), F32),
            vmem((2, 2, 512, 256), F32),
            vmem((2, 256, 256), F32),
            vmem((2, 256, 256), F32),
            vmem((2, 2, 256, 256), F32),
            vmem((2, 2, 512, 256), F32),
            vmem((2, CHUNKS, 16, 2, 8, 256), F32),
            vmem((2, CHUNKS, 8, 32, 256), F32),
            vmem((2, CHUNKS, 8, 32, 256), F32),
            vmem((4, 128, 128), F32),
            vmem((CHUNKS, 2, 8, 8, 128), F32),
            vmem((CHUNKS, 2, 8, 8, 128), F32),
            vmem((2, 2, 4, 32, 128), F32),
            vmem((2, 2, 4, 32, 128), F32),
            vmem((2, 2, 2, 8, 128), F32),
            dma((6,)),
            dma((slots // GROUP,)),
            dma,
            dma,
            dma((8,)),
            dma((8,)),
            dma((8,)),
            dma((CHUNKS, 2)),
            dma((6,)),
            dma,
            dma((2, CHUNKS)),
            dma,
            dma((2,)),
            dma,
            dma((2, CHUNKS)),
            dma,
            dma((2, CHUNKS)),
        ],
        compiler_params=pltpu.CompilerParams(
            collective_id=0, has_side_effects=True, vmem_limit_bytes=57 << 20
        ),
        cost_estimate=pl.CostEstimate(flops=10**10, bytes_accessed=10**7, transcendentals=0),
    )(anchors, count, pairs, charges, grid, projection, matrices, kernel, *tables)


def shards(charges, projection, anchors, block_count, near_pairs, near_matrices, kernel_hat):
    grid = pltpu.with_memory_space_constraint(scatter(anchors.T, block_count, projection, charges), pltpu.VMEM)
    levels = jnp.transpose(kernel_hat.reshape(NX, 4, 2, 128), (0, 2, 1, 3)).reshape(NX * 8, 128)
    total = field(anchors.T, block_count, near_pairs.T, charges, grid, projection, near_matrices, levels)
    in_use = lax.broadcasted_iota(jnp.int32, total.shape, 0) < block_count[0]
    return jnp.where(in_use, total, 0.0)


def solution(mesh):
    return jax.shard_map(
        shards,
        mesh=mesh,
        in_specs=(
            P(("slab", "pencil"), None),
            P(("slab", "pencil"), None, None),
            P(("slab", "pencil"), None),
            P(("slab", "pencil")),
            P(("slab", "pencil"), None),
            P(("slab", "pencil"), None, None),
            P(None, ("slab", "pencil"), None),
        ),
        out_specs=P(("slab", "pencil"), None),
        check_vma=False,
    )
```

```python
import jax
import jax.numpy as jnp
import ml_dtypes
import numpy as np
from jax import lax
from jax.experimental import pallas as pl
from jax.experimental.pallas import tpu as pltpu
from jax.sharding import PartitionSpec as P

NX, NY, NZ, BOX = 512, 512, 256, 64
GROUP = 64
UNROLL = 4
AHEAD = 2
F32, BF16 = jnp.float32, jnp.bfloat16


def halves(value):
    high = value.astype(BF16)
    return high, (value - high.astype(F32)).astype(BF16)


def lane_sums(value):
    ones = jnp.ones((128, 128), BF16)
    high, low = halves(value)
    return jnp.dot(high, ones, preferred_element_type=F32) + jnp.dot(low, ones, preferred_element_type=F32)


def row_of(x, tile, z):
    return (x * 4 + tile) * 48 + z


def window(anchors, slot):
    corner = row_of(anchors[0, slot] & 31, 0, (anchors[2, slot] & 31) + 6)
    y_at = (anchors[1, slot] + (NY - 2)) & (NY - 1)
    tile = y_at >> 7
    return corner + 48 * tile, corner + 48 * ((tile + 1) & 3), y_at & 127


def window_masks(lane_0):
    row = lax.broadcasted_iota(jnp.int32, (8, 128), 0)
    lane = lax.broadcasted_iota(jnp.int32, (8, 128), 1)
    shifted = (lane - row // 4 - lane_0) & 127
    return (shifted == 0, shifted == 2), lane >= lane_0, row < 4


def group_rows(step):
    return pl.ds(pl.multiple_of(step * GROUP, GROUP), GROUP)


def group_copy(step, source, target, sems):
    return pltpu.make_async_copy(source.at[group_rows(step)], target.at[group_rows(step)], sems.at[step])


def scatter_kernel(anchors, count, projection_at, charges, cells, projection, values, load):
    grid = cells.reshape(36 * 4 * 48, 128)
    for step in range(AHEAD):
        group_copy(step, projection_at, projection, load).start()

    def clear(x, carry):
        grid[pl.ds(pl.multiple_of(x * 192, 8), 192), :] = jnp.zeros((192, 128), F32)
        return carry

    lax.fori_loop(0, 36, clear, 0)

    def group(step, carry):
        @pl.when(step < charges.shape[0] // GROUP - AHEAD)
        def _():
            group_copy(step + AHEAD, projection_at, projection, load).start()

        group_copy(step, projection_at, projection, load).wait()
        rows = group_rows(step)
        slot = step * GROUP + lax.broadcasted_iota(jnp.int32, (GROUP, 128), 0)
        masked = jnp.where(slot < count[0], charges[rows, :], 0.0)
        products = projection[rows] * masked[:, None, :]
        values[...] = lane_sums(products.reshape(GROUP * BOX, 128)).reshape(GROUP, BOX, 128)

        def place(turn, carry):
            firsts, seconds, furthest = [], [], 0
            for u in range(UNROLL):
                b = turn * UNROLL + u
                row_0, row_1, lane_0 = window(anchors, step * GROUP + b)
                masks, beyond, top = window_masks(lane_0)
                here, there = beyond & top, top & ~beyond
                furthest = jnp.maximum(furthest, lane_0)
                for i in range(4):
                    patch = jnp.where(masks[0], values[b, 16 * i : 16 * i + 8], 0.0)
                    patch = jnp.where(masks[1], values[b, 16 * i + 8 : 16 * i + 16], patch)
                    patch = patch + pltpu.roll(patch, 4, 0)
                    firsts.append((row_0 + 192 * i, jnp.where(here, patch, 0.0)))
                    seconds.append((row_1 + 192 * i, there, patch))
            for row, patch in firsts:
                grid[pl.ds(row, 8), :] += patch

            @pl.when(furthest > 124)
            def _():
                for row, there, patch in seconds:
                    grid[pl.ds(row, 8), :] += jnp.where(there, patch, 0.0)

            return carry

        return lax.fori_loop(0, GROUP // UNROLL, place, carry)

    lax.fori_loop(0, charges.shape[0] // GROUP, group, 0)


def scatter(anchors, count, projection, charges):
    slots = charges.shape[0]
    smem, vmem = pl.BlockSpec(memory_space=pltpu.SMEM), pl.BlockSpec(memory_space=pltpu.VMEM)
    return pl.pallas_call(
        scatter_kernel,
        in_specs=[smem, smem, pl.BlockSpec(memory_space=pl.ANY), vmem],
        out_specs=pl.BlockSpec(memory_space=pltpu.VMEM),
        scratch_shapes=[
            pltpu.VMEM(projection.shape, F32),
            pltpu.VMEM((GROUP, BOX, 128), F32),
            pltpu.SemaphoreType.DMA((slots // GROUP,)),
        ],
        out_shape=pltpu.VMEM((36, 4, 48, 128), F32),
        compiler_params=pltpu.CompilerParams(vmem_limit_bytes=57 << 20),
    )(anchors, count, projection, charges)


CHUNKS = 4
MESH = pl.DeviceIdType.MESH


def phases(product, length):
    angle = 2.0 * np.pi * (product % length) / length
    return np.cos(angle), np.sin(angle)


def split_table(table):
    table = table.astype(np.float32)
    high = table.astype(ml_dtypes.bfloat16)
    return high, (table - high.astype(np.float32)).astype(ml_dtypes.bfloat16)


def y_tables():
    slab, part, pencil = np.meshgrid(np.arange(8), np.arange(2), np.arange(16), indexing="ij")
    device = (slab * 16 + pencil).reshape(-1, 1)
    part = part.reshape(-1, 1)
    even = np.where(device < 64, 4 * device, 4 * device + 2)
    odd = 4 * device + 1
    position = np.arange(256)[None, :]
    result = []
    for freq in (even, odd):
        cos, sin = phases(freq * position, NY)
        table = np.where(part == 0, cos, -sin)
        if freq is even:
            table[(device[:, 0] == 0) & (part[:, 0] == 1)] = 1.0 - 2.0 * (position[0] % 2)
        result.append(table)
    return np.stack(result)


def z_table():
    position = np.arange(NZ)
    cos, sin = phases(position[:, None] * position[None, :], NZ)
    return np.block([[cos, -sin], [sin, cos]])


def x_tables():
    position = np.arange(256)
    result = []
    for parity in range(2):
        cos, sin = phases((2 * position[:, None] + parity) * position[None, :], NX)
        result.append(np.concatenate([cos, sin], axis=1))
        if parity:
            result.append(np.concatenate([cos.T, sin.T], axis=1))
    return np.stack(result)


def dot_3(left, right, dims=((1,), (0,))):
    def one(a, b):
        return lax.dot_general(a, b, (dims, ((), ())), preferred_element_type=F32)

    return one(left[0], right[0]) + (one(left[0], right[1]) + one(left[1], right[0]))


def swap_groups(tiles):
    lane = lax.broadcasted_iota(jnp.int32, tiles[0].shape, 1)
    low, even = lane < 64, lane % 64 < 32
    firsts, lasts = [], []
    for a, b in ((tiles[0], tiles[2]), (tiles[1], tiles[3])):
        firsts.append(jnp.where(low, a, pltpu.roll(b, 64, 1)))
        lasts.append(jnp.where(low, pltpu.roll(a, 64, 1), b))
    result = []
    for a, b in (firsts, lasts):
        result.append(jnp.where(even, a, pltpu.roll(b, 32, 1)))
        result.append(jnp.where(even, pltpu.roll(a, 96, 1), b))
    return result


def field_kernel(
    anchors, count, pairs, charges, grid, projection_at, matrices_at, kernel_at, ty_at, tz_at, tx_at,
    result,
    projection, matrices, kernel, ty, tz, tx, sources, terms, near, values, out, mirror,
    charge, z_out, z_in, x_in, corner_in, sent_1, got_1, sent_2, got_2, level_out, level_in, spectra, back_2, took_2,
    back_1, took_1, lines, last_z_out, last_z_in, last_x_out, last_x_in, last_corner_in,
    load, group_load, level_send, level_recv, rim_send, rim_recv, last_send, last_recv, corner_recv,
    send_1, recv_1, send_2, recv_2, send_3, recv_3, send_4, recv_4,
):
    slab, pencil = lax.axis_index("slab"), lax.axis_index("pencil")
    n_slab, n_pencil = 8, 16

    def at(slab_step, pencil_step):
        return (lax.rem(slab + n_slab + slab_step, n_slab), lax.rem(pencil + n_pencil + pencil_step, n_pencil))

    def on_slab(step):
        return at(step, 0)

    def on_pencil(step):
        return at(0, step)

    def remote(source, target, send_sem, recv_sem, device):
        return pltpu.make_async_remote_copy(
            src_ref=source, dst_ref=target, send_sem=send_sem, recv_sem=recv_sem, device_id=device, device_id_type=MESH
        )

    def wait_recv(ref, sem):
        remote(ref, ref, sem, sem, on_slab(1)).wait_recv()

    def wait_send(ref, sem):
        remote(ref, ref, sem, sem, on_slab(1)).wait_send()

    barrier = pltpu.get_barrier_semaphore()

    def greet(device):
        pl.semaphore_signal(barrier, inc=1, device_id=device, device_id_type=MESH)

    def greet_slab(step, carry):
        greet(on_slab(step))
        return carry

    def greet_pencil(step, carry):
        greet(on_pencil(step))
        return carry

    sides = ((0, -1), (1, 1))
    lax.fori_loop(1, n_slab, greet_slab, 0)
    lax.fori_loop(1, n_pencil, greet_pencil, 0)
    for _, dz in sides:
        for _, dx in sides:
            greet(at(dz, dx))

    loads = [
        pltpu.make_async_copy(source, target, load.at[i])
        for i, (source, target) in enumerate(
            (
                (grid.at[2:34, :, 8:40, :], charge),
                (ty_at, ty),
                (tz_at, tz),
                (kernel_at, kernel),
                (tx_at, tx),
                (matrices_at, matrices),
            )
        )
    ]
    for copy in loads[:2]:
        copy.start()

    def pack_rims(x, carry):
        for tile in range(4):
            z_out[0, x, 2 * tile : 2 * tile + 2, :] = grid[x, tile, 6:8, :]
            z_out[1, x, 2 * tile : 2 * tile + 2, :] = grid[x, tile, 40:42, :]
        return carry

    lax.fori_loop(0, 36, pack_rims, 0, unroll=4)
    pl.semaphore_wait(barrier, n_slab + n_pencil + 2)
    ends = ((0, 2), (34, 36))
    rims = []
    for a, dz in sides:
        rims.append((z_out.at[a, 2:34], z_in.at[1 - a], on_slab(dz)))
    for b, dx in sides:
        rims.append((grid.at[ends[b][0] : ends[b][1], :, 8:40, :], x_in.at[1 - b], on_pencil(dx)))
    for a, dz in sides:
        for b, dx in sides:
            rims.append((z_out.at[a, ends[b][0] : ends[b][1]], corner_in.at[1 - a, 1 - b], at(dz, dx)))
    for i, (source, target, device) in enumerate(rims):
        remote(source, target, rim_send.at[i], rim_recv.at[i], device).start()
    for copy in loads[2:]:
        copy.start()

    loads[0].wait()
    wait_recv(z_in.at[1], rim_recv.at[0])
    wait_recv(z_in.at[0], rim_recv.at[1])

    def add_rims(x, carry):
        for tile in range(4):
            charge[x, tile, 0:2, :] += z_in[0, x, 2 * tile : 2 * tile + 2, :]
            charge[x, tile, 30:32, :] += z_in[1, x, 2 * tile : 2 * tile + 2, :]
        return carry

    lax.fori_loop(0, 32, add_rims, 0, unroll=4)
    loads[1].wait()

    def forward_y(step, carry):
        chunk = lax.rem(step + 1, CHUNKS)

        @pl.when(step == 2)
        def _():
            for i in range(2, 8):
                wait_recv(rims[i][1], rim_recv.at[i])
            for b, start in ((0, 0), (1, 30)):
                charge[start : start + 2] += x_in[b]
                for a, row in ((0, 0), (1, 30)):
                    for x in range(2):
                        for tile in range(4):
                            charge[start + x, tile, row : row + 2, :] += corner_in[a, b, x, 2 * tile : 2 * tile + 2, :]

        tiles = [charge[pl.ds(8 * chunk, 8), tile].reshape(256, 128) for tile in range(4)]
        for parity in range(2):
            if parity:
                halved = [tiles[0] - tiles[2], tiles[1] - tiles[3]]
            else:
                halved = [tiles[0] + tiles[2], tiles[1] + tiles[3]]
            columns = halves(jnp.concatenate(halved, axis=1))
            freqs = dot_3((ty[0, parity], ty[1, parity]), columns, ((1,), (1,)))
            sent_1[parity, chunk] = freqs.reshape(n_slab, 32, 256)
        return to_slabs(0, chunk)

    def to_slabs(parity, chunk):
        got_1[parity, chunk, slab] = sent_1[parity, chunk, slab]

        def send(k, carry):
            device = on_slab(k)
            remote(
                sent_1.at[parity, chunk, device[0]], got_1.at[parity, chunk, slab], send_1, recv_1.at[parity, chunk], device
            ).start()
            return carry

        return lax.fori_loop(1, n_slab, send, 0)

    lax.fori_loop(0, CHUNKS, forward_y, 0)
    lax.fori_loop(0, CHUNKS, lambda step, carry: to_slabs(1, lax.rem(step + 1, CHUNKS)), 0)
    for step in range(charges.shape[0] // GROUP):
        group_copy(step, projection_at, projection, group_load).start()

    slots, panels = charges.shape
    loads[3].wait()
    first = jnp.logical_and(slab == 0, pencil == 0)
    middle = jnp.logical_and(slab == 4, pencil == 0)

    @pl.when(middle)
    def _():
        for kx in range(2):
            for i in range(2):
                level_out[kx, :, 128 * i : 128 * i + 128] = kernel[pl.ds(8 * kx + 4 * i, 256, stride=16), :]
        remote(level_out, level_in, level_send, level_recv, (0, pencil)).start()

    slot = lax.broadcasted_iota(jnp.int32, (slots, panels), 0)
    coarse = jnp.where(slot < count[0], charges[...], 0.0).astype(BF16)
    slot = lax.broadcasted_iota(jnp.int32, (slots, slots), 0)
    chosen = jnp.where(slot == pairs[1:2, :], 1.0, 0.0)
    row = lax.broadcasted_iota(jnp.int32, (256, 256), 0)
    lane = lax.broadcasted_iota(jnp.int32, (256, 256), 1)
    mirror[...] = jnp.where((row + lane) & 255 == 0, 1.0, 0.0).astype(BF16)
    sources[...] = jnp.dot(chosen.T.astype(BF16), coarse, preferred_element_type=F32)
    loads[2].wait()
    loads[5].wait()

    def near_group(group, carry):
        rows = pl.ds(pl.multiple_of(8 * group, 8), 8)
        taken = sources[rows, :].astype(BF16)
        row = lax.broadcasted_iota(jnp.int32, (8, panels), 0)
        total = jnp.zeros((8, panels), F32)
        for i in range(8):
            found = lax.dot_general(
                taken, matrices[8 * group + i], (((1,), (1,)), ((), ())), preferred_element_type=F32
            )
            total = jnp.where(row == i, found, total)
        terms[rows, :] = total
        return carry

    near_groups = slots // 8 // (4 * CHUNKS)

    def near_share(turn):
        lax.fori_loop(turn * near_groups, (turn + 1) * near_groups, near_group, 0)

    def forward_z(turn, carry):
        parity, chunk = turn // CHUNKS, lax.rem(turn + 1, CHUNKS)
        near_share(turn)
        wait_recv(got_1.at[parity, chunk, 0 : n_slab - 1], recv_1.at[parity, chunk])
        for h in range(2):
            for q in range(2):
                tiles = swap_groups([got_1[parity, chunk, 4 * q + s, :, 128 * h : 128 * h + 128] for s in range(4)])
                for a in range(4):
                    for part in range(2):
                        lines[2 * part + q, pl.ds(4 * h + a, 16, stride=8), :] = tiles[a][16 * part : 16 * part + 16]
        rows = halves(jnp.concatenate([lines[i] for i in range(4)], axis=1))
        freqs = dot_3(rows, (tz[0], tz[1]))
        for part in range(2):
            sent_2[parity, chunk, :, part] = freqs[:, 256 * part : 256 * part + 256].reshape(n_pencil, 8, 256)
        mine = pl.ds(pl.multiple_of(pencil * 32 + chunk * 8, 8), 8)
        got_2[parity, :, mine, :] = sent_2[parity, chunk, pencil]

        def send(k, carry):
            device = on_pencil(k)
            remote(
                sent_2.at[parity, chunk, device[1]], got_2.at[parity, :, mine, :], send_2, recv_2.at[parity], device
            ).start()
            return carry

        return lax.fori_loop(1, n_pencil, send, carry)

    lax.fori_loop(0, 2 * CHUNKS - 2, forward_z, 0)

    loads[4].wait()
    unit = 1.0 / (NX * NY * NZ)

    def stacked(real, imag):
        return tuple(
            jnp.concatenate([jnp.concatenate([r, i], axis=1), jnp.concatenate([i, -r], axis=1)], axis=0)
            for r, i in zip(real, imag)
        )

    def mirrored(pieces):
        return tuple(jnp.dot(piece, mirror[...], preferred_element_type=F32).astype(BF16) for piece in pieces)

    def levels(start, unit):
        pieces = [kernel[pl.ds(start + 4 * i, 256, stride=16), :] for i in range(2)]
        return jnp.concatenate(pieces, axis=1) * unit

    def along_x(parity):
        wait_recv(got_2.at[parity, :, 0 : 32 * (n_pencil - 1), :], recv_2.at[parity])

        def found(kx, twin):
            parts = []
            for part in range(2):
                low, high = got_2[parity, part, 0:256, :], got_2[parity, part, 256:512, :]
                parts.append(halves(low - high if kx else low + high))
            right = stacked(*parts)
            if twin:
                real, imag = (mirrored(pieces) for pieces in parts)
                other = stacked(real, tuple(-piece for piece in imag))
                right = tuple(jnp.concatenate(both, axis=1) for both in zip(right, other))
            return dot_3((tx[0, kx], tx[1, kx]), right)

        def plain():
            own = 1 if parity else jnp.where(slab < 4, 0, 2)
            for kx in range(2):
                both, green = found(kx, False), levels(own + 8 * kx, 2.0 * unit)
                spectra[kx, 0] = both[:, 0:256] * green
                spectra[kx, 1] = both[:, 256:512] * green

        if parity:
            plain()
        else:
            pl.when(jnp.logical_not(first))(plain)

            @pl.when(first)
            def _():
                wait_recv(level_in, level_recv)
                for kx in range(2):
                    both, green, other = found(kx, True), levels(8 * kx, 0.5 * unit), level_in[kx] * (0.5 * unit)
                    mean, rest = green + other, green - other
                    for part in range(2):
                        one, two = (both[:, 256 * k : 256 * k + 256] for k in (part, part + 2))
                        spectra[kx, part] = mean * one + rest * two

        ends = []
        for kx in range(2):
            table = (tx[0, 2 * kx], tx[1, 2 * kx])
            real, imag = halves(spectra[kx, 0]), halves(spectra[kx, 1])
            right = tuple(
                jnp.concatenate([jnp.concatenate([r, i], axis=1), jnp.concatenate([-i, r], axis=1)], axis=0)
                for r, i in zip(real, imag)
            )
            ends.append(dot_3(table, right))
        for part in range(2):
            lanes = slice(256 * part, 256 * part + 256)
            back_2[parity, part, 0:256, :] = ends[0][:, lanes] + ends[1][:, lanes]
            back_2[parity, part, 256:512, :] = ends[0][:, lanes] - ends[1][:, lanes]

    def turns(step):
        return jnp.where(step < 2, 3 * step, step - 1)

    def return_x(turn, carry):
        parity, chunk = turn // CHUNKS, turns(lax.rem(turn, CHUNKS))
        own = pl.ds(pl.multiple_of(pencil * 32 + chunk * 8, 8), 8)
        took_2[parity, chunk, pencil] = back_2[parity, :, own, :]

        def send(k, carry):
            device = on_pencil(k)
            rows = pl.ds(pl.multiple_of(device[1] * 32 + chunk * 8, 8), 8)
            remote(
                back_2.at[parity, :, rows, :], took_2.at[parity, chunk, pencil], send_3, recv_3.at[parity, chunk], device
            ).start()
            return carry

        return lax.fori_loop(1, n_pencil, send, carry)

    def inverse_z(turn, carry):
        parity, chunk = turn // CHUNKS, turns(lax.rem(turn, CHUNKS))
        near_share(2 * CHUNKS + turn)
        wait_recv(took_2.at[parity, chunk, 0 : n_pencil - 1], recv_3.at[parity, chunk])
        rows = jnp.concatenate([took_2[parity, chunk, :, part].reshape(128, 256) for part in range(2)], axis=1)
        space = dot_3(halves(rows), (tz[0], tz[1]), ((1,), (1,)))
        for i in range(4):
            lines[i] = space[:, 128 * i : 128 * i + 128]
        for h in range(2):
            for q in range(2):
                tiles = []
                for a in range(4):
                    pieces = [lines[2 * part + q, pl.ds(4 * h + a, 16, stride=8), :] for part in range(2)]
                    tiles.append(jnp.concatenate(pieces, axis=0))
                for s, tile in enumerate(swap_groups(tiles)):
                    back_1[parity, chunk, 4 * q + s, :, 128 * h : 128 * h + 128] = tile
        took_1[parity, chunk, slab] = back_1[parity, chunk, slab]

        def send(k, carry):
            device = on_slab(k)
            remote(
                back_1.at[parity, chunk, device[0]], took_1.at[parity, chunk, slab], send_4, recv_4.at[parity, chunk], device
            ).start()
            return carry

        return lax.fori_loop(1, n_slab, send, carry)

    along_x(0)
    lax.fori_loop(0, 1, return_x, 0)
    lax.fori_loop(1, 3, lambda turn, carry: return_x(turn, forward_z(turn + 5, carry)), 0)
    lax.fori_loop(3, 4, return_x, 0)
    lax.fori_loop(0, 2, inverse_z, 0)
    along_x(1)
    lax.fori_loop(4, 8, return_x, 0)
    lax.fori_loop(2, 8, inverse_z, 0)

    row_starts = (2, 32)
    last = []
    for b, dx in sides:
        last.append((last_x_out.at[b], last_x_in.at[1 - b], on_pencil(dx)))
        for a, dz in sides:
            rows = (0, 2) if b == 0 else (6, 8)
            last.append(
                (last_z_out.at[3 * b, a, rows[0] : rows[1]], last_corner_in.at[1 - b, 1 - a], at(dz, dx))
            )

    def planes(chunk, a):
        return (last_z_out.at[chunk, a], last_z_in.at[chunk, 1 - a], last_send.at[6 + a], last_recv.at[chunk, 1 - a])

    def take_planes(step, carry):
        chunk = turns(step)
        for a, row in ((0, 6), (1, 40)):
            wait_recv(last_z_in.at[chunk, a], last_recv.at[chunk, a])
            for x in range(8):
                for tile in range(4):
                    out[pl.ds(row_of(2 + 8 * chunk + x, tile, row), 2), :] = last_z_in[chunk, a, x, 2 * tile : 2 * tile + 2, :]
        return carry

    def inverse_y(step, carry):
        chunk = turns(step)
        ends = []
        for parity in range(2):
            wait_recv(took_1.at[parity, chunk, 0 : n_slab - 1], recv_4.at[parity, chunk])
            columns = took_1[parity, chunk].reshape(256, 256).T
            ends.append(dot_3(halves(columns), (ty[0, parity], ty[1, parity])))
        space = (ends[0] + ends[1], ends[0] - ends[1])
        for tile in range(4):
            lanes = slice(128 * (tile % 2), 128 * (tile % 2) + 128)
            cells = space[tile // 2][:, lanes].reshape(8, 32, 128)
            for x in range(8):
                out[pl.ds(pl.multiple_of(row_of(2 + 8 * chunk + x, tile, 8), 8), 32), :] = cells[x]
            last_z_out[chunk, 0, :, 2 * tile : 2 * tile + 2, :] = cells[:, 0:2, :]
            last_z_out[chunk, 1, :, 2 * tile : 2 * tile + 2, :] = cells[:, 30:32, :]
        for a, dz in sides:
            remote(*planes(chunk, a), on_slab(dz)).start()
        for b in range(2):

            @pl.when(chunk == 3 * b)
            def _():
                for x in range(2):
                    for tile in range(4):
                        last_x_out[b, x, tile] = out[pl.ds(row_of(row_starts[b] + x, tile, 8), 32), :]
                for i in range(3 * b, 3 * b + 3):
                    source, target, device = last[i]
                    remote(source, target, last_send.at[i], corner_recv.at[i], device).start()

        return carry

    lax.fori_loop(0, CHUNKS, inverse_y, 0)

    slot = lax.broadcasted_iota(jnp.int32, (slots, slots), 0)
    chosen = jnp.where(slot == pairs[0:1, :], 1.0, 0.0).astype(BF16)
    rest = terms[...]
    total = jnp.zeros(near.shape, F32)
    for _ in range(3):
        part = rest.astype(BF16)
        rest = rest - part.astype(F32)
        total = total + jnp.dot(chosen, part, preferred_element_type=F32)
    near[...] = total

    lax.fori_loop(0, CHUNKS - 1, take_planes, 0)
    for i, (source, target, device) in enumerate(last):
        wait_recv(target, corner_recv.at[i])
        wait_send(source, last_send.at[i])
    for b, start in ((0, 0), (1, 34)):
        for x in range(2):
            for tile in range(4):
                out[pl.ds(row_of(start + x, tile, 8), 32), :] = last_x_in[b, x, tile]
                for a, row in ((0, 6), (1, 40)):
                    out[pl.ds(row_of(start + x, tile, row), 2), :] = last_corner_in[b, a, x, 2 * tile : 2 * tile + 2, :]
    for i, (source, target, device) in enumerate(rims):
        wait_send(source, rim_send.at[i])
    wait_send(sent_1.at[:, :, 0 : n_slab - 1], send_1)
    wait_send(got_2.at[:, :, 0 : 32 * (n_pencil - 1), :], send_2)
    wait_send(got_2.at[:, :, 0 : 32 * (n_pencil - 1), :], send_3)
    wait_send(back_1.at[:, :, 0 : n_slab - 1], send_4)

    @pl.when(middle)
    def _():
        wait_send(level_out, level_send)

    take_planes(CHUNKS - 1, 0)
    for a in range(2):
        wait_send(last_z_out.at[:, a], last_send.at[6 + a])

    def gather_group(step, carry):
        def pick(turn, carry):
            for u in range(UNROLL):
                b = turn * UNROLL + u
                row_0, row_1, lane_0 = window(anchors, step * GROUP + b)
                masks, beyond, top = window_masks(lane_0)
                for i in range(4):
                    cells = jnp.where(beyond, out[pl.ds(row_0 + 192 * i, 8), :], out[pl.ds(row_1 + 192 * i, 8), :])
                    cells = jnp.where(top, cells, pltpu.roll(cells, 4, 0))
                    for j in range(2):
                        values[b, 16 * i + 8 * j : 16 * i + 8 * j + 8] = jnp.where(masks[j], cells, 0.0)
            return carry

        lax.fori_loop(0, GROUP // UNROLL, pick, 0)
        group_copy(step, projection_at, projection, group_load).wait()
        rows = group_rows(step)
        box = lane_sums(values[...].reshape(GROUP * BOX, 128)).reshape(GROUP, BOX, 128)
        far = jnp.sum(projection[rows] * box, axis=1)
        result[rows, :] = far + near[rows, :]
        return carry

    lax.fori_loop(0, slots // GROUP, gather_group, 0)


def field(anchors, count, pairs, charges, grid, projection, matrices, kernel):
    tables = [jnp.asarray(np.stack(split_table(table))) for table in (y_tables(), z_table(), x_tables())]
    slots, panels = charges.shape
    dma = pltpu.SemaphoreType.DMA
    vmem = pltpu.VMEM
    return pl.pallas_call(
        field_kernel,
        in_specs=[
            *[pl.BlockSpec(memory_space=pltpu.SMEM)] * 2,
            *[pl.BlockSpec(memory_space=vmem)] * 3,
            *[pl.BlockSpec(memory_space=pl.ANY)] * 6,
        ],
        out_specs=pl.BlockSpec(memory_space=vmem),
        out_shape=pltpu.VMEM((slots, panels), F32),
        scratch_shapes=[
            vmem(projection.shape, F32),
            vmem(matrices.shape, BF16),
            vmem(kernel.shape, F32),
            *(vmem(table.shape, BF16) for table in tables),
            vmem((slots, panels), F32),
            vmem((slots, panels), F32),
            vmem((slots, panels), F32),
            vmem((GROUP, BOX, panels), F32),
            vmem((36 * 4 * 48, 128), F32),
            vmem((256, 256), BF16),
            vmem((32, 4, 32, 128), F32),
            vmem((2, 36, 8, 128), F32),
            vmem((2, 32, 8, 128), F32),
            vmem((2, 2, 4, 32, 128), F32),
            vmem((2, 2, 2, 8, 128), F32),
            vmem((2, CHUNKS, 8, 32, 256), F32),
            vmem((2, CHUNKS, 8, 32, 256), F32),
            vmem((2, CHUNKS, 16, 2, 8, 256), F32),
            vmem((2, 2, 512, 256), F32),
            vmem((2, 256, 256), F32),
            vmem((2, 256, 256), F32),
            vmem((2, 2, 256, 256), F32),
            vmem((2, 2, 512, 256), F32),
            vmem((2, CHUNKS, 16, 2, 8, 256), F32),
            vmem((2, CHUNKS, 8, 32, 256), F32),
            vmem((2, CHUNKS, 8, 32, 256), F32),
            vmem((4, 128, 128), F32),
            vmem((CHUNKS, 2, 8, 8, 128), F32),
            vmem((CHUNKS, 2, 8, 8, 128), F32),
            vmem((2, 2, 4, 32, 128), F32),
            vmem((2, 2, 4, 32, 128), F32),
            vmem((2, 2, 2, 8, 128), F32),
            dma((6,)),
            dma((slots // GROUP,)),
            dma,
            dma,
            dma((8,)),
            dma((8,)),
            dma((8,)),
            dma((CHUNKS, 2)),
            dma((6,)),
            dma,
            dma((2, CHUNKS)),
            dma,
            dma((2,)),
            dma,
            dma((2, CHUNKS)),
            dma,
            dma((2, CHUNKS)),
        ],
        compiler_params=pltpu.CompilerParams(
            collective_id=0, has_side_effects=True, vmem_limit_bytes=57 << 20
        ),
        cost_estimate=pl.CostEstimate(flops=10**10, bytes_accessed=10**7, transcendentals=0),
    )(anchors, count, pairs, charges, grid, projection, matrices, kernel, *tables)


def shards(charges, projection, anchors, block_count, near_pairs, near_matrices, kernel_hat):
    grid = pltpu.with_memory_space_constraint(scatter(anchors.T, block_count, projection, charges), pltpu.VMEM)
    levels = jnp.transpose(kernel_hat.reshape(NX, 4, 2, 128), (0, 2, 1, 3)).reshape(NX * 8, 128)
    total = field(anchors.T, block_count, near_pairs.T, charges, grid, projection, near_matrices, levels)
    in_use = lax.broadcasted_iota(jnp.int32, total.shape, 0) < block_count[0]
    return jnp.where(in_use, total, 0.0)


def solution(mesh):
    return jax.shard_map(
        shards,
        mesh=mesh,
        in_specs=(
            P(("slab", "pencil"), None),
            P(("slab", "pencil"), None, None),
            P(("slab", "pencil"), None),
            P(("slab", "pencil")),
            P(("slab", "pencil"), None),
            P(("slab", "pencil"), None, None),
            P(None, ("slab", "pencil"), None),
        ),
        out_specs=P(("slab", "pencil"), None),
        check_vma=False,
    )
```

```python
import jax
import jax.numpy as jnp
import ml_dtypes
import numpy as np
from jax import lax
from jax.experimental import pallas as pl
from jax.experimental.pallas import tpu as pltpu
from jax.sharding import PartitionSpec as P

NX, NY, NZ, BOX = 512, 512, 256, 64
GROUP = 64
UNROLL = 4
AHEAD = 2
F32, BF16 = jnp.float32, jnp.bfloat16


def halves(value):
    high = value.astype(BF16)
    return high, (value - high.astype(F32)).astype(BF16)


def lane_sums(value):
    ones = jnp.ones((128, 128), BF16)
    high, low = halves(value)
    return jnp.dot(high, ones, preferred_element_type=F32) + jnp.dot(low, ones, preferred_element_type=F32)


def row_of(x, tile, z):
    return (x * 4 + tile) * 48 + z


def window(anchors, slot):
    corner = row_of(anchors[0, slot] & 31, 0, (anchors[2, slot] & 31) + 6)
    y_at = (anchors[1, slot] + (NY - 2)) & (NY - 1)
    tile = y_at >> 7
    return corner + 48 * tile, corner + 48 * ((tile + 1) & 3), y_at & 127


def window_masks(lane_0):
    row = lax.broadcasted_iota(jnp.int32, (8, 128), 0)
    lane = lax.broadcasted_iota(jnp.int32, (8, 128), 1)
    shifted = (lane - row // 4 - lane_0) & 127
    return (shifted == 0, shifted == 2), lane >= lane_0, row < 4


def group_rows(step):
    return pl.ds(pl.multiple_of(step * GROUP, GROUP), GROUP)


def group_copy(step, source, target, sems):
    return pltpu.make_async_copy(source.at[group_rows(step)], target.at[group_rows(step)], sems.at[step])


def scatter_kernel(anchors, count, projection_at, charges, cells, projection, values, load):
    grid = cells.reshape(36 * 4 * 48, 128)
    for step in range(AHEAD):
        group_copy(step, projection_at, projection, load).start()

    def clear(x, carry):
        grid[pl.ds(pl.multiple_of(x * 192, 8), 192), :] = jnp.zeros((192, 128), F32)
        return carry

    lax.fori_loop(0, 36, clear, 0)

    def group(step, carry):
        @pl.when(step < charges.shape[0] // GROUP - AHEAD)
        def _():
            group_copy(step + AHEAD, projection_at, projection, load).start()

        group_copy(step, projection_at, projection, load).wait()
        rows = group_rows(step)
        slot = step * GROUP + lax.broadcasted_iota(jnp.int32, (GROUP, 128), 0)
        masked = jnp.where(slot < count[0], charges[rows, :], 0.0)
        products = projection[rows] * masked[:, None, :]
        values[...] = lane_sums(products.reshape(GROUP * BOX, 128)).reshape(GROUP, BOX, 128)

        def place(turn, carry):
            firsts, seconds, furthest = [], [], 0
            for u in range(UNROLL):
                b = turn * UNROLL + u
                row_0, row_1, lane_0 = window(anchors, step * GROUP + b)
                masks, beyond, top = window_masks(lane_0)
                here, there = beyond & top, top & ~beyond
                furthest = jnp.maximum(furthest, lane_0)
                for i in range(4):
                    patch = jnp.where(masks[0], values[b, 16 * i : 16 * i + 8], 0.0)
                    patch = jnp.where(masks[1], values[b, 16 * i + 8 : 16 * i + 16], patch)
                    patch = patch + pltpu.roll(patch, 4, 0)
                    firsts.append((row_0 + 192 * i, jnp.where(here, patch, 0.0)))
                    seconds.append((row_1 + 192 * i, there, patch))
            for row, patch in firsts:
                grid[pl.ds(row, 8), :] += patch

            @pl.when(furthest > 124)
            def _():
                for row, there, patch in seconds:
                    grid[pl.ds(row, 8), :] += jnp.where(there, patch, 0.0)

            return carry

        return lax.fori_loop(0, GROUP // UNROLL, place, carry)

    lax.fori_loop(0, charges.shape[0] // GROUP, group, 0)


def scatter(anchors, count, projection, charges):
    slots = charges.shape[0]
    smem, vmem = pl.BlockSpec(memory_space=pltpu.SMEM), pl.BlockSpec(memory_space=pltpu.VMEM)
    return pl.pallas_call(
        scatter_kernel,
        in_specs=[smem, smem, pl.BlockSpec(memory_space=pl.ANY), vmem],
        out_specs=pl.BlockSpec(memory_space=pltpu.VMEM),
        scratch_shapes=[
            pltpu.VMEM(projection.shape, F32),
            pltpu.VMEM((GROUP, BOX, 128), F32),
            pltpu.SemaphoreType.DMA((slots // GROUP,)),
        ],
        out_shape=pltpu.VMEM((36, 4, 48, 128), F32),
        compiler_params=pltpu.CompilerParams(vmem_limit_bytes=57 << 20),
    )(anchors, count, projection, charges)


CHUNKS = 4
MESH = pl.DeviceIdType.MESH


def phases(product, length):
    angle = 2.0 * np.pi * (product % length) / length
    return np.cos(angle), np.sin(angle)


def split_table(table):
    table = table.astype(np.float32)
    high = table.astype(ml_dtypes.bfloat16)
    return high, (table - high.astype(np.float32)).astype(ml_dtypes.bfloat16)


def y_tables():
    slab, part, pencil = np.meshgrid(np.arange(8), np.arange(2), np.arange(16), indexing="ij")
    device = (slab * 16 + pencil).reshape(-1, 1)
    part = part.reshape(-1, 1)
    even = np.where(device < 64, 4 * device, 4 * device + 2)
    odd = 4 * device + 1
    position = np.arange(256)[None, :]
    result = []
    for freq in (even, odd):
        cos, sin = phases(freq * position, NY)
        table = np.where(part == 0, cos, -sin)
        if freq is even:
            table[(device[:, 0] == 0) & (part[:, 0] == 1)] = 1.0 - 2.0 * (position[0] % 2)
        result.append(table)
    return np.stack(result)


def z_table():
    position = np.arange(NZ)
    cos, sin = phases(position[:, None] * position[None, :], NZ)
    return np.block([[cos, -sin], [sin, cos]])


def x_tables():
    position = np.arange(256)
    result = []
    for parity in range(2):
        cos, sin = phases((2 * position[:, None] + parity) * position[None, :], NX)
        result.append(np.concatenate([cos, sin], axis=1))
        if parity:
            result.append(np.concatenate([cos.T, sin.T], axis=1))
    return np.stack(result)


def dot_3(left, right, dims=((1,), (0,))):
    def one(a, b):
        return lax.dot_general(a, b, (dims, ((), ())), preferred_element_type=F32)

    return one(left[0], right[0]) + (one(left[0], right[1]) + one(left[1], right[0]))


def swap_groups(tiles):
    lane = lax.broadcasted_iota(jnp.int32, tiles[0].shape, 1)
    low, even = lane < 64, lane % 64 < 32
    firsts, lasts = [], []
    for a, b in ((tiles[0], tiles[2]), (tiles[1], tiles[3])):
        firsts.append(jnp.where(low, a, pltpu.roll(b, 64, 1)))
        lasts.append(jnp.where(low, pltpu.roll(a, 64, 1), b))
    result = []
    for a, b in (firsts, lasts):
        result.append(jnp.where(even, a, pltpu.roll(b, 32, 1)))
        result.append(jnp.where(even, pltpu.roll(a, 96, 1), b))
    return result


def field_kernel(
    anchors, count, pairs, charges, grid, projection_at, matrices_at, kernel_at, ty_at, tz_at, tx_at,
    result,
    projection, matrices, kernel, ty, tz, tx, sources, terms, near, values, out, mirror,
    charge, z_out, z_in, x_in, corner_in, sent_1, got_1, sent_2, got_2, level_out, level_in, spectra, back_2, took_2,
    back_1, took_1, lines, last_z_out, last_z_in, last_x_out, last_x_in, last_corner_in,
    load, group_load, level_send, level_recv, rim_send, rim_recv, last_send, last_recv, corner_recv,
    send_1, recv_1, send_2, recv_2, send_3, recv_3, send_4, recv_4,
):
    slab, pencil = lax.axis_index("slab"), lax.axis_index("pencil")
    n_slab, n_pencil = 8, 16

    def at(slab_step, pencil_step):
        return (lax.rem(slab + n_slab + slab_step, n_slab), lax.rem(pencil + n_pencil + pencil_step, n_pencil))

    def on_slab(step):
        return at(step, 0)

    def on_pencil(step):
        return at(0, step)

    def remote(source, target, send_sem, recv_sem, device):
        return pltpu.make_async_remote_copy(
            src_ref=source, dst_ref=target, send_sem=send_sem, recv_sem=recv_sem, device_id=device, device_id_type=MESH
        )

    def wait_recv(ref, sem):
        remote(ref, ref, sem, sem, on_slab(1)).wait_recv()

    def wait_send(ref, sem):
        remote(ref, ref, sem, sem, on_slab(1)).wait_send()

    barrier = pltpu.get_barrier_semaphore()

    def greet(device):
        pl.semaphore_signal(barrier, inc=1, device_id=device, device_id_type=MESH)

    def greet_slab(step, carry):
        greet(on_slab(step))
        return carry

    def greet_pencil(step, carry):
        greet(on_pencil(step))
        return carry

    sides = ((0, -1), (1, 1))
    lax.fori_loop(1, n_slab, greet_slab, 0)
    lax.fori_loop(1, n_pencil, greet_pencil, 0)
    for _, dz in sides:
        for _, dx in sides:
            greet(at(dz, dx))

    loads = [
        pltpu.make_async_copy(source, target, load.at[i])
        for i, (source, target) in enumerate(
            (
                (grid.at[2:34, :, 8:40, :], charge),
                (kernel_at, kernel),
                (ty_at, ty),
                (tz_at, tz),
                (tx_at, tx),
                (matrices_at, matrices),
            )
        )
    ]
    for copy in loads[:3]:
        copy.start()

    def pack_rims(x, carry):
        for tile in range(4):
            z_out[0, x, 2 * tile : 2 * tile + 2, :] = grid[x, tile, 6:8, :]
            z_out[1, x, 2 * tile : 2 * tile + 2, :] = grid[x, tile, 40:42, :]
        return carry

    lax.fori_loop(0, 36, pack_rims, 0, unroll=4)
    pl.semaphore_wait(barrier, n_slab + n_pencil + 2)
    ends = ((0, 2), (34, 36))
    rims = []
    for a, dz in sides:
        rims.append((z_out.at[a, 2:34], z_in.at[1 - a], on_slab(dz)))
    for b, dx in sides:
        rims.append((grid.at[ends[b][0] : ends[b][1], :, 8:40, :], x_in.at[1 - b], on_pencil(dx)))
    for a, dz in sides:
        for b, dx in sides:
            rims.append((z_out.at[a, ends[b][0] : ends[b][1]], corner_in.at[1 - a, 1 - b], at(dz, dx)))
    for i, (source, target, device) in enumerate(rims):
        remote(source, target, rim_send.at[i], rim_recv.at[i], device).start()
    first = jnp.logical_and(slab == 0, pencil == 0)
    middle = jnp.logical_and(slab == 4, pencil == 0)
    loads[1].wait()

    @pl.when(middle)
    def _():
        for kx in range(2):
            for i in range(2):
                level_out[kx, :, 128 * i : 128 * i + 128] = kernel[pl.ds(8 * kx + 4 * i, 256, stride=16), :]
        remote(level_out, level_in, level_send, level_recv, (0, pencil)).start()

    for copy in loads[3:]:
        copy.start()

    loads[0].wait()
    wait_recv(z_in.at[1], rim_recv.at[0])
    wait_recv(z_in.at[0], rim_recv.at[1])

    def add_rims(x, carry):
        for tile in range(4):
            charge[x, tile, 0:2, :] += z_in[0, x, 2 * tile : 2 * tile + 2, :]
            charge[x, tile, 30:32, :] += z_in[1, x, 2 * tile : 2 * tile + 2, :]
        return carry

    lax.fori_loop(0, 32, add_rims, 0, unroll=4)
    loads[2].wait()

    def forward_y(step, carry):
        chunk = lax.rem(step + 1, CHUNKS)

        @pl.when(step == 2)
        def _():
            for i in range(2, 8):
                wait_recv(rims[i][1], rim_recv.at[i])
            for b, start in ((0, 0), (1, 30)):
                charge[start : start + 2] += x_in[b]
                for a, row in ((0, 0), (1, 30)):
                    for x in range(2):
                        for tile in range(4):
                            charge[start + x, tile, row : row + 2, :] += corner_in[a, b, x, 2 * tile : 2 * tile + 2, :]

        tiles = [charge[pl.ds(8 * chunk, 8), tile].reshape(256, 128) for tile in range(4)]
        for parity in range(2):
            if parity:
                halved = [tiles[0] - tiles[2], tiles[1] - tiles[3]]
            else:
                halved = [tiles[0] + tiles[2], tiles[1] + tiles[3]]
            columns = halves(jnp.concatenate(halved, axis=1))
            freqs = dot_3((ty[0, parity], ty[1, parity]), columns, ((1,), (1,)))
            sent_1[parity, chunk] = freqs.reshape(n_slab, 32, 256)
            if not parity:
                to_slabs(0, chunk)
        return carry

    def to_slabs(parity, chunk):
        got_1[parity, chunk, slab] = sent_1[parity, chunk, slab]

        def send(k, carry):
            device = on_slab(k)
            remote(
                sent_1.at[parity, chunk, device[0]], got_1.at[parity, chunk, slab], send_1, recv_1.at[parity, chunk], device
            ).start()
            return carry

        return lax.fori_loop(1, n_slab, send, 0)

    lax.fori_loop(0, CHUNKS, forward_y, 0)
    lax.fori_loop(0, CHUNKS, lambda step, carry: to_slabs(1, lax.rem(step + 1, CHUNKS)), 0)
    for step in range(charges.shape[0] // GROUP):
        group_copy(step, projection_at, projection, group_load).start()

    slots, panels = charges.shape
    slot = lax.broadcasted_iota(jnp.int32, (slots, panels), 0)
    coarse = jnp.where(slot < count[0], charges[...], 0.0).astype(BF16)
    slot = lax.broadcasted_iota(jnp.int32, (slots, slots), 0)
    chosen = jnp.where(slot == pairs[1:2, :], 1.0, 0.0)
    row = lax.broadcasted_iota(jnp.int32, (256, 256), 0)
    lane = lax.broadcasted_iota(jnp.int32, (256, 256), 1)
    mirror[...] = jnp.where((row + lane) & 255 == 0, 1.0, 0.0).astype(BF16)
    sources[...] = jnp.dot(chosen.T.astype(BF16), coarse, preferred_element_type=F32)
    loads[3].wait()
    loads[5].wait()

    def near_group(group, carry):
        rows = pl.ds(pl.multiple_of(8 * group, 8), 8)
        taken = sources[rows, :].astype(BF16)
        row = lax.broadcasted_iota(jnp.int32, (8, panels), 0)
        total = jnp.zeros((8, panels), F32)
        for i in range(8):
            found = lax.dot_general(
                taken, matrices[8 * group + i], (((1,), (1,)), ((), ())), preferred_element_type=F32
            )
            total = jnp.where(row == i, found, total)
        terms[rows, :] = total
        return carry

    near_groups = slots // 8 // (4 * CHUNKS)

    def near_share(turn):
        lax.fori_loop(turn * near_groups, (turn + 1) * near_groups, near_group, 0)

    def forward_z(turn, carry):
        parity, chunk = turn // CHUNKS, lax.rem(turn + 1, CHUNKS)
        near_share(turn)
        wait_recv(got_1.at[parity, chunk, 0 : n_slab - 1], recv_1.at[parity, chunk])
        for h in range(2):
            for q in range(2):
                tiles = swap_groups([got_1[parity, chunk, 4 * q + s, :, 128 * h : 128 * h + 128] for s in range(4)])
                for a in range(4):
                    for part in range(2):
                        lines[2 * part + q, pl.ds(4 * h + a, 16, stride=8), :] = tiles[a][16 * part : 16 * part + 16]
        rows = halves(jnp.concatenate([lines[i] for i in range(4)], axis=1))
        freqs = dot_3(rows, (tz[0], tz[1]))
        for part in range(2):
            sent_2[parity, chunk, :, part] = freqs[:, 256 * part : 256 * part + 256].reshape(n_pencil, 8, 256)
        mine = pl.ds(pl.multiple_of(pencil * 32 + chunk * 8, 8), 8)
        got_2[parity, :, mine, :] = sent_2[parity, chunk, pencil]

        def send(k, carry):
            device = on_pencil(k)
            remote(
                sent_2.at[parity, chunk, device[1]], got_2.at[parity, :, mine, :], send_2, recv_2.at[parity], device
            ).start()
            return carry

        return lax.fori_loop(1, n_pencil, send, carry)

    lax.fori_loop(0, 2 * CHUNKS - 2, forward_z, 0)

    loads[4].wait()
    unit = 1.0 / (NX * NY * NZ)

    def stacked(real, imag):
        return tuple(
            jnp.concatenate([jnp.concatenate([r, i], axis=1), jnp.concatenate([i, -r], axis=1)], axis=0)
            for r, i in zip(real, imag)
        )

    def mirrored(pieces):
        return tuple(jnp.dot(piece, mirror[...], preferred_element_type=F32).astype(BF16) for piece in pieces)

    def levels(start, unit):
        pieces = [kernel[pl.ds(start + 4 * i, 256, stride=16), :] for i in range(2)]
        return jnp.concatenate(pieces, axis=1) * unit

    def along_x(parity):
        wait_recv(got_2.at[parity, :, 0 : 32 * (n_pencil - 1), :], recv_2.at[parity])

        def found(kx, twin):
            parts = []
            for part in range(2):
                low, high = got_2[parity, part, 0:256, :], got_2[parity, part, 256:512, :]
                parts.append(halves(low - high if kx else low + high))
            right = stacked(*parts)
            if twin:
                real, imag = (mirrored(pieces) for pieces in parts)
                other = stacked(real, tuple(-piece for piece in imag))
                right = tuple(jnp.concatenate(both, axis=1) for both in zip(right, other))
            return dot_3((tx[0, kx], tx[1, kx]), right)

        def plain():
            own = 1 if parity else jnp.where(slab < 4, 0, 2)
            for kx in range(2):
                both, green = found(kx, False), levels(own + 8 * kx, 2.0 * unit)
                spectra[kx, 0] = both[:, 0:256] * green
                spectra[kx, 1] = both[:, 256:512] * green

        if parity:
            plain()
        else:
            pl.when(jnp.logical_not(first))(plain)

            @pl.when(first)
            def _():
                wait_recv(level_in, level_recv)
                for kx in range(2):
                    both, green, other = found(kx, True), levels(8 * kx, 0.5 * unit), level_in[kx] * (0.5 * unit)
                    mean, rest = green + other, green - other
                    for part in range(2):
                        one, two = (both[:, 256 * k : 256 * k + 256] for k in (part, part + 2))
                        spectra[kx, part] = mean * one + rest * two

        ends = []
        for kx in range(2):
            table = (tx[0, 2 * kx], tx[1, 2 * kx])
            real, imag = halves(spectra[kx, 0]), halves(spectra[kx, 1])
            right = tuple(
                jnp.concatenate([jnp.concatenate([r, i], axis=1), jnp.concatenate([-i, r], axis=1)], axis=0)
                for r, i in zip(real, imag)
            )
            ends.append(dot_3(table, right))
        for part in range(2):
            lanes = slice(256 * part, 256 * part + 256)
            back_2[parity, part, 0:256, :] = ends[0][:, lanes] + ends[1][:, lanes]
            back_2[parity, part, 256:512, :] = ends[0][:, lanes] - ends[1][:, lanes]

    def turns(step):
        return jnp.where(step < 2, 3 * step, step - 1)

    def return_x(turn, carry):
        parity, chunk = turn // CHUNKS, turns(lax.rem(turn, CHUNKS))
        own = pl.ds(pl.multiple_of(pencil * 32 + chunk * 8, 8), 8)
        took_2[parity, chunk, pencil] = back_2[parity, :, own, :]

        def send(k, carry):
            device = on_pencil(k)
            rows = pl.ds(pl.multiple_of(device[1] * 32 + chunk * 8, 8), 8)
            remote(
                back_2.at[parity, :, rows, :], took_2.at[parity, chunk, pencil], send_3, recv_3.at[parity, chunk], device
            ).start()
            return carry

        return lax.fori_loop(1, n_pencil, send, carry)

    def inverse_z(turn, carry):
        parity, chunk = turn // CHUNKS, turns(lax.rem(turn, CHUNKS))
        near_share(2 * CHUNKS + turn)
        wait_recv(took_2.at[parity, chunk, 0 : n_pencil - 1], recv_3.at[parity, chunk])
        rows = jnp.concatenate([took_2[parity, chunk, :, part].reshape(128, 256) for part in range(2)], axis=1)
        space = dot_3(halves(rows), (tz[0], tz[1]), ((1,), (1,)))
        for i in range(4):
            lines[i] = space[:, 128 * i : 128 * i + 128]
        for h in range(2):
            for q in range(2):
                tiles = []
                for a in range(4):
                    pieces = [lines[2 * part + q, pl.ds(4 * h + a, 16, stride=8), :] for part in range(2)]
                    tiles.append(jnp.concatenate(pieces, axis=0))
                for s, tile in enumerate(swap_groups(tiles)):
                    back_1[parity, chunk, 4 * q + s, :, 128 * h : 128 * h + 128] = tile
        took_1[parity, chunk, slab] = back_1[parity, chunk, slab]

        def send(k, carry):
            device = on_slab(k)
            remote(
                back_1.at[parity, chunk, device[0]], took_1.at[parity, chunk, slab], send_4, recv_4.at[parity, chunk], device
            ).start()
            return carry

        return lax.fori_loop(1, n_slab, send, carry)

    along_x(0)
    lax.fori_loop(0, 1, return_x, 0)
    lax.fori_loop(1, 3, lambda turn, carry: return_x(turn, forward_z(turn + 5, carry)), 0)
    lax.fori_loop(3, 4, return_x, 0)
    lax.fori_loop(0, 2, inverse_z, 0)
    along_x(1)
    lax.fori_loop(4, 8, return_x, 0)
    lax.fori_loop(2, 8, inverse_z, 0)

    row_starts = (2, 32)
    last = []
    for b, dx in sides:
        last.append((last_x_out.at[b], last_x_in.at[1 - b], on_pencil(dx)))
        for a, dz in sides:
            rows = (0, 2) if b == 0 else (6, 8)
            last.append(
                (last_z_out.at[3 * b, a, rows[0] : rows[1]], last_corner_in.at[1 - b, 1 - a], at(dz, dx))
            )

    def planes(chunk, a):
        return (last_z_out.at[chunk, a], last_z_in.at[chunk, 1 - a], last_send.at[6 + a], last_recv.at[chunk, 1 - a])

    def take_planes(step, carry):
        chunk = turns(step)
        for a, row in ((0, 6), (1, 40)):
            wait_recv(last_z_in.at[chunk, a], last_recv.at[chunk, a])
            for x in range(8):
                for tile in range(4):
                    out[pl.ds(row_of(2 + 8 * chunk + x, tile, row), 2), :] = last_z_in[chunk, a, x, 2 * tile : 2 * tile + 2, :]
        return carry

    def inverse_y(step, carry):
        chunk = turns(step)
        ends = []
        for parity in range(2):
            wait_recv(took_1.at[parity, chunk, 0 : n_slab - 1], recv_4.at[parity, chunk])
            columns = took_1[parity, chunk].reshape(256, 256).T
            ends.append(dot_3(halves(columns), (ty[0, parity], ty[1, parity])))
        space = (ends[0] + ends[1], ends[0] - ends[1])
        for tile in range(4):
            lanes = slice(128 * (tile % 2), 128 * (tile % 2) + 128)
            cells = space[tile // 2][:, lanes].reshape(8, 32, 128)
            for x in range(8):
                out[pl.ds(pl.multiple_of(row_of(2 + 8 * chunk + x, tile, 8), 8), 32), :] = cells[x]
            last_z_out[chunk, 0, :, 2 * tile : 2 * tile + 2, :] = cells[:, 0:2, :]
            last_z_out[chunk, 1, :, 2 * tile : 2 * tile + 2, :] = cells[:, 30:32, :]
        for a, dz in sides:
            remote(*planes(chunk, a), on_slab(dz)).start()
        for b in range(2):

            @pl.when(chunk == 3 * b)
            def _():
                for x in range(2):
                    for tile in range(4):
                        last_x_out[b, x, tile] = out[pl.ds(row_of(row_starts[b] + x, tile, 8), 32), :]
                for i in range(3 * b, 3 * b + 3):
                    source, target, device = last[i]
                    remote(source, target, last_send.at[i], corner_recv.at[i], device).start()

        return carry

    lax.fori_loop(0, CHUNKS, inverse_y, 0)

    slot = lax.broadcasted_iota(jnp.int32, (slots, slots), 0)
    chosen = jnp.where(slot == pairs[0:1, :], 1.0, 0.0).astype(BF16)
    rest = terms[...]
    total = jnp.zeros(near.shape, F32)
    for _ in range(3):
        part = rest.astype(BF16)
        rest = rest - part.astype(F32)
        total = total + jnp.dot(chosen, part, preferred_element_type=F32)
    near[...] = total

    lax.fori_loop(0, CHUNKS - 1, take_planes, 0)
    for i, (source, target, device) in enumerate(last):
        wait_recv(target, corner_recv.at[i])
    for b, start in ((0, 0), (1, 34)):
        for x in range(2):
            for tile in range(4):
                out[pl.ds(row_of(start + x, tile, 8), 32), :] = last_x_in[b, x, tile]
                for a, row in ((0, 6), (1, 40)):
                    out[pl.ds(row_of(start + x, tile, row), 2), :] = last_corner_in[b, a, x, 2 * tile : 2 * tile + 2, :]
    take_planes(CHUNKS - 1, 0)

    def gather_group(step, carry):
        def pick(turn, carry):
            for u in range(UNROLL):
                b = turn * UNROLL + u
                row_0, row_1, lane_0 = window(anchors, step * GROUP + b)
                masks, beyond, top = window_masks(lane_0)
                for i in range(4):
                    cells = jnp.where(beyond, out[pl.ds(row_0 + 192 * i, 8), :], out[pl.ds(row_1 + 192 * i, 8), :])
                    cells = jnp.where(top, cells, pltpu.roll(cells, 4, 0))
                    for j in range(2):
                        values[b, 16 * i + 8 * j : 16 * i + 8 * j + 8] = jnp.where(masks[j], cells, 0.0)
            return carry

        lax.fori_loop(0, GROUP // UNROLL, pick, 0)
        group_copy(step, projection_at, projection, group_load).wait()
        rows = group_rows(step)
        box = lane_sums(values[...].reshape(GROUP * BOX, 128)).reshape(GROUP, BOX, 128)
        far = jnp.sum(projection[rows] * box, axis=1)
        result[rows, :] = far + near[rows, :]
        return carry

    lax.fori_loop(0, slots // GROUP, gather_group, 0)
    for i, (source, target, device) in enumerate(last):
        wait_send(source, last_send.at[i])
    for a in range(2):
        wait_send(last_z_out.at[:, a], last_send.at[6 + a])
    for i, (source, target, device) in enumerate(rims):
        wait_send(source, rim_send.at[i])
    wait_send(sent_1.at[:, :, 0 : n_slab - 1], send_1)
    wait_send(got_2.at[:, :, 0 : 32 * (n_pencil - 1), :], send_2)
    wait_send(got_2.at[:, :, 0 : 32 * (n_pencil - 1), :], send_3)
    wait_send(back_1.at[:, :, 0 : n_slab - 1], send_4)

    @pl.when(middle)
    def _():
        wait_send(level_out, level_send)


def field(anchors, count, pairs, charges, grid, projection, matrices, kernel):
    tables = [jnp.asarray(np.stack(split_table(table))) for table in (y_tables(), z_table(), x_tables())]
    slots, panels = charges.shape
    dma = pltpu.SemaphoreType.DMA
    vmem = pltpu.VMEM
    return pl.pallas_call(
        field_kernel,
        in_specs=[
            *[pl.BlockSpec(memory_space=pltpu.SMEM)] * 2,
            *[pl.BlockSpec(memory_space=vmem)] * 3,
            *[pl.BlockSpec(memory_space=pl.ANY)] * 6,
        ],
        out_specs=pl.BlockSpec(memory_space=vmem),
        out_shape=pltpu.VMEM((slots, panels), F32),
        scratch_shapes=[
            vmem(projection.shape, F32),
            vmem(matrices.shape, BF16),
            vmem(kernel.shape, F32),
            *(vmem(table.shape, BF16) for table in tables),
            vmem((slots, panels), F32),
            vmem((slots, panels), F32),
            vmem((slots, panels), F32),
            vmem((GROUP, BOX, panels), F32),
            vmem((36 * 4 * 48, 128), F32),
            vmem((256, 256), BF16),
            vmem((32, 4, 32, 128), F32),
            vmem((2, 36, 8, 128), F32),
            vmem((2, 32, 8, 128), F32),
            vmem((2, 2, 4, 32, 128), F32),
            vmem((2, 2, 2, 8, 128), F32),
            vmem((2, CHUNKS, 8, 32, 256), F32),
            vmem((2, CHUNKS, 8, 32, 256), F32),
            vmem((2, CHUNKS, 16, 2, 8, 256), F32),
            vmem((2, 2, 512, 256), F32),
            vmem((2, 256, 256), F32),
            vmem((2, 256, 256), F32),
            vmem((2, 2, 256, 256), F32),
            vmem((2, 2, 512, 256), F32),
            vmem((2, CHUNKS, 16, 2, 8, 256), F32),
            vmem((2, CHUNKS, 8, 32, 256), F32),
            vmem((2, CHUNKS, 8, 32, 256), F32),
            vmem((4, 128, 128), F32),
            vmem((CHUNKS, 2, 8, 8, 128), F32),
            vmem((CHUNKS, 2, 8, 8, 128), F32),
            vmem((2, 2, 4, 32, 128), F32),
            vmem((2, 2, 4, 32, 128), F32),
            vmem((2, 2, 2, 8, 128), F32),
            dma((6,)),
            dma((slots // GROUP,)),
            dma,
            dma,
            dma((8,)),
            dma((8,)),
            dma((8,)),
            dma((CHUNKS, 2)),
            dma((6,)),
            dma,
            dma((2, CHUNKS)),
            dma,
            dma((2,)),
            dma,
            dma((2, CHUNKS)),
            dma,
            dma((2, CHUNKS)),
        ],
        compiler_params=pltpu.CompilerParams(
            collective_id=0, has_side_effects=True, vmem_limit_bytes=57 << 20
        ),
        cost_estimate=pl.CostEstimate(flops=10**10, bytes_accessed=10**7, transcendentals=0),
    )(anchors, count, pairs, charges, grid, projection, matrices, kernel, *tables)


def shards(charges, projection, anchors, block_count, near_pairs, near_matrices, kernel_hat):
    grid = pltpu.with_memory_space_constraint(scatter(anchors.T, block_count, projection, charges), pltpu.VMEM)
    levels = jnp.transpose(kernel_hat.reshape(NX, 4, 2, 128), (0, 2, 1, 3)).reshape(NX * 8, 128)
    total = field(anchors.T, block_count, near_pairs.T, charges, grid, projection, near_matrices, levels)
    in_use = lax.broadcasted_iota(jnp.int32, total.shape, 0) < block_count[0]
    return jnp.where(in_use, total, 0.0)


def solution(mesh):
    return jax.shard_map(
        shards,
        mesh=mesh,
        in_specs=(
            P(("slab", "pencil"), None),
            P(("slab", "pencil"), None, None),
            P(("slab", "pencil"), None),
            P(("slab", "pencil")),
            P(("slab", "pencil"), None),
            P(("slab", "pencil"), None, None),
            P(None, ("slab", "pencil"), None),
        ),
        out_specs=P(("slab", "pencil"), None),
        check_vma=False,
    )
```

```python
import jax
import jax.numpy as jnp
import ml_dtypes
import numpy as np
from jax import lax
from jax.experimental import pallas as pl
from jax.experimental.pallas import tpu as pltpu
from jax.sharding import PartitionSpec as P

NX, NY, NZ, BOX = 512, 512, 256, 64
GROUP = 64
UNROLL = 4
AHEAD = 2
F32, BF16 = jnp.float32, jnp.bfloat16


def halves(value):
    high = value.astype(BF16)
    return high, (value - high.astype(F32)).astype(BF16)


def lane_sums(value):
    ones = jnp.ones((128, 128), BF16)
    high, low = halves(value)
    return jnp.dot(high, ones, preferred_element_type=F32) + jnp.dot(low, ones, preferred_element_type=F32)


def row_of(x, tile, z):
    return (x * 4 + tile) * 48 + z


def window(anchors, slot):
    corner = row_of(anchors[0, slot] & 31, 0, (anchors[2, slot] & 31) + 6)
    y_at = (anchors[1, slot] + (NY - 2)) & (NY - 1)
    tile = y_at >> 7
    return corner + 48 * tile, corner + 48 * ((tile + 1) & 3), y_at & 127


def window_masks(lane_0):
    row = lax.broadcasted_iota(jnp.int32, (8, 128), 0)
    lane = lax.broadcasted_iota(jnp.int32, (8, 128), 1)
    shifted = (lane - row // 4 - lane_0) & 127
    return (shifted == 0, shifted == 2), lane >= lane_0, row < 4


def group_rows(step):
    return pl.ds(pl.multiple_of(step * GROUP, GROUP), GROUP)


def group_copy(step, source, target, sems):
    return pltpu.make_async_copy(source.at[group_rows(step)], target.at[group_rows(step)], sems.at[step])


def scatter_kernel(anchors, count, projection_at, charges, cells, projection, values, load):
    grid = cells.reshape(36 * 4 * 48, 128)
    for step in range(AHEAD):
        group_copy(step, projection_at, projection, load).start()

    def clear(x, carry):
        grid[pl.ds(pl.multiple_of(x * 192, 8), 192), :] = jnp.zeros((192, 128), F32)
        return carry

    lax.fori_loop(0, 36, clear, 0)

    def group(step, carry):
        @pl.when(step < charges.shape[0] // GROUP - AHEAD)
        def _():
            group_copy(step + AHEAD, projection_at, projection, load).start()

        group_copy(step, projection_at, projection, load).wait()
        rows = group_rows(step)
        slot = step * GROUP + lax.broadcasted_iota(jnp.int32, (GROUP, 128), 0)
        masked = jnp.where(slot < count[0], charges[rows, :], 0.0)
        products = projection[rows] * masked[:, None, :]
        values[...] = lane_sums(products.reshape(GROUP * BOX, 128)).reshape(GROUP, BOX, 128)

        def place(turn, carry):
            firsts, seconds, furthest = [], [], 0
            for u in range(UNROLL):
                b = turn * UNROLL + u
                row_0, row_1, lane_0 = window(anchors, step * GROUP + b)
                masks, beyond, top = window_masks(lane_0)
                here, there = beyond & top, top & ~beyond
                furthest = jnp.maximum(furthest, lane_0)
                for i in range(4):
                    patch = jnp.where(masks[0], values[b, 16 * i : 16 * i + 8], 0.0)
                    patch = jnp.where(masks[1], values[b, 16 * i + 8 : 16 * i + 16], patch)
                    patch = patch + pltpu.roll(patch, 4, 0)
                    firsts.append((row_0 + 192 * i, jnp.where(here, patch, 0.0)))
                    seconds.append((row_1 + 192 * i, there, patch))
            for row, patch in firsts:
                grid[pl.ds(row, 8), :] += patch

            @pl.when(furthest > 124)
            def _():
                for row, there, patch in seconds:
                    grid[pl.ds(row, 8), :] += jnp.where(there, patch, 0.0)

            return carry

        return lax.fori_loop(0, GROUP // UNROLL, place, carry)

    lax.fori_loop(0, charges.shape[0] // GROUP, group, 0)


def scatter(anchors, count, projection, charges):
    slots = charges.shape[0]
    smem, vmem = pl.BlockSpec(memory_space=pltpu.SMEM), pl.BlockSpec(memory_space=pltpu.VMEM)
    return pl.pallas_call(
        scatter_kernel,
        in_specs=[smem, smem, pl.BlockSpec(memory_space=pl.ANY), vmem],
        out_specs=pl.BlockSpec(memory_space=pltpu.VMEM),
        scratch_shapes=[
            pltpu.VMEM(projection.shape, F32),
            pltpu.VMEM((GROUP, BOX, 128), F32),
            pltpu.SemaphoreType.DMA((slots // GROUP,)),
        ],
        out_shape=pltpu.VMEM((36, 4, 48, 128), F32),
        compiler_params=pltpu.CompilerParams(vmem_limit_bytes=57 << 20),
    )(anchors, count, projection, charges)


CHUNKS = 4
MESH = pl.DeviceIdType.MESH


def phases(product, length):
    angle = 2.0 * np.pi * (product % length) / length
    return np.cos(angle), np.sin(angle)


def split_table(table):
    table = table.astype(np.float32)
    high = table.astype(ml_dtypes.bfloat16)
    return high, (table - high.astype(np.float32)).astype(ml_dtypes.bfloat16)


def y_tables():
    slab, part, pencil = np.meshgrid(np.arange(8), np.arange(2), np.arange(16), indexing="ij")
    device = (slab * 16 + pencil).reshape(-1, 1)
    part = part.reshape(-1, 1)
    even = np.where(device < 64, 4 * device, 4 * device + 2)
    odd = 4 * device + 1
    position = np.arange(256)[None, :]
    result = []
    for freq in (even, odd):
        cos, sin = phases(freq * position, NY)
        table = np.where(part == 0, cos, -sin)
        if freq is even:
            table[(device[:, 0] == 0) & (part[:, 0] == 1)] = 1.0 - 2.0 * (position[0] % 2)
        result.append(table)
    return np.stack(result)


def z_table():
    position = np.arange(NZ)
    cos, sin = phases(position[:, None] * position[None, :], NZ)
    return np.block([[cos, -sin], [sin, cos]])


def x_tables():
    position = np.arange(256)
    result = []
    for parity in range(2):
        cos, sin = phases((2 * position[:, None] + parity) * position[None, :], NX)
        result.append(np.concatenate([cos, sin], axis=1))
        if parity:
            result.append(np.concatenate([cos.T, sin.T], axis=1))
    return np.stack(result)


def dot_3(left, right, dims=((1,), (0,))):
    def one(a, b):
        return lax.dot_general(a, b, (dims, ((), ())), preferred_element_type=F32)

    return one(left[0], right[0]) + (one(left[0], right[1]) + one(left[1], right[0]))


def swap_groups(tiles):
    lane = lax.broadcasted_iota(jnp.int32, tiles[0].shape, 1)
    low, even = lane < 64, lane % 64 < 32
    firsts, lasts = [], []
    for a, b in ((tiles[0], tiles[2]), (tiles[1], tiles[3])):
        firsts.append(jnp.where(low, a, pltpu.roll(b, 64, 1)))
        lasts.append(jnp.where(low, pltpu.roll(a, 64, 1), b))
    result = []
    for a, b in (firsts, lasts):
        result.append(jnp.where(even, a, pltpu.roll(b, 32, 1)))
        result.append(jnp.where(even, pltpu.roll(a, 96, 1), b))
    return result


def field_kernel(
    anchors, count, pairs, charges, grid, projection_at, matrices_at, kernel_at, ty_at, tz_at, tx_at,
    result,
    projection, matrices, kernel, ty, tz, tx, sources, terms, near, values, out, mirror,
    charge, z_out, z_in, x_in, corner_in, sent_1, got_1, sent_2, got_2, level_out, level_in, spectra, back_2, took_2,
    back_1, took_1, lines, last_z_out, last_z_in, last_x_out, last_x_in, last_corner_in,
    load, group_load, level_send, level_recv, rim_send, rim_recv, last_send, last_recv, corner_recv,
    send_1, recv_1, send_2, recv_2, send_3, recv_3, send_4, recv_4,
):
    slab, pencil = lax.axis_index("slab"), lax.axis_index("pencil")
    n_slab, n_pencil = 8, 16

    def at(slab_step, pencil_step):
        return (lax.rem(slab + n_slab + slab_step, n_slab), lax.rem(pencil + n_pencil + pencil_step, n_pencil))

    def on_slab(step):
        return at(step, 0)

    def on_pencil(step):
        return at(0, step)

    def remote(source, target, send_sem, recv_sem, device):
        return pltpu.make_async_remote_copy(
            src_ref=source, dst_ref=target, send_sem=send_sem, recv_sem=recv_sem, device_id=device, device_id_type=MESH
        )

    def wait_recv(ref, sem):
        remote(ref, ref, sem, sem, on_slab(1)).wait_recv()

    def wait_send(ref, sem):
        remote(ref, ref, sem, sem, on_slab(1)).wait_send()

    barrier = pltpu.get_barrier_semaphore()

    def greet(device):
        pl.semaphore_signal(barrier, inc=1, device_id=device, device_id_type=MESH)

    def greet_slab(step, carry):
        greet(on_slab(step))
        return carry

    def greet_pencil(step, carry):
        greet(on_pencil(step))
        return carry

    sides = ((0, -1), (1, 1))
    lax.fori_loop(1, n_slab, greet_slab, 0)
    lax.fori_loop(1, n_pencil, greet_pencil, 0)
    for _, dz in sides:
        for _, dx in sides:
            greet(at(dz, dx))

    loads = [
        pltpu.make_async_copy(source, target, load.at[i])
        for i, (source, target) in enumerate(
            (
                (grid.at[2:34, :, 8:40, :], charge),
                (ty_at, ty),
                (kernel_at, kernel),
                (tz_at, tz),
                (tx_at, tx),
                (matrices_at, matrices),
            )
        )
    ]
    for copy in loads[:2]:
        copy.start()

    def pack_rims(x, carry):
        for tile in range(4):
            z_out[0, x, 2 * tile : 2 * tile + 2, :] = grid[x, tile, 6:8, :]
            z_out[1, x, 2 * tile : 2 * tile + 2, :] = grid[x, tile, 40:42, :]
        return carry

    lax.fori_loop(0, 36, pack_rims, 0, unroll=4)
    pl.semaphore_wait(barrier, n_slab + n_pencil + 2)
    ends = ((0, 2), (34, 36))
    rims = []
    for a, dz in sides:
        rims.append((z_out.at[a, 2:34], z_in.at[1 - a], on_slab(dz)))
    for b, dx in sides:
        rims.append((grid.at[ends[b][0] : ends[b][1], :, 8:40, :], x_in.at[1 - b], on_pencil(dx)))
    for a, dz in sides:
        for b, dx in sides:
            rims.append((z_out.at[a, ends[b][0] : ends[b][1]], corner_in.at[1 - a, 1 - b], at(dz, dx)))
    for i, (source, target, device) in enumerate(rims):
        remote(source, target, rim_send.at[i], rim_recv.at[i], device).start()
    first = jnp.logical_and(slab == 0, pencil == 0)
    middle = jnp.logical_and(slab == 4, pencil == 0)
    for copy in loads[2:]:
        copy.start()

    @pl.when(middle)
    def _():
        loads[2].wait()
        for kx in range(2):
            for i in range(2):
                level_out[kx, :, 128 * i : 128 * i + 128] = kernel[pl.ds(8 * kx + 4 * i, 256, stride=16), :]
        remote(level_out, level_in, level_send, level_recv, (0, pencil)).start()


    loads[0].wait()
    wait_recv(z_in.at[1], rim_recv.at[0])
    wait_recv(z_in.at[0], rim_recv.at[1])

    def add_rims(x, carry):
        for tile in range(4):
            charge[x, tile, 0:2, :] += z_in[0, x, 2 * tile : 2 * tile + 2, :]
            charge[x, tile, 30:32, :] += z_in[1, x, 2 * tile : 2 * tile + 2, :]
        return carry

    lax.fori_loop(0, 32, add_rims, 0, unroll=4)
    loads[1].wait()

    def forward_y(step, carry):
        chunk = lax.rem(step + 1, CHUNKS)

        @pl.when(step == 2)
        def _():
            for i in range(2, 8):
                wait_recv(rims[i][1], rim_recv.at[i])
            for b, start in ((0, 0), (1, 30)):
                charge[start : start + 2] += x_in[b]
                for a, row in ((0, 0), (1, 30)):
                    for x in range(2):
                        for tile in range(4):
                            charge[start + x, tile, row : row + 2, :] += corner_in[a, b, x, 2 * tile : 2 * tile + 2, :]

        tiles = [charge[pl.ds(8 * chunk, 8), tile].reshape(256, 128) for tile in range(4)]
        for parity in range(2):
            if parity:
                halved = [tiles[0] - tiles[2], tiles[1] - tiles[3]]
            else:
                halved = [tiles[0] + tiles[2], tiles[1] + tiles[3]]
            columns = halves(jnp.concatenate(halved, axis=1))
            freqs = dot_3((ty[0, parity], ty[1, parity]), columns, ((1,), (1,)))
            sent_1[parity, chunk] = freqs.reshape(n_slab, 32, 256)
            if not parity:
                to_slabs(0, chunk)
        return carry

    def to_slabs(parity, chunk):
        got_1[parity, chunk, slab] = sent_1[parity, chunk, slab]

        def send(k, carry):
            device = on_slab(k)
            remote(
                sent_1.at[parity, chunk, device[0]], got_1.at[parity, chunk, slab], send_1, recv_1.at[parity, chunk], device
            ).start()
            return carry

        return lax.fori_loop(1, n_slab, send, 0)

    lax.fori_loop(0, CHUNKS, forward_y, 0)
    lax.fori_loop(0, CHUNKS, lambda step, carry: to_slabs(1, lax.rem(step + 1, CHUNKS)), 0)
    for step in range(charges.shape[0] // GROUP):
        group_copy(step, projection_at, projection, group_load).start()

    slots, panels = charges.shape
    slot = lax.broadcasted_iota(jnp.int32, (slots, panels), 0)
    coarse = jnp.where(slot < count[0], charges[...], 0.0).astype(BF16)
    slot = lax.broadcasted_iota(jnp.int32, (slots, slots), 0)
    chosen = jnp.where(slot == pairs[1:2, :], 1.0, 0.0)
    row = lax.broadcasted_iota(jnp.int32, (256, 256), 0)
    lane = lax.broadcasted_iota(jnp.int32, (256, 256), 1)
    mirror[...] = jnp.where((row + lane) & 255 == 0, 1.0, 0.0).astype(BF16)
    sources[...] = jnp.dot(chosen.T.astype(BF16), coarse, preferred_element_type=F32)
    pl.when(jnp.logical_not(middle))(loads[2].wait)
    loads[3].wait()
    loads[5].wait()

    def near_group(group, carry):
        rows = pl.ds(pl.multiple_of(8 * group, 8), 8)
        taken = sources[rows, :].astype(BF16)
        row = lax.broadcasted_iota(jnp.int32, (8, panels), 0)
        total = jnp.zeros((8, panels), F32)
        for i in range(8):
            found = lax.dot_general(
                taken, matrices[8 * group + i], (((1,), (1,)), ((), ())), preferred_element_type=F32
            )
            total = jnp.where(row == i, found, total)
        terms[rows, :] = total
        return carry

    near_turns = 2 * CHUNKS - 2

    def near_share(turn):
        start, stop = ((slots // 8) * t // near_turns for t in (jnp.minimum(turn, near_turns), jnp.minimum(turn + 1, near_turns)))
        lax.fori_loop(start, stop, near_group, 0)

    def forward_z(turn, carry):
        parity, chunk = turn // CHUNKS, lax.rem(turn + 1, CHUNKS)
        near_share(turn)
        wait_recv(got_1.at[parity, chunk, 0 : n_slab - 1], recv_1.at[parity, chunk])
        for h in range(2):
            for q in range(2):
                tiles = swap_groups([got_1[parity, chunk, 4 * q + s, :, 128 * h : 128 * h + 128] for s in range(4)])
                for a in range(4):
                    for part in range(2):
                        lines[2 * part + q, pl.ds(4 * h + a, 16, stride=8), :] = tiles[a][16 * part : 16 * part + 16]
        rows = halves(jnp.concatenate([lines[i] for i in range(4)], axis=1))
        freqs = dot_3(rows, (tz[0], tz[1]))
        for part in range(2):
            sent_2[parity, chunk, :, part] = freqs[:, 256 * part : 256 * part + 256].reshape(n_pencil, 8, 256)
        mine = pl.ds(pl.multiple_of(pencil * 32 + chunk * 8, 8), 8)
        got_2[parity, :, mine, :] = sent_2[parity, chunk, pencil]

        def send(k, carry):
            device = on_pencil(k)
            remote(
                sent_2.at[parity, chunk, device[1]], got_2.at[parity, :, mine, :], send_2, recv_2.at[parity], device
            ).start()
            return carry

        return lax.fori_loop(1, n_pencil, send, carry)

    lax.fori_loop(0, 2 * CHUNKS - 2, forward_z, 0)

    loads[4].wait()
    unit = 1.0 / (NX * NY * NZ)

    def stacked(real, imag):
        return tuple(
            jnp.concatenate([jnp.concatenate([r, i], axis=1), jnp.concatenate([i, -r], axis=1)], axis=0)
            for r, i in zip(real, imag)
        )

    def mirrored(pieces):
        return tuple(jnp.dot(piece, mirror[...], preferred_element_type=F32).astype(BF16) for piece in pieces)

    def levels(start, unit):
        pieces = [kernel[pl.ds(start + 4 * i, 256, stride=16), :] for i in range(2)]
        return jnp.concatenate(pieces, axis=1) * unit

    def along_x(parity):
        wait_recv(got_2.at[parity, :, 0 : 32 * (n_pencil - 1), :], recv_2.at[parity])

        def found(kx, twin):
            parts = []
            for part in range(2):
                low, high = got_2[parity, part, 0:256, :], got_2[parity, part, 256:512, :]
                parts.append(halves(low - high if kx else low + high))
            right = stacked(*parts)
            if twin:
                real, imag = (mirrored(pieces) for pieces in parts)
                other = stacked(real, tuple(-piece for piece in imag))
                right = tuple(jnp.concatenate(both, axis=1) for both in zip(right, other))
            return dot_3((tx[0, kx], tx[1, kx]), right)

        def plain():
            own = 1 if parity else jnp.where(slab < 4, 0, 2)
            for kx in range(2):
                both, green = found(kx, False), levels(own + 8 * kx, 2.0 * unit)
                spectra[kx, 0] = both[:, 0:256] * green
                spectra[kx, 1] = both[:, 256:512] * green

        if parity:
            plain()
        else:
            pl.when(jnp.logical_not(first))(plain)

            @pl.when(first)
            def _():
                wait_recv(level_in, level_recv)
                for kx in range(2):
                    both, green, other = found(kx, True), levels(8 * kx, 0.5 * unit), level_in[kx] * (0.5 * unit)
                    mean, rest = green + other, green - other
                    for part in range(2):
                        one, two = (both[:, 256 * k : 256 * k + 256] for k in (part, part + 2))
                        spectra[kx, part] = mean * one + rest * two

        ends = []
        for kx in range(2):
            table = (tx[0, 2 * kx], tx[1, 2 * kx])
            real, imag = halves(spectra[kx, 0]), halves(spectra[kx, 1])
            right = tuple(
                jnp.concatenate([jnp.concatenate([r, i], axis=1), jnp.concatenate([-i, r], axis=1)], axis=0)
                for r, i in zip(real, imag)
            )
            ends.append(dot_3(table, right))
        for part in range(2):
            lanes = slice(256 * part, 256 * part + 256)
            back_2[parity, part, 0:256, :] = ends[0][:, lanes] + ends[1][:, lanes]
            back_2[parity, part, 256:512, :] = ends[0][:, lanes] - ends[1][:, lanes]

    def turns(step):
        return jnp.where(step < 2, 3 * step, step - 1)

    def return_x(turn, carry):
        parity, chunk = turn // CHUNKS, turns(lax.rem(turn, CHUNKS))
        own = pl.ds(pl.multiple_of(pencil * 32 + chunk * 8, 8), 8)
        took_2[parity, chunk, pencil] = back_2[parity, :, own, :]

        def send(k, carry):
            device = on_pencil(k)
            rows = pl.ds(pl.multiple_of(device[1] * 32 + chunk * 8, 8), 8)
            remote(
                back_2.at[parity, :, rows, :], took_2.at[parity, chunk, pencil], send_3, recv_3.at[parity, chunk], device
            ).start()
            return carry

        return lax.fori_loop(1, n_pencil, send, carry)

    def inverse_z(turn, carry):
        parity, chunk = turn // CHUNKS, turns(lax.rem(turn, CHUNKS))
        wait_recv(took_2.at[parity, chunk, 0 : n_pencil - 1], recv_3.at[parity, chunk])
        rows = jnp.concatenate([took_2[parity, chunk, :, part].reshape(128, 256) for part in range(2)], axis=1)
        space = dot_3(halves(rows), (tz[0], tz[1]), ((1,), (1,)))
        for i in range(4):
            lines[i] = space[:, 128 * i : 128 * i + 128]
        for h in range(2):
            for q in range(2):
                tiles = []
                for a in range(4):
                    pieces = [lines[2 * part + q, pl.ds(4 * h + a, 16, stride=8), :] for part in range(2)]
                    tiles.append(jnp.concatenate(pieces, axis=0))
                for s, tile in enumerate(swap_groups(tiles)):
                    back_1[parity, chunk, 4 * q + s, :, 128 * h : 128 * h + 128] = tile
        took_1[parity, chunk, slab] = back_1[parity, chunk, slab]

        def send(k, carry):
            device = on_slab(k)
            remote(
                back_1.at[parity, chunk, device[0]], took_1.at[parity, chunk, slab], send_4, recv_4.at[parity, chunk], device
            ).start()
            return carry

        return lax.fori_loop(1, n_slab, send, carry)

    along_x(0)
    lax.fori_loop(0, 1, return_x, 0)
    lax.fori_loop(1, 3, lambda turn, carry: return_x(turn, forward_z(turn + 5, carry)), 0)
    lax.fori_loop(3, 4, return_x, 0)
    lax.fori_loop(0, 2, inverse_z, 0)
    along_x(1)
    lax.fori_loop(4, 8, return_x, 0)
    lax.fori_loop(2, 8, inverse_z, 0)

    row_starts = (2, 32)
    last = []
    for b, dx in sides:
        last.append((last_x_out.at[b], last_x_in.at[1 - b], on_pencil(dx)))
        for a, dz in sides:
            rows = (0, 2) if b == 0 else (6, 8)
            last.append(
                (last_z_out.at[3 * b, a, rows[0] : rows[1]], last_corner_in.at[1 - b, 1 - a], at(dz, dx))
            )

    def planes(chunk, a):
        return (last_z_out.at[chunk, a], last_z_in.at[chunk, 1 - a], last_send.at[6 + a], last_recv.at[chunk, 1 - a])

    def take_planes(step, carry):
        chunk = turns(step)
        for a, row in ((0, 6), (1, 40)):
            wait_recv(last_z_in.at[chunk, a], last_recv.at[chunk, a])
            for x in range(8):
                for tile in range(4):
                    out[pl.ds(row_of(2 + 8 * chunk + x, tile, row), 2), :] = last_z_in[chunk, a, x, 2 * tile : 2 * tile + 2, :]
        return carry

    def inverse_y(step, carry):
        chunk = turns(step)
        ends = []
        for parity in range(2):
            wait_recv(took_1.at[parity, chunk, 0 : n_slab - 1], recv_4.at[parity, chunk])
            columns = took_1[parity, chunk].reshape(256, 256).T
            ends.append(dot_3(halves(columns), (ty[0, parity], ty[1, parity])))
        space = (ends[0] + ends[1], ends[0] - ends[1])
        for tile in range(4):
            lanes = slice(128 * (tile % 2), 128 * (tile % 2) + 128)
            cells = space[tile // 2][:, lanes].reshape(8, 32, 128)
            for x in range(8):
                out[pl.ds(pl.multiple_of(row_of(2 + 8 * chunk + x, tile, 8), 8), 32), :] = cells[x]
            last_z_out[chunk, 0, :, 2 * tile : 2 * tile + 2, :] = cells[:, 0:2, :]
            last_z_out[chunk, 1, :, 2 * tile : 2 * tile + 2, :] = cells[:, 30:32, :]
        for a, dz in sides:
            remote(*planes(chunk, a), on_slab(dz)).start()
        for b in range(2):

            @pl.when(chunk == 3 * b)
            def _():
                for x in range(2):
                    for tile in range(4):
                        last_x_out[b, x, tile] = out[pl.ds(row_of(row_starts[b] + x, tile, 8), 32), :]
                for i in range(3 * b, 3 * b + 3):
                    source, target, device = last[i]
                    remote(source, target, last_send.at[i], corner_recv.at[i], device).start()

        return carry

    lax.fori_loop(0, CHUNKS, inverse_y, 0)

    slot = lax.broadcasted_iota(jnp.int32, (slots, slots), 0)
    chosen = jnp.where(slot == pairs[0:1, :], 1.0, 0.0).astype(BF16)
    rest = terms[...]
    total = jnp.zeros(near.shape, F32)
    for _ in range(3):
        part = rest.astype(BF16)
        rest = rest - part.astype(F32)
        total = total + jnp.dot(chosen, part, preferred_element_type=F32)
    near[...] = total

    lax.fori_loop(0, CHUNKS - 1, take_planes, 0)
    for i, (source, target, device) in enumerate(last):
        wait_recv(target, corner_recv.at[i])
    for b, start in ((0, 0), (1, 34)):
        for x in range(2):
            for tile in range(4):
                out[pl.ds(row_of(start + x, tile, 8), 32), :] = last_x_in[b, x, tile]
                for a, row in ((0, 6), (1, 40)):
                    out[pl.ds(row_of(start + x, tile, row), 2), :] = last_corner_in[b, a, x, 2 * tile : 2 * tile + 2, :]
    take_planes(CHUNKS - 1, 0)

    def gather_group(step, carry):
        def pick(turn, carry):
            for u in range(UNROLL):
                b = turn * UNROLL + u
                row_0, row_1, lane_0 = window(anchors, step * GROUP + b)
                masks, beyond, top = window_masks(lane_0)
                for i in range(4):
                    cells = jnp.where(beyond, out[pl.ds(row_0 + 192 * i, 8), :], out[pl.ds(row_1 + 192 * i, 8), :])
                    cells = jnp.where(top, cells, pltpu.roll(cells, 4, 0))
                    for j in range(2):
                        values[b, 16 * i + 8 * j : 16 * i + 8 * j + 8] = jnp.where(masks[j], cells, 0.0)
            return carry

        lax.fori_loop(0, GROUP // UNROLL, pick, 0)
        group_copy(step, projection_at, projection, group_load).wait()
        rows = group_rows(step)
        box = lane_sums(values[...].reshape(GROUP * BOX, 128)).reshape(GROUP, BOX, 128)
        far = jnp.sum(projection[rows] * box, axis=1)
        result[rows, :] = far + near[rows, :]
        return carry

    lax.fori_loop(0, slots // GROUP, gather_group, 0)
    for i, (source, target, device) in enumerate(last):
        wait_send(source, last_send.at[i])
    for a in range(2):
        wait_send(last_z_out.at[:, a], last_send.at[6 + a])
    for i, (source, target, device) in enumerate(rims):
        wait_send(source, rim_send.at[i])
    wait_send(sent_1.at[:, :, 0 : n_slab - 1], send_1)
    wait_send(got_2.at[:, :, 0 : 32 * (n_pencil - 1), :], send_2)
    wait_send(got_2.at[:, :, 0 : 32 * (n_pencil - 1), :], send_3)
    wait_send(back_1.at[:, :, 0 : n_slab - 1], send_4)

    @pl.when(middle)
    def _():
        wait_send(level_out, level_send)


def field(anchors, count, pairs, charges, grid, projection, matrices, kernel):
    tables = [jnp.asarray(np.stack(split_table(table))) for table in (y_tables(), z_table(), x_tables())]
    slots, panels = charges.shape
    dma = pltpu.SemaphoreType.DMA
    vmem = pltpu.VMEM
    return pl.pallas_call(
        field_kernel,
        in_specs=[
            *[pl.BlockSpec(memory_space=pltpu.SMEM)] * 2,
            *[pl.BlockSpec(memory_space=vmem)] * 3,
            *[pl.BlockSpec(memory_space=pl.ANY)] * 6,
        ],
        out_specs=pl.BlockSpec(memory_space=vmem),
        out_shape=pltpu.VMEM((slots, panels), F32),
        scratch_shapes=[
            vmem(projection.shape, F32),
            vmem(matrices.shape, BF16),
            vmem(kernel.shape, F32),
            *(vmem(table.shape, BF16) for table in tables),
            vmem((slots, panels), F32),
            vmem((slots, panels), F32),
            vmem((slots, panels), F32),
            vmem((GROUP, BOX, panels), F32),
            vmem((36 * 4 * 48, 128), F32),
            vmem((256, 256), BF16),
            vmem((32, 4, 32, 128), F32),
            vmem((2, 36, 8, 128), F32),
            vmem((2, 32, 8, 128), F32),
            vmem((2, 2, 4, 32, 128), F32),
            vmem((2, 2, 2, 8, 128), F32),
            vmem((2, CHUNKS, 8, 32, 256), F32),
            vmem((2, CHUNKS, 8, 32, 256), F32),
            vmem((2, CHUNKS, 16, 2, 8, 256), F32),
            vmem((2, 2, 512, 256), F32),
            vmem((2, 256, 256), F32),
            vmem((2, 256, 256), F32),
            vmem((2, 2, 256, 256), F32),
            vmem((2, 2, 512, 256), F32),
            vmem((2, CHUNKS, 16, 2, 8, 256), F32),
            vmem((2, CHUNKS, 8, 32, 256), F32),
            vmem((2, CHUNKS, 8, 32, 256), F32),
            vmem((4, 128, 128), F32),
            vmem((CHUNKS, 2, 8, 8, 128), F32),
            vmem((CHUNKS, 2, 8, 8, 128), F32),
            vmem((2, 2, 4, 32, 128), F32),
            vmem((2, 2, 4, 32, 128), F32),
            vmem((2, 2, 2, 8, 128), F32),
            dma((6,)),
            dma((slots // GROUP,)),
            dma,
            dma,
            dma((8,)),
            dma((8,)),
            dma((8,)),
            dma((CHUNKS, 2)),
            dma((6,)),
            dma,
            dma((2, CHUNKS)),
            dma,
            dma((2,)),
            dma,
            dma((2, CHUNKS)),
            dma,
            dma((2, CHUNKS)),
        ],
        compiler_params=pltpu.CompilerParams(
            collective_id=0, has_side_effects=True, vmem_limit_bytes=57 << 20
        ),
        cost_estimate=pl.CostEstimate(flops=10**10, bytes_accessed=10**7, transcendentals=0),
    )(anchors, count, pairs, charges, grid, projection, matrices, kernel, *tables)


def shards(charges, projection, anchors, block_count, near_pairs, near_matrices, kernel_hat):
    grid = pltpu.with_memory_space_constraint(scatter(anchors.T, block_count, projection, charges), pltpu.VMEM)
    levels = jnp.transpose(kernel_hat.reshape(NX, 4, 2, 128), (0, 2, 1, 3)).reshape(NX * 8, 128)
    total = field(anchors.T, block_count, near_pairs.T, charges, grid, projection, near_matrices, levels)
    in_use = lax.broadcasted_iota(jnp.int32, total.shape, 0) < block_count[0]
    return jnp.where(in_use, total, 0.0)


def solution(mesh):
    return jax.shard_map(
        shards,
        mesh=mesh,
        in_specs=(
            P(("slab", "pencil"), None),
            P(("slab", "pencil"), None, None),
            P(("slab", "pencil"), None),
            P(("slab", "pencil")),
            P(("slab", "pencil"), None),
            P(("slab", "pencil"), None, None),
            P(None, ("slab", "pencil"), None),
        ),
        out_specs=P(("slab", "pencil"), None),
        check_vma=False,
    )
```

```python
import jax
import jax.numpy as jnp
import ml_dtypes
import numpy as np
from jax import lax
from jax.experimental import pallas as pl
from jax.experimental.pallas import tpu as pltpu
from jax.sharding import PartitionSpec as P

NX, NY, NZ, BOX = 512, 512, 256, 64
GROUP = 64
UNROLL = 4
AHEAD = 2
F32, BF16 = jnp.float32, jnp.bfloat16


def halves(value):
    high = value.astype(BF16)
    return high, (value - high.astype(F32)).astype(BF16)


def lane_sums(value):
    ones = jnp.ones((128, 128), BF16)
    high, low = halves(value)
    return jnp.dot(high, ones, preferred_element_type=F32) + jnp.dot(low, ones, preferred_element_type=F32)


def row_of(x, tile, z):
    return (x * 4 + tile) * 48 + z


def window(anchors, slot):
    corner = row_of(anchors[0, slot] & 31, 0, (anchors[2, slot] & 31) + 6)
    y_at = (anchors[1, slot] + (NY - 2)) & (NY - 1)
    tile = y_at >> 7
    return corner + 48 * tile, corner + 48 * ((tile + 1) & 3), y_at & 127


def window_masks(lane_0):
    row = lax.broadcasted_iota(jnp.int32, (8, 128), 0)
    lane = lax.broadcasted_iota(jnp.int32, (8, 128), 1)
    shifted = (lane - row // 4 - lane_0) & 127
    return (shifted == 0, shifted == 2), lane >= lane_0, row < 4


def group_rows(step):
    return pl.ds(pl.multiple_of(step * GROUP, GROUP), GROUP)


def group_copy(step, source, target, sems):
    return pltpu.make_async_copy(source.at[group_rows(step)], target.at[group_rows(step)], sems.at[step])


def scatter_kernel(anchors, count, projection_at, charges, cells, projection, values, load):
    grid = cells.reshape(36 * 4 * 48, 128)
    for step in range(AHEAD):
        group_copy(step, projection_at, projection, load).start()

    def clear(x, carry):
        grid[pl.ds(pl.multiple_of(x * 192, 8), 192), :] = jnp.zeros((192, 128), F32)
        return carry

    lax.fori_loop(0, 36, clear, 0)

    def group(step, carry):
        @pl.when(step < charges.shape[0] // GROUP - AHEAD)
        def _():
            group_copy(step + AHEAD, projection_at, projection, load).start()

        group_copy(step, projection_at, projection, load).wait()
        rows = group_rows(step)
        slot = step * GROUP + lax.broadcasted_iota(jnp.int32, (GROUP, 128), 0)
        masked = jnp.where(slot < count[0], charges[rows, :], 0.0)
        products = projection[rows] * masked[:, None, :]
        values[...] = lane_sums(products.reshape(GROUP * BOX, 128)).reshape(GROUP, BOX, 128)

        def place(turn, carry):
            firsts, seconds, furthest = [], [], 0
            for u in range(UNROLL):
                b = turn * UNROLL + u
                row_0, row_1, lane_0 = window(anchors, step * GROUP + b)
                masks, beyond, top = window_masks(lane_0)
                here, there = beyond & top, top & ~beyond
                furthest = jnp.maximum(furthest, lane_0)
                for i in range(4):
                    patch = jnp.where(masks[0], values[b, 16 * i : 16 * i + 8], 0.0)
                    patch = jnp.where(masks[1], values[b, 16 * i + 8 : 16 * i + 16], patch)
                    patch = patch + pltpu.roll(patch, 4, 0)
                    firsts.append((row_0 + 192 * i, jnp.where(here, patch, 0.0)))
                    seconds.append((row_1 + 192 * i, there, patch))
            for row, patch in firsts:
                grid[pl.ds(row, 8), :] += patch

            @pl.when(furthest > 124)
            def _():
                for row, there, patch in seconds:
                    grid[pl.ds(row, 8), :] += jnp.where(there, patch, 0.0)

            return carry

        return lax.fori_loop(0, GROUP // UNROLL, place, carry)

    lax.fori_loop(0, charges.shape[0] // GROUP, group, 0)


def scatter(anchors, count, projection, charges):
    slots = charges.shape[0]
    smem, vmem = pl.BlockSpec(memory_space=pltpu.SMEM), pl.BlockSpec(memory_space=pltpu.VMEM)
    return pl.pallas_call(
        scatter_kernel,
        in_specs=[smem, smem, pl.BlockSpec(memory_space=pl.ANY), vmem],
        out_specs=pl.BlockSpec(memory_space=pltpu.VMEM),
        scratch_shapes=[
            pltpu.VMEM(projection.shape, F32),
            pltpu.VMEM((GROUP, BOX, 128), F32),
            pltpu.SemaphoreType.DMA((slots // GROUP,)),
        ],
        out_shape=pltpu.VMEM((36, 4, 48, 128), F32),
        compiler_params=pltpu.CompilerParams(vmem_limit_bytes=57 << 20),
    )(anchors, count, projection, charges)


CHUNKS = 4
MESH = pl.DeviceIdType.MESH


def phases(product, length):
    angle = 2.0 * np.pi * (product % length) / length
    return np.cos(angle), np.sin(angle)


def split_table(table):
    table = table.astype(np.float32)
    high = table.astype(ml_dtypes.bfloat16)
    return high, (table - high.astype(np.float32)).astype(ml_dtypes.bfloat16)


def y_tables():
    slab, part, pencil = np.meshgrid(np.arange(8), np.arange(2), np.arange(16), indexing="ij")
    device = (slab * 16 + pencil).reshape(-1, 1)
    part = part.reshape(-1, 1)
    even = np.where(device < 64, 4 * device, 4 * device + 2)
    odd = 4 * device + 1
    position = np.arange(256)[None, :]
    result = []
    for freq in (even, odd):
        cos, sin = phases(freq * position, NY)
        table = np.where(part == 0, cos, -sin)
        if freq is even:
            table[(device[:, 0] == 0) & (part[:, 0] == 1)] = 1.0 - 2.0 * (position[0] % 2)
        result.append(table)
    return np.stack(result)


def z_table():
    position = np.arange(NZ)
    cos, sin = phases(position[:, None] * position[None, :], NZ)
    return np.block([[cos, -sin], [sin, cos]])


def x_tables():
    position = np.arange(256)
    result = []
    for parity in range(2):
        cos, sin = phases((2 * position[:, None] + parity) * position[None, :], NX)
        result.append(np.concatenate([cos, sin], axis=1))
        if parity:
            result.append(np.concatenate([cos.T, sin.T], axis=1))
    return np.stack(result)


def dot_3(left, right, dims=((1,), (0,))):
    def one(a, b):
        return lax.dot_general(a, b, (dims, ((), ())), preferred_element_type=F32)

    return one(left[0], right[0]) + (one(left[0], right[1]) + one(left[1], right[0]))


def swap_groups(tiles):
    lane = lax.broadcasted_iota(jnp.int32, tiles[0].shape, 1)
    low, even = lane < 64, lane % 64 < 32
    firsts, lasts = [], []
    for a, b in ((tiles[0], tiles[2]), (tiles[1], tiles[3])):
        firsts.append(jnp.where(low, a, pltpu.roll(b, 64, 1)))
        lasts.append(jnp.where(low, pltpu.roll(a, 64, 1), b))
    result = []
    for a, b in (firsts, lasts):
        result.append(jnp.where(even, a, pltpu.roll(b, 32, 1)))
        result.append(jnp.where(even, pltpu.roll(a, 96, 1), b))
    return result


def field_kernel(
    anchors, count, pairs, charges, grid, projection_at, matrices_at, kernel_at, ty_at, tz_at, tx_at,
    result,
    projection, matrices, kernel, ty, tz, tx, sources, terms, near, values, out, mirror,
    charge, z_out, z_in, x_in, corner_in, sent_1, got_1, sent_2, got_2, level_out, level_in, spectra, back_2, took_2,
    back_1, took_1, lines, last_z_out, last_z_in, last_x_out, last_x_in, last_corner_in,
    load, group_load, level_send, level_recv, rim_send, rim_recv, last_send, last_recv, corner_recv,
    send_1, recv_1, send_2, recv_2, send_3, recv_3, send_4, recv_4,
):
    slab, pencil = lax.axis_index("slab"), lax.axis_index("pencil")
    n_slab, n_pencil = 8, 16

    def at(slab_step, pencil_step):
        return (lax.rem(slab + n_slab + slab_step, n_slab), lax.rem(pencil + n_pencil + pencil_step, n_pencil))

    def on_slab(step):
        return at(step, 0)

    def on_pencil(step):
        return at(0, step)

    def remote(source, target, send_sem, recv_sem, device):
        return pltpu.make_async_remote_copy(
            src_ref=source, dst_ref=target, send_sem=send_sem, recv_sem=recv_sem, device_id=device, device_id_type=MESH
        )

    def wait_recv(ref, sem):
        remote(ref, ref, sem, sem, on_slab(1)).wait_recv()

    def wait_send(ref, sem):
        remote(ref, ref, sem, sem, on_slab(1)).wait_send()

    barrier = pltpu.get_barrier_semaphore()

    def greet(device):
        pl.semaphore_signal(barrier, inc=1, device_id=device, device_id_type=MESH)

    def greet_slab(step, carry):
        greet(on_slab(step))
        return carry

    def greet_pencil(step, carry):
        greet(on_pencil(step))
        return carry

    sides = ((0, -1), (1, 1))
    lax.fori_loop(1, n_slab, greet_slab, 0, unroll=7)
    lax.fori_loop(1, n_pencil, greet_pencil, 0, unroll=5)
    for _, dz in sides:
        for _, dx in sides:
            greet(at(dz, dx))

    loads = [
        pltpu.make_async_copy(source, target, load.at[i])
        for i, (source, target) in enumerate(
            (
                (grid.at[2:34, :, 8:40, :], charge),
                (ty_at, ty),
                (kernel_at, kernel),
                (tz_at, tz),
                (tx_at, tx),
                (matrices_at, matrices),
            )
        )
    ]
    for copy in loads[:2]:
        copy.start()

    def pack_rims(x, carry):
        for tile in range(4):
            z_out[0, x, 2 * tile : 2 * tile + 2, :] = grid[x, tile, 6:8, :]
            z_out[1, x, 2 * tile : 2 * tile + 2, :] = grid[x, tile, 40:42, :]
        return carry

    lax.fori_loop(0, 36, pack_rims, 0, unroll=4)
    pl.semaphore_wait(barrier, n_slab + n_pencil + 2)
    ends = ((0, 2), (34, 36))
    rims = []
    for a, dz in sides:
        rims.append((z_out.at[a, 2:34], z_in.at[1 - a], on_slab(dz)))
    for b, dx in sides:
        rims.append((grid.at[ends[b][0] : ends[b][1], :, 8:40, :], x_in.at[1 - b], on_pencil(dx)))
    for a, dz in sides:
        for b, dx in sides:
            rims.append((z_out.at[a, ends[b][0] : ends[b][1]], corner_in.at[1 - a, 1 - b], at(dz, dx)))
    for i, (source, target, device) in enumerate(rims):
        remote(source, target, rim_send.at[i], rim_recv.at[i], device).start()
    first = jnp.logical_and(slab == 0, pencil == 0)
    middle = jnp.logical_and(slab == 4, pencil == 0)
    for copy in loads[2:]:
        copy.start()

    @pl.when(middle)
    def _():
        loads[2].wait()
        for kx in range(2):
            for i in range(2):
                level_out[kx, :, 128 * i : 128 * i + 128] = kernel[pl.ds(8 * kx + 4 * i, 256, stride=16), :]
        remote(level_out, level_in, level_send, level_recv, (0, pencil)).start()


    loads[0].wait()
    wait_recv(z_in.at[1], rim_recv.at[0])
    wait_recv(z_in.at[0], rim_recv.at[1])

    def add_rims(x, carry):
        for tile in range(4):
            charge[x, tile, 0:2, :] += z_in[0, x, 2 * tile : 2 * tile + 2, :]
            charge[x, tile, 30:32, :] += z_in[1, x, 2 * tile : 2 * tile + 2, :]
        return carry

    lax.fori_loop(0, 32, add_rims, 0, unroll=4)
    loads[1].wait()

    def forward_y(step, carry):
        chunk = lax.rem(step + 1, CHUNKS)

        @pl.when(step == 2)
        def _():
            for i in range(2, 8):
                wait_recv(rims[i][1], rim_recv.at[i])
            for b, start in ((0, 0), (1, 30)):
                charge[start : start + 2] += x_in[b]
                for a, row in ((0, 0), (1, 30)):
                    for x in range(2):
                        for tile in range(4):
                            charge[start + x, tile, row : row + 2, :] += corner_in[a, b, x, 2 * tile : 2 * tile + 2, :]

        tiles = [charge[pl.ds(8 * chunk, 8), tile].reshape(256, 128) for tile in range(4)]
        for parity in range(2):
            if parity:
                halved = [tiles[0] - tiles[2], tiles[1] - tiles[3]]
            else:
                halved = [tiles[0] + tiles[2], tiles[1] + tiles[3]]
            columns = halves(jnp.concatenate(halved, axis=1))
            freqs = dot_3((ty[0, parity], ty[1, parity]), columns, ((1,), (1,)))
            sent_1[parity, chunk] = freqs.reshape(n_slab, 32, 256)
            if not parity:
                to_slabs(0, chunk)
        return carry

    def to_slabs(parity, chunk):
        got_1[parity, chunk, slab] = sent_1[parity, chunk, slab]

        def send(k, carry):
            device = on_slab(k)
            remote(
                sent_1.at[parity, chunk, device[0]], got_1.at[parity, chunk, slab], send_1, recv_1.at[parity, chunk], device
            ).start()
            return carry

        return lax.fori_loop(1, n_slab, send, 0, unroll=7)

    lax.fori_loop(0, CHUNKS, forward_y, 0)
    lax.fori_loop(0, CHUNKS, lambda step, carry: to_slabs(1, lax.rem(step + 1, CHUNKS)), 0)
    for step in range(charges.shape[0] // GROUP):
        group_copy(step, projection_at, projection, group_load).start()

    slots, panels = charges.shape
    slot = lax.broadcasted_iota(jnp.int32, (slots, panels), 0)
    coarse = jnp.where(slot < count[0], charges[...], 0.0).astype(BF16)
    slot = lax.broadcasted_iota(jnp.int32, (slots, slots), 0)
    chosen = jnp.where(slot == pairs[1:2, :], 1.0, 0.0)
    row = lax.broadcasted_iota(jnp.int32, (256, 256), 0)
    lane = lax.broadcasted_iota(jnp.int32, (256, 256), 1)
    mirror[...] = jnp.where((row + lane) & 255 == 0, 1.0, 0.0).astype(BF16)
    sources[...] = jnp.dot(chosen.T.astype(BF16), coarse, preferred_element_type=F32)
    pl.when(jnp.logical_not(middle))(loads[2].wait)
    loads[3].wait()
    loads[5].wait()

    def near_group(group, carry):
        rows = pl.ds(pl.multiple_of(8 * group, 8), 8)
        taken = sources[rows, :].astype(BF16)
        row = lax.broadcasted_iota(jnp.int32, (8, panels), 0)
        total = jnp.zeros((8, panels), F32)
        for i in range(8):
            found = lax.dot_general(
                taken, matrices[8 * group + i], (((1,), (1,)), ((), ())), preferred_element_type=F32
            )
            total = jnp.where(row == i, found, total)
        terms[rows, :] = total
        return carry

    near_turns = 2 * CHUNKS - 2

    def near_share(turn):
        start, stop = ((slots // 8) * t // near_turns for t in (jnp.minimum(turn, near_turns), jnp.minimum(turn + 1, near_turns)))
        lax.fori_loop(start, stop, near_group, 0)

    def forward_z(turn, carry):
        parity, chunk = turn // CHUNKS, lax.rem(turn + 1, CHUNKS)
        near_share(turn)
        wait_recv(got_1.at[parity, chunk, 0 : n_slab - 1], recv_1.at[parity, chunk])
        for h in range(2):
            for q in range(2):
                tiles = swap_groups([got_1[parity, chunk, 4 * q + s, :, 128 * h : 128 * h + 128] for s in range(4)])
                for a in range(4):
                    for part in range(2):
                        lines[2 * part + q, pl.ds(4 * h + a, 16, stride=8), :] = tiles[a][16 * part : 16 * part + 16]
        rows = halves(jnp.concatenate([lines[i] for i in range(4)], axis=1))
        freqs = dot_3(rows, (tz[0], tz[1]))
        for part in range(2):
            sent_2[parity, chunk, :, part] = freqs[:, 256 * part : 256 * part + 256].reshape(n_pencil, 8, 256)
        mine = pl.ds(pl.multiple_of(pencil * 32 + chunk * 8, 8), 8)
        got_2[parity, :, mine, :] = sent_2[parity, chunk, pencil]

        def send(k, carry):
            device = on_pencil(k)
            remote(
                sent_2.at[parity, chunk, device[1]], got_2.at[parity, :, mine, :], send_2, recv_2.at[parity], device
            ).start()
            return carry

        return lax.fori_loop(1, n_pencil, send, carry, unroll=5)

    lax.fori_loop(0, 2 * CHUNKS - 2, forward_z, 0)

    loads[4].wait()
    unit = 1.0 / (NX * NY * NZ)

    def stacked(real, imag):
        return tuple(
            jnp.concatenate([jnp.concatenate([r, i], axis=1), jnp.concatenate([i, -r], axis=1)], axis=0)
            for r, i in zip(real, imag)
        )

    def mirrored(pieces):
        return tuple(jnp.dot(piece, mirror[...], preferred_element_type=F32).astype(BF16) for piece in pieces)

    def levels(start, unit):
        pieces = [kernel[pl.ds(start + 4 * i, 256, stride=16), :] for i in range(2)]
        return jnp.concatenate(pieces, axis=1) * unit

    def along_x(parity):
        wait_recv(got_2.at[parity, :, 0 : 32 * (n_pencil - 1), :], recv_2.at[parity])

        def found(kx, twin):
            parts = []
            for part in range(2):
                low, high = got_2[parity, part, 0:256, :], got_2[parity, part, 256:512, :]
                parts.append(halves(low - high if kx else low + high))
            right = stacked(*parts)
            if twin:
                real, imag = (mirrored(pieces) for pieces in parts)
                other = stacked(real, tuple(-piece for piece in imag))
                right = tuple(jnp.concatenate(both, axis=1) for both in zip(right, other))
            return dot_3((tx[0, kx], tx[1, kx]), right)

        def plain():
            own = 1 if parity else jnp.where(slab < 4, 0, 2)
            for kx in range(2):
                both, green = found(kx, False), levels(own + 8 * kx, 2.0 * unit)
                spectra[kx, 0] = both[:, 0:256] * green
                spectra[kx, 1] = both[:, 256:512] * green

        if parity:
            plain()
        else:
            pl.when(jnp.logical_not(first))(plain)

            @pl.when(first)
            def _():
                wait_recv(level_in, level_recv)
                for kx in range(2):
                    both, green, other = found(kx, True), levels(8 * kx, 0.5 * unit), level_in[kx] * (0.5 * unit)
                    mean, rest = green + other, green - other
                    for part in range(2):
                        one, two = (both[:, 256 * k : 256 * k + 256] for k in (part, part + 2))
                        spectra[kx, part] = mean * one + rest * two

        ends = []
        for kx in range(2):
            table = (tx[0, 2 * kx], tx[1, 2 * kx])
            real, imag = halves(spectra[kx, 0]), halves(spectra[kx, 1])
            right = tuple(
                jnp.concatenate([jnp.concatenate([r, i], axis=1), jnp.concatenate([-i, r], axis=1)], axis=0)
                for r, i in zip(real, imag)
            )
            ends.append(dot_3(table, right))
        for part in range(2):
            lanes = slice(256 * part, 256 * part + 256)
            back_2[parity, part, 0:256, :] = ends[0][:, lanes] + ends[1][:, lanes]
            back_2[parity, part, 256:512, :] = ends[0][:, lanes] - ends[1][:, lanes]

    def turns(step):
        return jnp.where(step < 2, 3 * step, step - 1)

    def return_x(turn, carry):
        parity, chunk = turn // CHUNKS, turns(lax.rem(turn, CHUNKS))
        own = pl.ds(pl.multiple_of(pencil * 32 + chunk * 8, 8), 8)
        took_2[parity, chunk, pencil] = back_2[parity, :, own, :]

        def send(k, carry):
            device = on_pencil(k)
            rows = pl.ds(pl.multiple_of(device[1] * 32 + chunk * 8, 8), 8)
            remote(
                back_2.at[parity, :, rows, :], took_2.at[parity, chunk, pencil], send_3, recv_3.at[parity, chunk], device
            ).start()
            return carry

        return lax.fori_loop(1, n_pencil, send, carry, unroll=5)

    def inverse_z(turn, carry):
        parity, chunk = turn // CHUNKS, turns(lax.rem(turn, CHUNKS))
        wait_recv(took_2.at[parity, chunk, 0 : n_pencil - 1], recv_3.at[parity, chunk])
        rows = jnp.concatenate([took_2[parity, chunk, :, part].reshape(128, 256) for part in range(2)], axis=1)
        space = dot_3(halves(rows), (tz[0], tz[1]), ((1,), (1,)))
        for i in range(4):
            lines[i] = space[:, 128 * i : 128 * i + 128]
        for h in range(2):
            for q in range(2):
                tiles = []
                for a in range(4):
                    pieces = [lines[2 * part + q, pl.ds(4 * h + a, 16, stride=8), :] for part in range(2)]
                    tiles.append(jnp.concatenate(pieces, axis=0))
                for s, tile in enumerate(swap_groups(tiles)):
                    back_1[parity, chunk, 4 * q + s, :, 128 * h : 128 * h + 128] = tile
        took_1[parity, chunk, slab] = back_1[parity, chunk, slab]

        def send(k, carry):
            device = on_slab(k)
            remote(
                back_1.at[parity, chunk, device[0]], took_1.at[parity, chunk, slab], send_4, recv_4.at[parity, chunk], device
            ).start()
            return carry

        return lax.fori_loop(1, n_slab, send, carry, unroll=7)

    along_x(0)
    lax.fori_loop(0, 1, return_x, 0)
    lax.fori_loop(1, 3, lambda turn, carry: return_x(turn, forward_z(turn + 5, carry)), 0)
    lax.fori_loop(3, 4, return_x, 0)
    lax.fori_loop(0, 2, inverse_z, 0)
    along_x(1)
    lax.fori_loop(4, 5, return_x, 0)
    lax.fori_loop(5, 7, lambda turn, carry: inverse_z(turn - 3, return_x(turn, carry)), 0)
    lax.fori_loop(7, 8, return_x, 0)
    lax.fori_loop(4, 8, inverse_z, 0)

    row_starts = (2, 32)
    last = []
    for b, dx in sides:
        last.append((last_x_out.at[b], last_x_in.at[1 - b], on_pencil(dx)))
        for a, dz in sides:
            rows = (0, 2) if b == 0 else (6, 8)
            last.append(
                (last_z_out.at[3 * b, a, rows[0] : rows[1]], last_corner_in.at[1 - b, 1 - a], at(dz, dx))
            )

    def planes(chunk, a):
        return (last_z_out.at[chunk, a], last_z_in.at[chunk, 1 - a], last_send.at[6 + a], last_recv.at[chunk, 1 - a])

    def take_planes(step, carry):
        chunk = turns(step)
        for a, row in ((0, 6), (1, 40)):
            wait_recv(last_z_in.at[chunk, a], last_recv.at[chunk, a])
            for x in range(8):
                for tile in range(4):
                    out[pl.ds(row_of(2 + 8 * chunk + x, tile, row), 2), :] = last_z_in[chunk, a, x, 2 * tile : 2 * tile + 2, :]
        return carry

    def inverse_y(step, carry):
        chunk = turns(step)
        ends = []
        for parity in range(2):
            wait_recv(took_1.at[parity, chunk, 0 : n_slab - 1], recv_4.at[parity, chunk])
            columns = took_1[parity, chunk].reshape(256, 256).T
            ends.append(dot_3(halves(columns), (ty[0, parity], ty[1, parity])))
        space = (ends[0] + ends[1], ends[0] - ends[1])
        for tile in range(4):
            lanes = slice(128 * (tile % 2), 128 * (tile % 2) + 128)
            cells = space[tile // 2][:, lanes].reshape(8, 32, 128)
            for x in range(8):
                out[pl.ds(pl.multiple_of(row_of(2 + 8 * chunk + x, tile, 8), 8), 32), :] = cells[x]
            last_z_out[chunk, 0, :, 2 * tile : 2 * tile + 2, :] = cells[:, 0:2, :]
            last_z_out[chunk, 1, :, 2 * tile : 2 * tile + 2, :] = cells[:, 30:32, :]
        for a, dz in sides:
            remote(*planes(chunk, a), on_slab(dz)).start()
        for b in range(2):

            @pl.when(chunk == 3 * b)
            def _():
                for x in range(2):
                    for tile in range(4):
                        last_x_out[b, x, tile] = out[pl.ds(row_of(row_starts[b] + x, tile, 8), 32), :]
                for i in range(3 * b, 3 * b + 3):
                    source, target, device = last[i]
                    remote(source, target, last_send.at[i], corner_recv.at[i], device).start()

        return carry

    lax.fori_loop(0, CHUNKS, inverse_y, 0)

    slot = lax.broadcasted_iota(jnp.int32, (slots, slots), 0)
    chosen = jnp.where(slot == pairs[0:1, :], 1.0, 0.0).astype(BF16)
    rest = terms[...]
    total = jnp.zeros(near.shape, F32)
    for _ in range(3):
        part = rest.astype(BF16)
        rest = rest - part.astype(F32)
        total = total + jnp.dot(chosen, part, preferred_element_type=F32)
    near[...] = total

    lax.fori_loop(0, CHUNKS - 1, take_planes, 0)
    for i, (source, target, device) in enumerate(last):
        wait_recv(target, corner_recv.at[i])
    for b, start in ((0, 0), (1, 34)):
        for x in range(2):
            for tile in range(4):
                out[pl.ds(row_of(start + x, tile, 8), 32), :] = last_x_in[b, x, tile]
                for a, row in ((0, 6), (1, 40)):
                    out[pl.ds(row_of(start + x, tile, row), 2), :] = last_corner_in[b, a, x, 2 * tile : 2 * tile + 2, :]
    take_planes(CHUNKS - 1, 0)

    def gather_group(step, carry):
        def pick(turn, carry):
            for u in range(UNROLL):
                b = turn * UNROLL + u
                row_0, row_1, lane_0 = window(anchors, step * GROUP + b)
                masks, beyond, top = window_masks(lane_0)
                for i in range(4):
                    cells = jnp.where(beyond, out[pl.ds(row_0 + 192 * i, 8), :], out[pl.ds(row_1 + 192 * i, 8), :])
                    cells = jnp.where(top, cells, pltpu.roll(cells, 4, 0))
                    for j in range(2):
                        values[b, 16 * i + 8 * j : 16 * i + 8 * j + 8] = jnp.where(masks[j], cells, 0.0)
            return carry

        lax.fori_loop(0, GROUP // UNROLL, pick, 0)
        group_copy(step, projection_at, projection, group_load).wait()
        rows = group_rows(step)
        box = lane_sums(values[...].reshape(GROUP * BOX, 128)).reshape(GROUP, BOX, 128)
        far = jnp.sum(projection[rows] * box, axis=1)
        result[rows, :] = far + near[rows, :]
        return carry

    lax.fori_loop(0, slots // GROUP, gather_group, 0)
    for i, (source, target, device) in enumerate(last):
        wait_send(source, last_send.at[i])
    for a in range(2):
        wait_send(last_z_out.at[:, a], last_send.at[6 + a])
    for i, (source, target, device) in enumerate(rims):
        wait_send(source, rim_send.at[i])
    wait_send(sent_1.at[:, :, 0 : n_slab - 1], send_1)
    wait_send(got_2.at[:, :, 0 : 32 * (n_pencil - 1), :], send_2)
    wait_send(got_2.at[:, :, 0 : 32 * (n_pencil - 1), :], send_3)
    wait_send(back_1.at[:, :, 0 : n_slab - 1], send_4)

    @pl.when(middle)
    def _():
        wait_send(level_out, level_send)


def field(anchors, count, pairs, charges, grid, projection, matrices, kernel):
    tables = [jnp.asarray(np.stack(split_table(table))) for table in (y_tables(), z_table(), x_tables())]
    slots, panels = charges.shape
    dma = pltpu.SemaphoreType.DMA
    vmem = pltpu.VMEM
    return pl.pallas_call(
        field_kernel,
        in_specs=[
            *[pl.BlockSpec(memory_space=pltpu.SMEM)] * 2,
            *[pl.BlockSpec(memory_space=vmem)] * 3,
            *[pl.BlockSpec(memory_space=pl.ANY)] * 6,
        ],
        out_specs=pl.BlockSpec(memory_space=vmem),
        out_shape=pltpu.VMEM((slots, panels), F32),
        scratch_shapes=[
            vmem(projection.shape, F32),
            vmem(matrices.shape, BF16),
            vmem(kernel.shape, F32),
            *(vmem(table.shape, BF16) for table in tables),
            vmem((slots, panels), F32),
            vmem((slots, panels), F32),
            vmem((slots, panels), F32),
            vmem((GROUP, BOX, panels), F32),
            vmem((36 * 4 * 48, 128), F32),
            vmem((256, 256), BF16),
            vmem((32, 4, 32, 128), F32),
            vmem((2, 36, 8, 128), F32),
            vmem((2, 32, 8, 128), F32),
            vmem((2, 2, 4, 32, 128), F32),
            vmem((2, 2, 2, 8, 128), F32),
            vmem((2, CHUNKS, 8, 32, 256), F32),
            vmem((2, CHUNKS, 8, 32, 256), F32),
            vmem((2, CHUNKS, 16, 2, 8, 256), F32),
            vmem((2, 2, 512, 256), F32),
            vmem((2, 256, 256), F32),
            vmem((2, 256, 256), F32),
            vmem((2, 2, 256, 256), F32),
            vmem((2, 2, 512, 256), F32),
            vmem((2, CHUNKS, 16, 2, 8, 256), F32),
            vmem((2, CHUNKS, 8, 32, 256), F32),
            vmem((2, CHUNKS, 8, 32, 256), F32),
            vmem((4, 128, 128), F32),
            vmem((CHUNKS, 2, 8, 8, 128), F32),
            vmem((CHUNKS, 2, 8, 8, 128), F32),
            vmem((2, 2, 4, 32, 128), F32),
            vmem((2, 2, 4, 32, 128), F32),
            vmem((2, 2, 2, 8, 128), F32),
            dma((6,)),
            dma((slots // GROUP,)),
            dma,
            dma,
            dma((8,)),
            dma((8,)),
            dma((8,)),
            dma((CHUNKS, 2)),
            dma((6,)),
            dma,
            dma((2, CHUNKS)),
            dma,
            dma((2,)),
            dma,
            dma((2, CHUNKS)),
            dma,
            dma((2, CHUNKS)),
        ],
        compiler_params=pltpu.CompilerParams(
            collective_id=0, has_side_effects=True, vmem_limit_bytes=57 << 20
        ),
        cost_estimate=pl.CostEstimate(flops=10**10, bytes_accessed=10**7, transcendentals=0),
    )(anchors, count, pairs, charges, grid, projection, matrices, kernel, *tables)


def shards(charges, projection, anchors, block_count, near_pairs, near_matrices, kernel_hat):
    grid = pltpu.with_memory_space_constraint(scatter(anchors.T, block_count, projection, charges), pltpu.VMEM)
    levels = jnp.transpose(kernel_hat.reshape(NX, 4, 2, 128), (0, 2, 1, 3)).reshape(NX * 8, 128)
    total = field(anchors.T, block_count, near_pairs.T, charges, grid, projection, near_matrices, levels)
    in_use = lax.broadcasted_iota(jnp.int32, total.shape, 0) < block_count[0]
    return jnp.where(in_use, total, 0.0)


def solution(mesh):
    return jax.shard_map(
        shards,
        mesh=mesh,
        in_specs=(
            P(("slab", "pencil"), None),
            P(("slab", "pencil"), None, None),
            P(("slab", "pencil"), None),
            P(("slab", "pencil")),
            P(("slab", "pencil"), None),
            P(("slab", "pencil"), None, None),
            P(None, ("slab", "pencil"), None),
        ),
        out_specs=P(("slab", "pencil"), None),
        check_vma=False,
    )
```

```python
import jax
import jax.numpy as jnp
import ml_dtypes
import numpy as np
from jax import lax
from jax.experimental import pallas as pl
from jax.experimental.pallas import tpu as pltpu
from jax.sharding import PartitionSpec as P

NX, NY, NZ, BOX = 512, 512, 256, 64
GROUP = 64
UNROLL = 4
AHEAD = 2
F32, BF16 = jnp.float32, jnp.bfloat16


def halves(value):
    high = value.astype(BF16)
    return high, (value - high.astype(F32)).astype(BF16)


def lane_sums(value):
    ones = jnp.ones((128, 128), BF16)
    high, low = halves(value)
    return jnp.dot(high, ones, preferred_element_type=F32) + jnp.dot(low, ones, preferred_element_type=F32)


def row_of(x, tile, z):
    return (x * 4 + tile) * 48 + z


def window(anchors, slot):
    corner = row_of(anchors[0, slot] & 31, 0, (anchors[2, slot] & 31) + 6)
    y_at = (anchors[1, slot] + (NY - 2)) & (NY - 1)
    tile = y_at >> 7
    return corner + 48 * tile, corner + 48 * ((tile + 1) & 3), y_at & 127


def window_masks(lane_0):
    row = lax.broadcasted_iota(jnp.int32, (8, 128), 0)
    lane = lax.broadcasted_iota(jnp.int32, (8, 128), 1)
    shifted = (lane - row // 4 - lane_0) & 127
    return (shifted == 0, shifted == 2), lane >= lane_0, row < 4


def group_rows(step):
    return pl.ds(pl.multiple_of(step * GROUP, GROUP), GROUP)


def group_copy(step, source, target, sems):
    return pltpu.make_async_copy(source.at[group_rows(step)], target.at[group_rows(step)], sems.at[step])


def scatter_kernel(anchors, count, projection_at, charges, cells, projection, values, load):
    grid = cells.reshape(36 * 4 * 48, 128)
    for step in range(AHEAD):
        group_copy(step, projection_at, projection, load).start()

    def clear(x, carry):
        grid[pl.ds(pl.multiple_of(x * 192, 8), 192), :] = jnp.zeros((192, 128), F32)
        return carry

    lax.fori_loop(0, 36, clear, 0)

    def group(step, carry):
        @pl.when(step < charges.shape[0] // GROUP - AHEAD)
        def _():
            group_copy(step + AHEAD, projection_at, projection, load).start()

        group_copy(step, projection_at, projection, load).wait()
        rows = group_rows(step)
        slot = step * GROUP + lax.broadcasted_iota(jnp.int32, (GROUP, 128), 0)
        masked = jnp.where(slot < count[0], charges[rows, :], 0.0)
        products = projection[rows] * masked[:, None, :]
        values[...] = lane_sums(products.reshape(GROUP * BOX, 128)).reshape(GROUP, BOX, 128)

        def place(turn, carry):
            firsts, seconds, furthest = [], [], 0
            for u in range(UNROLL):
                b = turn * UNROLL + u
                row_0, row_1, lane_0 = window(anchors, step * GROUP + b)
                masks, beyond, top = window_masks(lane_0)
                here, there = beyond & top, top & ~beyond
                furthest = jnp.maximum(furthest, lane_0)
                for i in range(4):
                    patch = jnp.where(masks[0], values[b, 16 * i : 16 * i + 8], 0.0)
                    patch = jnp.where(masks[1], values[b, 16 * i + 8 : 16 * i + 16], patch)
                    patch = patch + pltpu.roll(patch, 4, 0)
                    firsts.append((row_0 + 192 * i, jnp.where(here, patch, 0.0)))
                    seconds.append((row_1 + 192 * i, there, patch))
            for row, patch in firsts:
                grid[pl.ds(row, 8), :] += patch

            @pl.when(furthest > 124)
            def _():
                for row, there, patch in seconds:
                    grid[pl.ds(row, 8), :] += jnp.where(there, patch, 0.0)

            return carry

        return lax.fori_loop(0, GROUP // UNROLL, place, carry)

    lax.fori_loop(0, charges.shape[0] // GROUP, group, 0)


def scatter(anchors, count, projection, charges):
    slots = charges.shape[0]
    smem, vmem = pl.BlockSpec(memory_space=pltpu.SMEM), pl.BlockSpec(memory_space=pltpu.VMEM)
    return pl.pallas_call(
        scatter_kernel,
        in_specs=[smem, smem, pl.BlockSpec(memory_space=pl.ANY), vmem],
        out_specs=pl.BlockSpec(memory_space=pltpu.VMEM),
        scratch_shapes=[
            pltpu.VMEM(projection.shape, F32),
            pltpu.VMEM((GROUP, BOX, 128), F32),
            pltpu.SemaphoreType.DMA((slots // GROUP,)),
        ],
        out_shape=pltpu.VMEM((36, 4, 48, 128), F32),
        compiler_params=pltpu.CompilerParams(vmem_limit_bytes=57 << 20),
    )(anchors, count, projection, charges)


CHUNKS = 4
MESH = pl.DeviceIdType.MESH


def phases(product, length):
    angle = 2.0 * np.pi * (product % length) / length
    return np.cos(angle), np.sin(angle)


def split_table(table):
    table = table.astype(np.float32)
    high = table.astype(ml_dtypes.bfloat16)
    return high, (table - high.astype(np.float32)).astype(ml_dtypes.bfloat16)


def y_tables():
    slab, part, pencil = np.meshgrid(np.arange(8), np.arange(2), np.arange(16), indexing="ij")
    device = (slab * 16 + pencil).reshape(-1, 1)
    part = part.reshape(-1, 1)
    even = np.where(device < 64, 4 * device, 4 * device + 2)
    odd = 4 * device + 1
    position = np.arange(256)[None, :]
    result = []
    for freq in (even, odd):
        cos, sin = phases(freq * position, NY)
        table = np.where(part == 0, cos, -sin)
        if freq is even:
            table[(device[:, 0] == 0) & (part[:, 0] == 1)] = 1.0 - 2.0 * (position[0] % 2)
        result.append(table)
    return np.stack(result)


def z_table():
    position = np.arange(NZ)
    cos, sin = phases(position[:, None] * position[None, :], NZ)
    return np.block([[cos, -sin], [sin, cos]])


def x_tables():
    position = np.arange(256)
    result = []
    for parity in range(2):
        cos, sin = phases((2 * position[:, None] + parity) * position[None, :], NX)
        result.append(np.concatenate([cos, sin], axis=1))
        if parity:
            result.append(np.concatenate([cos.T, sin.T], axis=1))
    return np.stack(result)


def dot_3(left, right, dims=((1,), (0,))):
    def one(a, b):
        return lax.dot_general(a, b, (dims, ((), ())), preferred_element_type=F32)

    return one(left[0], right[0]) + (one(left[0], right[1]) + one(left[1], right[0]))


def swap_groups(tiles):
    lane = lax.broadcasted_iota(jnp.int32, tiles[0].shape, 1)
    low, even = lane < 64, lane % 64 < 32
    firsts, lasts = [], []
    for a, b in ((tiles[0], tiles[2]), (tiles[1], tiles[3])):
        firsts.append(jnp.where(low, a, pltpu.roll(b, 64, 1)))
        lasts.append(jnp.where(low, pltpu.roll(a, 64, 1), b))
    result = []
    for a, b in (firsts, lasts):
        result.append(jnp.where(even, a, pltpu.roll(b, 32, 1)))
        result.append(jnp.where(even, pltpu.roll(a, 96, 1), b))
    return result


def field_kernel(
    anchors, count, pairs, charges, grid, projection_at, matrices_at, kernel_at, ty_at, tz_at, tx_at,
    result,
    projection, matrices, kernel, ty, tz, tx, sources, terms, near, values, out, mirror,
    charge, z_out, z_in, x_in, corner_in, sent_1, got_1, sent_2, got_2, level_out, level_in, spectra, back_2, took_2,
    back_1, took_1, lines, last_z_out, last_z_in, last_x_out, last_x_in, last_corner_in,
    load, group_load, level_send, level_recv, rim_send, rim_recv, last_send, last_recv, corner_recv,
    send_1, recv_1, send_2, recv_2, send_3, recv_3, send_4, recv_4,
):
    slab, pencil = lax.axis_index("slab"), lax.axis_index("pencil")
    n_slab, n_pencil = 8, 16

    def at(slab_step, pencil_step):
        return (lax.rem(slab + n_slab + slab_step, n_slab), lax.rem(pencil + n_pencil + pencil_step, n_pencil))

    def on_slab(step):
        return at(step, 0)

    def on_pencil(step):
        return at(0, step)

    def to_pencil(step):
        core = lax.rem(slab, 2)
        one, two = lax.div(step, 4), lax.rem(step, 4)
        y_step = (1 - core) * one + core * (4 - two)
        x_step = (1 - core) * two + core * (4 - one)
        y_at = lax.rem(lax.div(pencil, 4) + y_step, 4)
        x_at = lax.rem(lax.rem(pencil, 4) + x_step, 4)
        return (slab, 4 * y_at + x_at)

    def remote(source, target, send_sem, recv_sem, device):
        return pltpu.make_async_remote_copy(
            src_ref=source, dst_ref=target, send_sem=send_sem, recv_sem=recv_sem, device_id=device, device_id_type=MESH
        )

    def wait_recv(ref, sem):
        remote(ref, ref, sem, sem, on_slab(1)).wait_recv()

    def wait_send(ref, sem):
        remote(ref, ref, sem, sem, on_slab(1)).wait_send()

    barrier = pltpu.get_barrier_semaphore()

    def greet(device):
        pl.semaphore_signal(barrier, inc=1, device_id=device, device_id_type=MESH)

    def greet_slab(step, carry):
        greet(on_slab(step))
        return carry

    def greet_pencil(step, carry):
        greet(on_pencil(step))
        return carry

    sides = ((0, -1), (1, 1))
    lax.fori_loop(1, n_slab, greet_slab, 0, unroll=7)
    lax.fori_loop(1, n_pencil, greet_pencil, 0, unroll=5)
    for _, dz in sides:
        for _, dx in sides:
            greet(at(dz, dx))

    loads = [
        pltpu.make_async_copy(source, target, load.at[i])
        for i, (source, target) in enumerate(
            (
                (grid.at[2:34, :, 8:40, :], charge),
                (ty_at, ty),
                (kernel_at, kernel),
                (tz_at, tz),
                (tx_at, tx),
                (matrices_at, matrices),
            )
        )
    ]
    for copy in loads[:2]:
        copy.start()

    def pack_rims(x, carry):
        for tile in range(4):
            z_out[0, x, 2 * tile : 2 * tile + 2, :] = grid[x, tile, 6:8, :]
            z_out[1, x, 2 * tile : 2 * tile + 2, :] = grid[x, tile, 40:42, :]
        return carry

    lax.fori_loop(0, 36, pack_rims, 0, unroll=4)
    pl.semaphore_wait(barrier, n_slab + n_pencil + 2)
    ends = ((0, 2), (34, 36))
    rims = []
    for a, dz in sides:
        rims.append((z_out.at[a, 2:34], z_in.at[1 - a], on_slab(dz)))
    for b, dx in sides:
        rims.append((grid.at[ends[b][0] : ends[b][1], :, 8:40, :], x_in.at[1 - b], on_pencil(dx)))
    for a, dz in sides:
        for b, dx in sides:
            rims.append((z_out.at[a, ends[b][0] : ends[b][1]], corner_in.at[1 - a, 1 - b], at(dz, dx)))
    for i, (source, target, device) in enumerate(rims):
        remote(source, target, rim_send.at[i], rim_recv.at[i], device).start()
    first = jnp.logical_and(slab == 0, pencil == 0)
    middle = jnp.logical_and(slab == 4, pencil == 0)
    for copy in loads[2:]:
        copy.start()

    @pl.when(middle)
    def _():
        loads[2].wait()
        for kx in range(2):
            for i in range(2):
                level_out[kx, :, 128 * i : 128 * i + 128] = kernel[pl.ds(8 * kx + 4 * i, 256, stride=16), :]
        remote(level_out, level_in, level_send, level_recv, (0, pencil)).start()


    loads[0].wait()
    wait_recv(z_in.at[1], rim_recv.at[0])
    wait_recv(z_in.at[0], rim_recv.at[1])

    def add_rims(x, carry):
        for tile in range(4):
            charge[x, tile, 0:2, :] += z_in[0, x, 2 * tile : 2 * tile + 2, :]
            charge[x, tile, 30:32, :] += z_in[1, x, 2 * tile : 2 * tile + 2, :]
        return carry

    lax.fori_loop(0, 32, add_rims, 0, unroll=4)
    loads[1].wait()

    def forward_y(step, carry):
        chunk = lax.rem(step + 1, CHUNKS)

        @pl.when(step == 2)
        def _():
            for i in range(2, 8):
                wait_recv(rims[i][1], rim_recv.at[i])
            for b, start in ((0, 0), (1, 30)):
                charge[start : start + 2] += x_in[b]
                for a, row in ((0, 0), (1, 30)):
                    for x in range(2):
                        for tile in range(4):
                            charge[start + x, tile, row : row + 2, :] += corner_in[a, b, x, 2 * tile : 2 * tile + 2, :]

        tiles = [charge[pl.ds(8 * chunk, 8), tile].reshape(256, 128) for tile in range(4)]
        for parity in range(2):
            if parity:
                halved = [tiles[0] - tiles[2], tiles[1] - tiles[3]]
            else:
                halved = [tiles[0] + tiles[2], tiles[1] + tiles[3]]
            columns = halves(jnp.concatenate(halved, axis=1))
            freqs = dot_3((ty[0, parity], ty[1, parity]), columns, ((1,), (1,)))
            sent_1[parity, chunk] = freqs.reshape(n_slab, 32, 256)
            if not parity:
                to_slabs(0, chunk)
        return carry

    def to_slabs(parity, chunk):
        got_1[parity, chunk, slab] = sent_1[parity, chunk, slab]

        def send(k, carry):
            device = on_slab(k)
            remote(
                sent_1.at[parity, chunk, device[0]], got_1.at[parity, chunk, slab], send_1, recv_1.at[parity, chunk], device
            ).start()
            return carry

        return lax.fori_loop(1, n_slab, send, 0, unroll=7)

    lax.fori_loop(0, CHUNKS, forward_y, 0)
    lax.fori_loop(0, CHUNKS, lambda step, carry: to_slabs(1, lax.rem(step + 1, CHUNKS)), 0)
    for step in range(charges.shape[0] // GROUP):
        group_copy(step, projection_at, projection, group_load).start()

    slots, panels = charges.shape
    slot = lax.broadcasted_iota(jnp.int32, (slots, panels), 0)
    coarse = jnp.where(slot < count[0], charges[...], 0.0).astype(BF16)
    slot = lax.broadcasted_iota(jnp.int32, (slots, slots), 0)
    chosen = jnp.where(slot == pairs[1:2, :], 1.0, 0.0)
    row = lax.broadcasted_iota(jnp.int32, (256, 256), 0)
    lane = lax.broadcasted_iota(jnp.int32, (256, 256), 1)
    mirror[...] = jnp.where((row + lane) & 255 == 0, 1.0, 0.0).astype(BF16)
    sources[...] = jnp.dot(chosen.T.astype(BF16), coarse, preferred_element_type=F32)
    pl.when(jnp.logical_not(middle))(loads[2].wait)
    loads[3].wait()
    loads[5].wait()

    def near_group(group, carry):
        rows = pl.ds(pl.multiple_of(8 * group, 8), 8)
        taken = sources[rows, :].astype(BF16)
        row = lax.broadcasted_iota(jnp.int32, (8, panels), 0)
        total = jnp.zeros((8, panels), F32)
        for i in range(8):
            found = lax.dot_general(
                taken, matrices[8 * group + i], (((1,), (1,)), ((), ())), preferred_element_type=F32
            )
            total = jnp.where(row == i, found, total)
        terms[rows, :] = total
        return carry

    near_turns = 2 * CHUNKS - 2

    def near_share(turn):
        start, stop = ((slots // 8) * t // near_turns for t in (jnp.minimum(turn, near_turns), jnp.minimum(turn + 1, near_turns)))
        lax.fori_loop(start, stop, near_group, 0)

    def forward_z(turn, carry):
        parity, chunk = turn // CHUNKS, lax.rem(turn + 1, CHUNKS)
        near_share(turn)
        wait_recv(got_1.at[parity, chunk, 0 : n_slab - 1], recv_1.at[parity, chunk])
        for h in range(2):
            for q in range(2):
                tiles = swap_groups([got_1[parity, chunk, 4 * q + s, :, 128 * h : 128 * h + 128] for s in range(4)])
                for a in range(4):
                    for part in range(2):
                        lines[2 * part + q, pl.ds(4 * h + a, 16, stride=8), :] = tiles[a][16 * part : 16 * part + 16]
        rows = halves(jnp.concatenate([lines[i] for i in range(4)], axis=1))
        freqs = dot_3(rows, (tz[0], tz[1]))
        for part in range(2):
            sent_2[parity, chunk, :, part] = freqs[:, 256 * part : 256 * part + 256].reshape(n_pencil, 8, 256)
        mine = pl.ds(pl.multiple_of(pencil * 32 + chunk * 8, 8), 8)
        got_2[parity, :, mine, :] = sent_2[parity, chunk, pencil]

        def send(k, carry):
            device = to_pencil(k)
            remote(
                sent_2.at[parity, chunk, device[1]], got_2.at[parity, :, mine, :], send_2, recv_2.at[parity], device
            ).start()
            return carry

        return lax.fori_loop(1, n_pencil, send, carry, unroll=5)

    lax.fori_loop(0, 2 * CHUNKS - 2, forward_z, 0)

    loads[4].wait()
    unit = 1.0 / (NX * NY * NZ)

    def stacked(real, imag):
        return tuple(
            jnp.concatenate([jnp.concatenate([r, i], axis=1), jnp.concatenate([i, -r], axis=1)], axis=0)
            for r, i in zip(real, imag)
        )

    def mirrored(pieces):
        return tuple(jnp.dot(piece, mirror[...], preferred_element_type=F32).astype(BF16) for piece in pieces)

    def levels(start, unit):
        pieces = [kernel[pl.ds(start + 4 * i, 256, stride=16), :] for i in range(2)]
        return jnp.concatenate(pieces, axis=1) * unit

    def along_x(parity):
        wait_recv(got_2.at[parity, :, 0 : 32 * (n_pencil - 1), :], recv_2.at[parity])

        def found(kx, twin):
            parts = []
            for part in range(2):
                low, high = got_2[parity, part, 0:256, :], got_2[parity, part, 256:512, :]
                parts.append(halves(low - high if kx else low + high))
            right = stacked(*parts)
            if twin:
                real, imag = (mirrored(pieces) for pieces in parts)
                other = stacked(real, tuple(-piece for piece in imag))
                right = tuple(jnp.concatenate(both, axis=1) for both in zip(right, other))
            return dot_3((tx[0, kx], tx[1, kx]), right)

        def plain():
            own = 1 if parity else jnp.where(slab < 4, 0, 2)
            for kx in range(2):
                both, green = found(kx, False), levels(own + 8 * kx, 2.0 * unit)
                spectra[kx, 0] = both[:, 0:256] * green
                spectra[kx, 1] = both[:, 256:512] * green

        if parity:
            plain()
        else:
            pl.when(jnp.logical_not(first))(plain)

            @pl.when(first)
            def _():
                wait_recv(level_in, level_recv)
                for kx in range(2):
                    both, green, other = found(kx, True), levels(8 * kx, 0.5 * unit), level_in[kx] * (0.5 * unit)
                    mean, rest = green + other, green - other
                    for part in range(2):
                        one, two = (both[:, 256 * k : 256 * k + 256] for k in (part, part + 2))
                        spectra[kx, part] = mean * one + rest * two

        ends = []
        for kx in range(2):
            table = (tx[0, 2 * kx], tx[1, 2 * kx])
            real, imag = halves(spectra[kx, 0]), halves(spectra[kx, 1])
            right = tuple(
                jnp.concatenate([jnp.concatenate([r, i], axis=1), jnp.concatenate([-i, r], axis=1)], axis=0)
                for r, i in zip(real, imag)
            )
            ends.append(dot_3(table, right))
        for part in range(2):
            lanes = slice(256 * part, 256 * part + 256)
            back_2[parity, part, 0:256, :] = ends[0][:, lanes] + ends[1][:, lanes]
            back_2[parity, part, 256:512, :] = ends[0][:, lanes] - ends[1][:, lanes]

    def turns(step):
        return jnp.where(step < 2, 3 * step, step - 1)

    def return_x(turn, carry):
        parity, chunk = turn // CHUNKS, turns(lax.rem(turn, CHUNKS))
        own = pl.ds(pl.multiple_of(pencil * 32 + chunk * 8, 8), 8)
        took_2[parity, chunk, pencil] = back_2[parity, :, own, :]

        def send(k, carry):
            device = to_pencil(k)
            rows = pl.ds(pl.multiple_of(device[1] * 32 + chunk * 8, 8), 8)
            remote(
                back_2.at[parity, :, rows, :], took_2.at[parity, chunk, pencil], send_3, recv_3.at[parity, chunk], device
            ).start()
            return carry

        return lax.fori_loop(1, n_pencil, send, carry, unroll=5)

    def inverse_z(turn, carry):
        parity, chunk = turn // CHUNKS, turns(lax.rem(turn, CHUNKS))
        wait_recv(took_2.at[parity, chunk, 0 : n_pencil - 1], recv_3.at[parity, chunk])
        rows = jnp.concatenate([took_2[parity, chunk, :, part].reshape(128, 256) for part in range(2)], axis=1)
        space = dot_3(halves(rows), (tz[0], tz[1]), ((1,), (1,)))
        for i in range(4):
            lines[i] = space[:, 128 * i : 128 * i + 128]
        for h in range(2):
            for q in range(2):
                tiles = []
                for a in range(4):
                    pieces = [lines[2 * part + q, pl.ds(4 * h + a, 16, stride=8), :] for part in range(2)]
                    tiles.append(jnp.concatenate(pieces, axis=0))
                for s, tile in enumerate(swap_groups(tiles)):
                    back_1[parity, chunk, 4 * q + s, :, 128 * h : 128 * h + 128] = tile
        took_1[parity, chunk, slab] = back_1[parity, chunk, slab]

        def send(k, carry):
            device = on_slab(k)
            remote(
                back_1.at[parity, chunk, device[0]], took_1.at[parity, chunk, slab], send_4, recv_4.at[parity, chunk], device
            ).start()
            return carry

        return lax.fori_loop(1, n_slab, send, carry, unroll=7)

    along_x(0)
    lax.fori_loop(0, 1, return_x, 0)
    lax.fori_loop(1, 3, lambda turn, carry: return_x(turn, forward_z(turn + 5, carry)), 0)
    lax.fori_loop(3, 4, return_x, 0)
    lax.fori_loop(0, 2, inverse_z, 0)
    along_x(1)
    lax.fori_loop(4, 5, return_x, 0)
    lax.fori_loop(5, 7, lambda turn, carry: inverse_z(turn - 3, return_x(turn, carry)), 0)
    lax.fori_loop(7, 8, return_x, 0)
    lax.fori_loop(4, 8, inverse_z, 0)

    row_starts = (2, 32)
    last = []
    for b, dx in sides:
        last.append((last_x_out.at[b], last_x_in.at[1 - b], on_pencil(dx)))
        for a, dz in sides:
            rows = (0, 2) if b == 0 else (6, 8)
            last.append(
                (last_z_out.at[3 * b, a, rows[0] : rows[1]], last_corner_in.at[1 - b, 1 - a], at(dz, dx))
            )

    def planes(chunk, a):
        return (last_z_out.at[chunk, a], last_z_in.at[chunk, 1 - a], last_send.at[6 + a], last_recv.at[chunk, 1 - a])

    def take_planes(step, carry):
        chunk = turns(step)
        for a, row in ((0, 6), (1, 40)):
            wait_recv(last_z_in.at[chunk, a], last_recv.at[chunk, a])
            for x in range(8):
                for tile in range(4):
                    out[pl.ds(row_of(2 + 8 * chunk + x, tile, row), 2), :] = last_z_in[chunk, a, x, 2 * tile : 2 * tile + 2, :]
        return carry

    def inverse_y(step, carry):
        chunk = turns(step)
        ends = []
        for parity in range(2):
            wait_recv(took_1.at[parity, chunk, 0 : n_slab - 1], recv_4.at[parity, chunk])
            columns = took_1[parity, chunk].reshape(256, 256).T
            ends.append(dot_3(halves(columns), (ty[0, parity], ty[1, parity])))
        space = (ends[0] + ends[1], ends[0] - ends[1])
        for tile in range(4):
            lanes = slice(128 * (tile % 2), 128 * (tile % 2) + 128)
            cells = space[tile // 2][:, lanes].reshape(8, 32, 128)
            for x in range(8):
                out[pl.ds(pl.multiple_of(row_of(2 + 8 * chunk + x, tile, 8), 8), 32), :] = cells[x]
            last_z_out[chunk, 0, :, 2 * tile : 2 * tile + 2, :] = cells[:, 0:2, :]
            last_z_out[chunk, 1, :, 2 * tile : 2 * tile + 2, :] = cells[:, 30:32, :]
        for a, dz in sides:
            remote(*planes(chunk, a), on_slab(dz)).start()
        for b in range(2):

            @pl.when(chunk == 3 * b)
            def _():
                for x in range(2):
                    for tile in range(4):
                        last_x_out[b, x, tile] = out[pl.ds(row_of(row_starts[b] + x, tile, 8), 32), :]
                for i in range(3 * b, 3 * b + 3):
                    source, target, device = last[i]
                    remote(source, target, last_send.at[i], corner_recv.at[i], device).start()

        return carry

    lax.fori_loop(0, CHUNKS, inverse_y, 0)

    slot = lax.broadcasted_iota(jnp.int32, (slots, slots), 0)
    chosen = jnp.where(slot == pairs[0:1, :], 1.0, 0.0).astype(BF16)
    rest = terms[...]
    total = jnp.zeros(near.shape, F32)
    for _ in range(3):
        part = rest.astype(BF16)
        rest = rest - part.astype(F32)
        total = total + jnp.dot(chosen, part, preferred_element_type=F32)
    near[...] = total

    lax.fori_loop(0, CHUNKS - 1, take_planes, 0)
    for i, (source, target, device) in enumerate(last):
        wait_recv(target, corner_recv.at[i])
    for b, start in ((0, 0), (1, 34)):
        for x in range(2):
            for tile in range(4):
                out[pl.ds(row_of(start + x, tile, 8), 32), :] = last_x_in[b, x, tile]
                for a, row in ((0, 6), (1, 40)):
                    out[pl.ds(row_of(start + x, tile, row), 2), :] = last_corner_in[b, a, x, 2 * tile : 2 * tile + 2, :]
    take_planes(CHUNKS - 1, 0)

    def gather_group(step, carry):
        def pick(turn, carry):
            for u in range(UNROLL):
                b = turn * UNROLL + u
                row_0, row_1, lane_0 = window(anchors, step * GROUP + b)
                masks, beyond, top = window_masks(lane_0)
                for i in range(4):
                    cells = jnp.where(beyond, out[pl.ds(row_0 + 192 * i, 8), :], out[pl.ds(row_1 + 192 * i, 8), :])
                    cells = jnp.where(top, cells, pltpu.roll(cells, 4, 0))
                    for j in range(2):
                        values[b, 16 * i + 8 * j : 16 * i + 8 * j + 8] = jnp.where(masks[j], cells, 0.0)
            return carry

        lax.fori_loop(0, GROUP // UNROLL, pick, 0)
        group_copy(step, projection_at, projection, group_load).wait()
        rows = group_rows(step)
        box = lane_sums(values[...].reshape(GROUP * BOX, 128)).reshape(GROUP, BOX, 128)
        far = jnp.sum(projection[rows] * box, axis=1)
        result[rows, :] = far + near[rows, :]
        return carry

    lax.fori_loop(0, slots // GROUP, gather_group, 0)
    for i, (source, target, device) in enumerate(last):
        wait_send(source, last_send.at[i])
    for a in range(2):
        wait_send(last_z_out.at[:, a], last_send.at[6 + a])
    for i, (source, target, device) in enumerate(rims):
        wait_send(source, rim_send.at[i])
    wait_send(sent_1.at[:, :, 0 : n_slab - 1], send_1)
    wait_send(got_2.at[:, :, 0 : 32 * (n_pencil - 1), :], send_2)
    wait_send(got_2.at[:, :, 0 : 32 * (n_pencil - 1), :], send_3)
    wait_send(back_1.at[:, :, 0 : n_slab - 1], send_4)

    @pl.when(middle)
    def _():
        wait_send(level_out, level_send)


def field(anchors, count, pairs, charges, grid, projection, matrices, kernel):
    tables = [jnp.asarray(np.stack(split_table(table))) for table in (y_tables(), z_table(), x_tables())]
    slots, panels = charges.shape
    dma = pltpu.SemaphoreType.DMA
    vmem = pltpu.VMEM
    return pl.pallas_call(
        field_kernel,
        in_specs=[
            *[pl.BlockSpec(memory_space=pltpu.SMEM)] * 2,
            *[pl.BlockSpec(memory_space=vmem)] * 3,
            *[pl.BlockSpec(memory_space=pl.ANY)] * 6,
        ],
        out_specs=pl.BlockSpec(memory_space=vmem),
        out_shape=pltpu.VMEM((slots, panels), F32),
        scratch_shapes=[
            vmem(projection.shape, F32),
            vmem(matrices.shape, BF16),
            vmem(kernel.shape, F32),
            *(vmem(table.shape, BF16) for table in tables),
            vmem((slots, panels), F32),
            vmem((slots, panels), F32),
            vmem((slots, panels), F32),
            vmem((GROUP, BOX, panels), F32),
            vmem((36 * 4 * 48, 128), F32),
            vmem((256, 256), BF16),
            vmem((32, 4, 32, 128), F32),
            vmem((2, 36, 8, 128), F32),
            vmem((2, 32, 8, 128), F32),
            vmem((2, 2, 4, 32, 128), F32),
            vmem((2, 2, 2, 8, 128), F32),
            vmem((2, CHUNKS, 8, 32, 256), F32),
            vmem((2, CHUNKS, 8, 32, 256), F32),
            vmem((2, CHUNKS, 16, 2, 8, 256), F32),
            vmem((2, 2, 512, 256), F32),
            vmem((2, 256, 256), F32),
            vmem((2, 256, 256), F32),
            vmem((2, 2, 256, 256), F32),
            vmem((2, 2, 512, 256), F32),
            vmem((2, CHUNKS, 16, 2, 8, 256), F32),
            vmem((2, CHUNKS, 8, 32, 256), F32),
            vmem((2, CHUNKS, 8, 32, 256), F32),
            vmem((4, 128, 128), F32),
            vmem((CHUNKS, 2, 8, 8, 128), F32),
            vmem((CHUNKS, 2, 8, 8, 128), F32),
            vmem((2, 2, 4, 32, 128), F32),
            vmem((2, 2, 4, 32, 128), F32),
            vmem((2, 2, 2, 8, 128), F32),
            dma((6,)),
            dma((slots // GROUP,)),
            dma,
            dma,
            dma((8,)),
            dma((8,)),
            dma((8,)),
            dma((CHUNKS, 2)),
            dma((6,)),
            dma,
            dma((2, CHUNKS)),
            dma,
            dma((2,)),
            dma,
            dma((2, CHUNKS)),
            dma,
            dma((2, CHUNKS)),
        ],
        compiler_params=pltpu.CompilerParams(
            collective_id=0, has_side_effects=True, vmem_limit_bytes=57 << 20
        ),
        cost_estimate=pl.CostEstimate(flops=10**10, bytes_accessed=10**7, transcendentals=0),
    )(anchors, count, pairs, charges, grid, projection, matrices, kernel, *tables)


def shards(charges, projection, anchors, block_count, near_pairs, near_matrices, kernel_hat):
    grid = pltpu.with_memory_space_constraint(scatter(anchors.T, block_count, projection, charges), pltpu.VMEM)
    levels = jnp.transpose(kernel_hat.reshape(NX, 4, 2, 128), (0, 2, 1, 3)).reshape(NX * 8, 128)
    total = field(anchors.T, block_count, near_pairs.T, charges, grid, projection, near_matrices, levels)
    in_use = lax.broadcasted_iota(jnp.int32, total.shape, 0) < block_count[0]
    return jnp.where(in_use, total, 0.0)


def solution(mesh):
    return jax.shard_map(
        shards,
        mesh=mesh,
        in_specs=(
            P(("slab", "pencil"), None),
            P(("slab", "pencil"), None, None),
            P(("slab", "pencil"), None),
            P(("slab", "pencil")),
            P(("slab", "pencil"), None),
            P(("slab", "pencil"), None, None),
            P(None, ("slab", "pencil"), None),
        ),
        out_specs=P(("slab", "pencil"), None),
        check_vma=False,
    )
```
